128 devices in a mesh: lat: 8 (over z, x_lo), lon: 16 (over y, x_hi, core).
Axes of the slice: x: 4 (x_hi: 2, x_lo: 2; x = x_hi * 2 + x_lo), y: 4, z: 4, core: 2. Of those that a mesh axis runs over, the one named last changes fastest.
Arguments:
- tokens: bfloat16 [144, 384, 1024], P('lat', 'lon'), may hold values from -6 to 6
- qkv_weight: bfloat16 [1024, 3072], replicated, may hold values from -1 to 1
- out_weight: bfloat16 [1024, 1024], replicated, may hold values from -0.1875 to 0.1875
- merge_weight: bfloat16 [4096, 2048], P(None, 'lon'), may hold values from -0.09375 to 0.09375
- up_weight: bfloat16 [2048, 8192], P(None, 'lon'), may hold values from -0.125 to 0.125
- down_weight: bfloat16 [8192, 2048], P('lon'), may hold values from -0.0625 to 0.0625
Outputs:
- middle_out: bfloat16 [144, 384, 1024], P('lat', 'lon')
- coarse_out: bfloat16 [72, 192, 2048], P('lat', 'lon')
The draws below stay inside these ranges and needn't reach their ends.
All inputs are finite; a program needn't handle non-finite values.
Results may differ from the reference program's by a relative error of at most 0.013.
Values may be sent and summed in bfloat16 or wider, within the bound.
A program may use at most 128 MiB of HBM per device.

```python
import math
import jax
import jax.numpy as jnp
from jax import lax

D = 1024
DC = 2048
FF = 8192
HEADS = 16
WLAT = 6
WLON = 12
NLAT = 144
NLON = 384


def draw_qkv_weight(key, part):
    first = jax.random.fold_in(jax.random.fold_in(key, 17), 0)
    base = jax.random.normal(first, (D, 3 * D), jnp.float32) / math.sqrt(D)
    return jnp.clip(base, -1.0, 1.0).astype(jnp.bfloat16)


def steps_of(rng, extent, pieces, least, high):
    def one(axis_at, parts):
        draws = jax.random.uniform(jax.random.fold_in(jax.random.fold_in(rng, 6), axis_at), (parts,), jnp.float32, least / len(pieces), high / len(pieces))
        return jnp.repeat(jnp.exp(draws), extent[axis_at] // parts).reshape((-1,) + (1,) * (len(extent) - axis_at - 1))

    factor_of = one(*pieces[0])
    for cut in pieces[1:]:
        factor_of = factor_of * one(*cut)
    return factor_of


def gaussian(rng, dims, scale, most, cuts=(), kind=jnp.bfloat16):
    loudness = steps_of(rng, dims, cuts, -0.22, 0.18) if cuts else 1.0
    array = jax.random.normal(rng, dims, jnp.float32) * scale * loudness
    return jnp.minimum(jnp.maximum(array, -most), most).astype(kind)


def setup_inputs(seed: int = 0) -> dict:
    seeds = jax.random.split(jax.random.key(seed), 7)
    tokens = gaussian(seeds[0], (NLAT, NLON, D), 1.0, 6.0, ((0, 8), (1, 16)))
    qkv_weight = draw_qkv_weight(jax.random.fold_in(seeds[6], 71), 0)
    out_weight = gaussian(seeds[2], (D, D), D ** -0.5, 0.1875)
    merge_weight = gaussian(seeds[3], (4 * D, DC), (4 * D) ** -0.5, 0.09375, ((1, 16),))
    up_weight = gaussian(seeds[4], (DC, FF), DC ** -0.5, 0.125, ((1, 16),))
    down_weight = gaussian(seeds[5], (FF, DC), FF ** -0.5, 0.0625, ((0, 16),))
    return dict(tokens=tokens, qkv_weight=qkv_weight, out_weight=out_weight, merge_weight=merge_weight, up_weight=up_weight, down_weight=down_weight)


def normalize(values):
    center = values - lax.optimization_barrier(jnp.mean(values, axis=-1, keepdims=True))
    spread = lax.optimization_barrier(jnp.mean(center * center, axis=-1, keepdims=True))
    return center * lax.rsqrt(spread + 1e-05)

def to_windows(grid):
    height, breadth, depth = grid.shape
    shaped = grid.reshape(height // WLAT, WLAT, breadth // WLON, WLON, depth)
    return shaped.transpose(0, 2, 1, 3, 4).reshape(-1, WLAT * WLON, depth)

def from_windows(windows, height, breadth):
    depth = windows.shape[-1]
    shaped = windows.reshape(height // WLAT, breadth // WLON, WLAT, WLON, depth)
    return shaped.transpose(0, 2, 1, 3, 4).reshape(height, breadth, depth)

def attend(query, keys, values, key_valid):
    scale = 1.0 / query.shape[-1] ** 0.5
    scores = jnp.einsum('wqhd,wkhd->whqk', query.astype(jnp.float32), keys.astype(jnp.float32)) * scale
    scores = jnp.where(key_valid[:, None, None, :], scores, jnp.float32(-1e+30))
    top = lax.optimization_barrier(jnp.max(scores, axis=-1, keepdims=True))
    raised = jnp.exp(scores - top)
    weights = (raised / lax.optimization_barrier(jnp.sum(raised, axis=-1, keepdims=True))).astype(jnp.bfloat16)
    summed = jnp.einsum('whqk,wkhd->wqhd', weights.astype(jnp.float32), values.astype(jnp.float32))
    return summed.astype(jnp.bfloat16)

def reference(tokens, qkv_weight, out_weight, merge_weight, up_weight, down_weight):
    nlat, nlon, width = tokens.shape
    rim_lat = WLAT // 2
    rim_lon = WLON // 2
    head_size = width // HEADS
    normed = normalize(tokens.astype(jnp.float32)).astype(jnp.bfloat16)
    projected = jnp.dot(normed.reshape(-1, width), qkv_weight, preferred_element_type=jnp.float32)
    projected = projected.astype(jnp.bfloat16).reshape(nlat, nlon, 3 * width)
    projected = jnp.roll(projected, rim_lon, axis=1)
    projected = jnp.pad(projected, ((rim_lat, rim_lat), (0, 0), (0, 0)))
    position = jnp.arange(nlat + 2 * rim_lat, dtype=jnp.int32) - rim_lat
    row_valid = (position >= 0) & (position < nlat)
    band_count = (nlat + 2 * rim_lat) // WLAT
    bands = projected.reshape(band_count, WLAT, nlon, 3 * width)
    band_valid = row_valid.reshape(band_count, WLAT)

    def one_band(item):
        band, valid = item
        windows = to_windows(band)
        count = windows.shape[0]
        flags = to_windows(jnp.broadcast_to(valid[:, None, None], (WLAT, nlon, 1)))[..., 0]
        split = windows.reshape(count, WLAT * WLON, 3, HEADS, head_size)
        result = attend(split[:, :, 0], split[:, :, 1], split[:, :, 2], flags)
        return from_windows(result.reshape(count, WLAT * WLON, width), WLAT, nlon)
    attended = lax.map(one_band, (bands, band_valid)).reshape(nlat + 2 * rim_lat, nlon, width)
    attended = jnp.roll(attended[rim_lat:rim_lat + nlat], -rim_lon, axis=1)
    mixed = jnp.dot(attended.reshape(-1, width), out_weight, preferred_element_type=jnp.float32)
    middle_out = (tokens.reshape(-1, width).astype(jnp.float32) + mixed).astype(jnp.bfloat16)
    middle_out = middle_out.reshape(nlat, nlon, width)
    patches = middle_out.reshape(nlat // 2, 2, nlon // 2, 2, width).transpose(0, 2, 1, 3, 4)
    merged = normalize(patches.reshape(-1, 4 * width).astype(jnp.float32)).astype(jnp.bfloat16)
    coarse = jnp.dot(merged, merge_weight, preferred_element_type=jnp.float32).astype(jnp.bfloat16)
    coarse_normed = normalize(coarse.astype(jnp.float32)).astype(jnp.bfloat16)
    hidden = jax.nn.gelu(jnp.dot(coarse_normed, up_weight, preferred_element_type=jnp.float32), approximate=False)
    hidden = hidden.astype(jnp.bfloat16)
    summed = jnp.dot(hidden, down_weight, preferred_element_type=jnp.float32)
    coarse_out = (coarse.astype(jnp.float32) + summed).astype(jnp.bfloat16)
    return (middle_out, coarse_out.reshape(nlat // 2, nlon // 2, -1))
```

```python
import functools

import jax
import jax.numpy as jnp
import numpy as np
from jax import lax
from jax.experimental import pallas as pl
from jax.experimental.pallas import tpu as pltpu
from jax.sharding import PartitionSpec as P

MESH = pl.DeviceIdType.MESH
BF = jnp.bfloat16
F32 = jnp.float32
NEG = -1e30

ROWS, COLS, D, DC, HEADS = 18, 24, 1024, 2048, 16
CELLS = ROWS * COLS
GROUP = 112
HIGH = (3, 6, 6, 3)
WIDE = (6, 12, 6)
TOP = (0, 3, 9, 15)
LEFT = (0, 6, 18)


def _round(n):
    return -(-n // 16) * 16


PIECE = {}
_at = 0
for _b in range(3):
    for _a in range(4):
        PIECE[_a, _b] = (_at, _round(HIGH[_a] * WIDE[_b]), HIGH[_a] * WIDE[_b])
        _at += PIECE[_a, _b][1]
OWN = _at
HALO_W, HALO_E, HALO_N, HALO_S = 0, 160, 320, 432
HALO_NW, HALO_NE, HALO_SW, HALO_SE = 544, 576, 608, 640
HALO = 672


def _tables():
    order = np.zeros((OWN, CELLS), np.float32)
    for (a, b), (at, _, _) in PIECE.items():
        k = 0
        for i in range(HIGH[a]):
            for j in range(WIDE[b]):
                order[at + k, (TOP[a] + i) * COLS + LEFT[b] + j] = 1
                k += 1
    patch = np.zeros((4 * GROUP, CELLS), np.float32)
    for g in range(4):
        for r in range(ROWS // 2):
            for c in range(COLS // 2):
                cell = (2 * r + g // 2) * COLS + 2 * c + g % 2
                patch[g * GROUP + r * (COLS // 2) + c, cell] = 1
    return order, patch


def _window_parts():
    out = []
    for b in range(3):
        for a in range(4):
            at, rows, valid = PIECE[a, b]
            parts = []
            side = "n" if a == 0 else "s" if a == 3 else ""
            if b == 0:
                off = PIECE[a, 2][0] - PIECE[0, 2][0]
                parts.append((HALO_W + off, PIECE[a, 2][1], PIECE[a, 2][2], ""))
            if b == 2:
                off = PIECE[a, 0][0]
                parts.append((HALO_E + off, PIECE[a, 0][1], PIECE[a, 0][2], ""))
            if a == 0:
                off = HALO_N + (0, 32, 80)[b]
                parts.append((off, PIECE[3, b][1], PIECE[3, b][2], side))
            if a == 3:
                off = HALO_S + (0, 32, 80)[b]
                parts.append((off, PIECE[0, b][1], PIECE[0, b][2], side))
            corner = {(0, 0): HALO_NW, (0, 2): HALO_NE, (3, 0): HALO_SW, (3, 2): HALO_SE}
            if (a, b) in corner:
                parts.append((corner[a, b], 32, 18, side))
            out.append(((at, rows, valid), parts))
    return out


WINDOWS = _window_parts()


def _bias():
    bias = np.full((3, 16, 128), NEG, np.float32)
    for edge in range(3):
        for w, ((_, rows, valid), parts) in enumerate(WINDOWS):
            bias[edge, w, :valid] = 0
            at = rows
            for _, prows, pvalid, side in parts:
                gone = (edge == 1 and side == "n") or (edge == 2 and side == "s")
                if not gone:
                    bias[edge, w, at : at + pvalid] = 0
                at += prows
    return bias


def place():
    lat, lon = lax.axis_index("lat"), lax.axis_index("lon")
    z, xl = lat // 2, lat % 2
    y, xh, c = lon // 4, (lon // 2) % 2, lon % 2
    return lat, lon, z, xl, y, xh, c


def norm_rows(x):
    center = x - jnp.mean(x, axis=-1, keepdims=True)
    spread = jnp.mean(center * center, axis=-1, keepdims=True)
    return center * lax.rsqrt(spread + 1e-5)


def loop(n, body):
    def step(i, carry):
        body(i)
        return carry

    lax.fori_loop(0, n, step, 0)


def cols(i, size, base=0):
    return pl.ds(pl.multiple_of(base + i * size, 128), size)


HALO_SENDS = 12
WSEMS = {}
for _n in (
    ["yq+", "yq-", "yqf+", "yqf-"]
    + [f"yr{s}{i}" for s in "+-" for i in (1, 2, 3)]
    + ["yrf1", "yrf3", "yrf2+", "yrf2-"]
    + [f"x{k}" for k in range(4)]
    + [f"z{k}{s}" for k in range(4) for s in ("+", "-", "f+", "f-")]
):
    WSEMS[_n] = len(WSEMS)


def attention_kernel(
    tok, p1, bias, qkvw, outw, mw, p1t, pg,
    mid_out, merged_out, wg,
    qkvv, outv, p1tv, pgv, normed, xp, halo, qkv, kvh, att, attr, mid, mgd,
    lsem, hs, hr, ws, wr,
):
    lat, lon, z, xl, y, xh, c = place()
    north, south = lat > 0, lat < 7
    west, east = (lon + 15) % 16, (lon + 1) % 16
    yp = (lat, (lon + 4) % 16)
    ym = (lat, (lon + 12) % 16)
    zp = ((lat + 2) % 8, lon)
    zm = ((lat + 6) % 8, lon)
    xpart = (2 * z + 1 - xl, 4 * y + 2 * (1 - xh) + c)

    barrier = pltpu.get_barrier_semaphore()

    def greet(dev):
        pl.semaphore_signal(barrier, inc=1, device_id=dev, device_id_type=MESH)

    for dev in ((lat, west), (lat, east), yp, ym, zp, zm, xpart):
        greet(dev)

    @pl.when(north)
    def _():
        for o in (west, lon, east):
            greet((lat - 1, o))

    @pl.when(south)
    def _():
        for o in (west, lon, east):
            greet((lat + 1, o))

    local = [
        pltpu.make_async_copy(qkvw, qkvv, lsem.at[0]),
        pltpu.make_async_copy(p1t, p1tv, lsem.at[1]),
        pltpu.make_async_copy(outw, outv, lsem.at[2]),
        pltpu.make_async_copy(pg, pgv, lsem.at[3]),
        pltpu.make_async_copy(mw, wg.at[2 * y + xh], lsem.at[4]),
    ]
    for cp in local:
        cp.start()

    count = 7 + jnp.where(north, 3, 0) + jnp.where(south, 3, 0)
    pl.semaphore_wait(barrier, count)

    def block(k, other):
        yy = (y + (0, 3, 1, 2)[k]) % 4
        return 2 * yy + (1 - xh if other else xh)

    def rows_of(quarter, part):
        base = (quarter % 4) * 1024
        if part == 0:
            return pl.ds(pl.multiple_of(base, 512), 1024)
        return pl.ds(pl.multiple_of(base + (part - 1) * 512, 512), 512)

    def wcopy(name, slot, quarter, part, dev, own=False):
        rows = rows_of(quarter, part)
        src = mw.at[rows, :] if own else wg.at[slot, rows, :]
        i = WSEMS[name]
        return pltpu.make_async_remote_copy(
            src_ref=src, dst_ref=wg.at[slot, rows, :], send_sem=ws.at[i], recv_sem=wr.at[i],
            device_id=dev, device_id_type=MESH,
        )

    sends = {}

    def send(name, slot, quarter, part, dev, own=False):
        sends[name] = wcopy(name, slot, quarter, part, dev, own)
        sends[name].start()

    def got(name, slot, quarter, part):
        wcopy(name, slot, quarter, part, yp).wait_recv()

    own = block(0, False)
    send("x0", own, z, 0, xpart, own=True)
    send("yq+", own, z, 0, yp, own=True)
    send("yq-", own, z, 0, ym, own=True)

    def pump_y():
        got("yq+", block(1, False), z, 0)
        send("yqf+", block(1, False), z, 1, yp)
        send("x1", block(1, False), z, 0, xpart)
        got("yq-", block(2, False), z, 0)
        send("yqf-", block(2, False), z, 2, ym)
        send("x2", block(2, False), z, 0, xpart)
        for i in (1, 3, 2):
            send(f"yr+{i}", own, z + i, 0, yp, own=True)
            send(f"yr-{i}", own, z + i, 0, ym, own=True)

    def pump_y2():
        got("yqf+", block(3, False), z, 1)
        got("yqf-", block(3, False), z, 2)
        send("x3", block(3, False), z, 0, xpart)

    def pump_x(k):
        got(f"x{k}", block(k, True), z, 0)
        send(f"z{k}+", block(k, True), z, 0, zp)
        send(f"z{k}-", block(k, True), z, 0, zm)

    def pump_z(k):
        got(f"z{k}+", block(k, True), z + 3, 0)
        send(f"z{k}f+", block(k, True), z + 3, 1, zp)
        got(f"z{k}-", block(k, True), z + 1, 0)
        send(f"z{k}f-", block(k, True), z + 1, 2, zm)

    def pump_r1():
        got("yr+1", block(1, False), z + 1, 0)
        send("yrf1", block(1, False), z + 1, 0, yp)
        got("yr-3", block(2, False), z + 3, 0)
        send("yrf3", block(2, False), z + 3, 0, ym)

    def pump_r2():
        got("yr+2", block(1, False), z + 2, 0)
        send("yrf2+", block(1, False), z + 2, 1, yp)
        got("yr-2", block(2, False), z + 2, 0)
        send("yrf2-", block(2, False), z + 2, 2, ym)

    def norm_block(i):
        r = pl.ds(pl.multiple_of(i * 48, 16), 48)
        normed[r, :] = norm_rows(tok[r, :].astype(F32)).astype(BF)

    loop(9, norm_block)

    def permute(i):
        xp[:, cols(i, 256)] = jnp.dot(
            p1[...], normed[:, cols(i, 256)], preferred_element_type=F32
        ).astype(BF)

    loop(4, permute)

    def hcopy(i, src_at, dst_at, rows, dev):
        return pltpu.make_async_remote_copy(
            src_ref=xp.at[pl.ds(src_at, rows), :], dst_ref=halo.at[pl.ds(dst_at, rows), :],
            send_sem=hs.at[i], recv_sem=hr.at[i], device_id=dev, device_id_type=MESH,
        )

    at = {k: v[0] for k, v in PIECE.items()}
    size = {k: v[1] for k, v in PIECE.items()}
    middle_sends = [
        hcopy(0, 0, HALO_E, 160, (lat, west)),
        hcopy(1, at[0, 2], HALO_W, 160, (lat, east)),
    ]
    north_sends = [
        hcopy(2, at[0, 0], HALO_S, 32, (lat - 1, lon)),
        hcopy(3, at[0, 1], HALO_S + 32, 48, (lat - 1, lon)),
        hcopy(4, at[0, 2], HALO_S + 80, 32, (lat - 1, lon)),
        hcopy(5, at[0, 0], HALO_SE, 32, (lat - 1, west)),
        hcopy(6, at[0, 2], HALO_SW, 32, (lat - 1, east)),
    ]
    south_sends = [
        hcopy(7, at[3, 0], HALO_N, 32, (lat + 1, lon)),
        hcopy(8, at[3, 1], HALO_N + 32, 48, (lat + 1, lon)),
        hcopy(9, at[3, 2], HALO_N + 80, 32, (lat + 1, lon)),
        hcopy(10, at[3, 0], HALO_NE, 32, (lat + 1, west)),
        hcopy(11, at[3, 2], HALO_NW, 32, (lat + 1, east)),
    ]
    for cp in middle_sends:
        cp.start()

    @pl.when(north)
    def _():
        for cp in north_sends:
            cp.start()

    @pl.when(south)
    def _():
        for cp in south_sends:
            cp.start()

    @pl.when(jnp.logical_not(north))
    def _():
        halo[HALO_N : HALO_N + 112, :] = jnp.zeros((112, D), BF)
        halo[HALO_NW : HALO_NW + 64, :] = jnp.zeros((64, D), BF)

    @pl.when(jnp.logical_not(south))
    def _():
        halo[HALO_S : HALO_S + 112, :] = jnp.zeros((112, D), BF)
        halo[HALO_SW : HALO_SW + 64, :] = jnp.zeros((64, D), BF)

    local[0].wait()

    def project(i):
        qkv[:, cols(i, 256)] = jnp.dot(
            xp[...], qkvv[:, cols(i, 256)], preferred_element_type=F32
        ).astype(BF)

    loop(6, project)
    pump_y()
    pump_x(0)
    loop(6, lambda i: project(i + 6))

    for cp in middle_sends:
        cp.wait_recv()

    @pl.when(north)
    def _():
        for cp in south_sends:
            cp.wait_recv()

    @pl.when(south)
    def _():
        for cp in north_sends:
            cp.wait_recv()

    def project_halo(i):
        kvh[:, cols(i, 256)] = jnp.dot(
            halo[...], qkvv[:, cols(i, 256, D)], preferred_element_type=F32
        ).astype(BF)

    loop(8, project_halo)
    pump_y2()
    pump_x(1)
    pump_x(2)
    pump_z(0)

    edge = jnp.where(north, jnp.where(south, 0, 2), 1)
    low = lax.broadcasted_iota(jnp.int32, (1, 128), 1) < 64

    def pair(i):
        head = cols(i, 128)
        head_k, head_v = cols(i, 128, D), cols(i, 128, 2 * D)
        for w, ((start, rows, _), parts) in enumerate(WINDOWS):
            r = slice(start, start + rows)
            q = qkv[r, head] * jnp.asarray(0.125, BF)
            zero = jnp.zeros_like(q)
            q = jnp.concatenate([jnp.where(low, q, zero), jnp.where(low, zero, q)], axis=0)
            ks, vs = [qkv[r, head_k]], [qkv[r, head_v]]
            for off, prows, _, _ in parts:
                ks.append(kvh[off : off + prows, head])
                vs.append(kvh[off : off + prows, head_k])
            k = jnp.concatenate(ks, axis=0) if parts else ks[0]
            v = jnp.concatenate(vs, axis=0) if parts else vs[0]
            m = k.shape[0]
            s = lax.dot_general(q, k, (((1,), (1,)), ((), ())), preferred_element_type=F32)
            s = s + bias[edge, w : w + 1, :m]
            e = jnp.exp(s - jnp.max(s, axis=-1, keepdims=True)).astype(BF)
            ve = jnp.concatenate([v, jnp.ones((m, 128), BF)], axis=1)
            o = jnp.dot(e, ve, preferred_element_type=F32)
            num = jnp.where(low, o[:rows, :128], o[rows:, :128])
            den = jnp.where(low, o[:rows, 128:], o[rows:, 128:])
            att[r, head] = (num / den).astype(BF)

    loop(4, pair)
    pump_x(3)
    pump_r1()
    pump_z(1)
    loop(4, lambda i: pair(i + 4))
    pump_z(2)
    pump_r2()

    local[1].wait()

    def unpermute(i):
        attr[:, cols(i, 256)] = jnp.dot(
            p1tv[...], att[:, cols(i, 256)], preferred_element_type=F32
        ).astype(BF)

    loop(4, unpermute)
    local[2].wait()

    def out_project(i):
        mixed = jnp.dot(attr[...], outv[:, cols(i, 256)], preferred_element_type=F32)
        mid[:, cols(i, 256)] = (tok[:, cols(i, 256)].astype(F32) + mixed).astype(BF)

    loop(4, out_project)
    store_mid = pltpu.make_async_copy(mid, mid_out, lsem.at[5])
    store_mid.start()
    local[3].wait()

    def patch(i):
        g, t = i // 4, i % 4
        mgd[:, cols(i, 256)] = jnp.dot(
            pgv[pl.ds(pl.multiple_of(g * GROUP, 16), GROUP), :], mid[:, cols(t, 256)],
            preferred_element_type=F32,
        ).astype(BF)

    loop(16, patch)

    def merge_norm(i):
        r = pl.ds(pl.multiple_of(i * 16, 16), 16)
        mgd[r, :] = norm_rows(mgd[r, :].astype(F32)).astype(BF)

    loop(GROUP // 16, merge_norm)
    store_mgd = pltpu.make_async_copy(mgd, merged_out, lsem.at[6])
    store_mgd.start()

    pump_z(3)
    got("yr+3", block(1, False), z + 3, 0)
    got("yr-1", block(2, False), z + 1, 0)
    got("yrf1", block(3, False), z + 1, 0)
    got("yrf3", block(3, False), z + 3, 0)
    got("yrf2+", block(3, False), z + 2, 1)
    got("yrf2-", block(3, False), z + 2, 2)
    for k in range(4):
        got(f"z{k}f+", block(k, True), z + 2, 1)
        got(f"z{k}f-", block(k, True), z + 2, 2)
    for name in sends:
        sends[name].wait_send()
    for cp in middle_sends:
        cp.wait_send()

    @pl.when(north)
    def _():
        for cp in north_sends:
            cp.wait_send()

    @pl.when(south)
    def _():
        for cp in south_sends:
            cp.wait_send()

    local[4].wait()
    store_mid.wait()
    store_mgd.wait()


AG = {n: i for i, n in enumerate(["01", "10", "30", "11", "31", "20a", "20b", "21a", "21b"])}


def gelu(x):
    return 0.5 * x * (1.0 + lax.erf(x * np.float32(0.5**0.5)))


def coarse_kernel(
    merged, wg, up, down,
    out,
    xs, wv, up2, down2, cc, theirs, coarse, cn, hid, acc, pt, rb,
    lsem, ss, sr, ags, agr, rss, rsr,
):
    lat, lon, z, xl, y, xh, c = place()
    sibling = (lat, lon + 1 - 2 * c)
    yp = (lat, (lon + 4) % 16)
    ym = (lat, (lon + 12) % 16)
    y2 = (lat, (lon + 8) % 16)
    lat_x, lon_x = 2 * z + 1 - xl, 4 * y + 2 * (1 - xh) + c
    xpart = (lat_x, lon_x)
    xyp = (lat_x, (lon_x + 4) % 16)
    xym = (lat_x, (lon_x + 12) % 16)
    xy2 = (lat_x, (lon_x + 8) % 16)
    barrier = pltpu.get_barrier_semaphore()
    everyone = (sibling, yp, ym, y2, xpart, xyp, xym, xy2)
    for dev in everyone:
        pl.semaphore_signal(barrier, inc=1, device_id=dev, device_id_type=MESH)

    mine = pl.ds(pl.multiple_of(c * GROUP, 16), GROUP)
    half = pl.ds(pl.multiple_of(c * 512, 128), 512)
    local = [
        pltpu.make_async_copy(merged, xs.at[mine, :], lsem.at[0]),
        pltpu.make_async_copy(up, up2.at[:, half], lsem.at[1]),
        pltpu.make_async_copy(down, down2.at[half, :], lsem.at[2]),
    ]
    load_w = [
        pltpu.make_async_copy(wg.at[j], wv.at[:, pl.ds(j * 128, 128)], lsem.at[3 + j])
        for j in range(8)
    ]
    local[0].start()
    for cp in load_w:
        cp.start()
    local[1].start()
    local[2].start()

    def remote(src, dst, s, r, i, dev):
        return pltpu.make_async_remote_copy(
            src_ref=src, dst_ref=dst, send_sem=s.at[i], recv_sem=r.at[i], device_id=dev,
            device_id_type=MESH,
        )

    pl.semaphore_wait(barrier, len(everyone))
    pair = [
        remote(merged, xs.at[mine, :], ss, sr, 0, sibling),
        remote(up, up2.at[:, half], ss, sr, 1, sibling),
        remote(down, down2.at[half, :], ss, sr, 2, sibling),
    ]
    for cp in pair:
        cp.start()
    local[0].wait()
    pair[0].wait_recv()
    for cp in load_w:
        cp.wait()

    def merge(i):
        v = jnp.dot(xs[...], wv[:, cols(i, 256)], preferred_element_type=F32).astype(BF)
        cc[0, :, cols(i, 256)] = v[:GROUP]
        cc[1, :, cols(i, 256)] = v[GROUP:]

    loop(4, merge)
    swap = remote(cc.at[1 - c], theirs, ss, sr, 3, sibling)
    swap.start()
    for j in range(8):
        coarse[:, pl.ds(pl.multiple_of((2 * j + c) * 128, 128), 128)] = cc[c, :, j * 128 : (j + 1) * 128]
    swap.wait_recv()
    for j in range(8):
        coarse[:, pl.ds(pl.multiple_of((2 * j + 1 - c) * 128, 128), 128)] = theirs[:, j * 128 : (j + 1) * 128]

    def coarse_norm(i):
        r = pl.ds(pl.multiple_of(i * 16, 16), 16)
        cn[0, 0, r, :] = norm_rows(coarse[r, :].astype(F32)).astype(BF)

    loop(GROUP // 16, coarse_norm)

    own = cn.at[0, 0]
    other = cn.at[0, 1]
    ag = {
        "01": remote(own, cn.at[0, 1], ags, agr, AG["01"], xpart),
        "30": remote(own, cn.at[3, 0], ags, agr, AG["30"], yp),
        "10": remote(own, cn.at[1, 0], ags, agr, AG["10"], ym),
        "31": remote(other, cn.at[3, 1], ags, agr, AG["31"], yp),
        "11": remote(other, cn.at[1, 1], ags, agr, AG["11"], ym),
    }
    A, B = pl.ds(0, 64), pl.ds(64, 48)
    for f in (0, 1):
        ag[f"2{f}a"] = remote(cn.at[3, f, A, :], cn.at[2, f, A, :], ags, agr, AG[f"2{f}a"], yp)
        ag[f"2{f}b"] = remote(cn.at[1, f, B, :], cn.at[2, f, B, :], ags, agr, AG[f"2{f}b"], ym)
    for n in ("01", "30", "10"):
        ag[n].start()

    def ffn(d, keep):
        def up_step(i):
            x = cn[d].reshape(2 * GROUP, DC)
            h = jnp.dot(x, up2[:, cols(i, 256)], preferred_element_type=F32)
            hid[:, cols(i, 256)] = gelu(h).astype(BF)

        loop(4, up_step)

        def down_step(i):
            t = cols(i, 512)
            v = jnp.dot(hid[...], down2[:, t], preferred_element_type=F32)
            if keep:
                acc[:, t] = v[:GROUP] + coarse[:, t].astype(F32)
            else:
                pt[d, 0, :, t] = v[:GROUP].astype(BF)
            pt[d, 1, :, t] = v[GROUP:].astype(BF)

        loop(4, down_step)

    owners = {1: (yp, xyp), 3: (ym, xym), 2: (y2, xy2), 0: (None, xpart)}
    rs = {}
    for d in range(4):
        for f in (0, 1):
            if (d, f) != (0, 0):
                e = (4 - d) % 4
                rs[d, f] = remote(pt.at[d, f], rb.at[e, f], rss, rsr, 2 * e + f, owners[d][f])

    local[1].wait()
    local[2].wait()
    pair[1].wait_recv()
    pair[2].wait_recv()
    ag["01"].wait_recv()
    ag["31"].start()
    ag["11"].start()
    ffn(0, True)
    rs[0, 1].start()
    ag["30"].wait_recv()
    ag["20a"].start()
    ag["10"].wait_recv()
    ag["20b"].start()
    ag["31"].wait_recv()
    ag["21a"].start()
    ag["11"].wait_recv()
    ag["21b"].start()
    ffn(1, False)
    rs[1, 0].start()
    rs[1, 1].start()
    ffn(3, False)
    rs[3, 0].start()
    rs[3, 1].start()
    for n in ("20a", "20b", "21a", "21b"):
        ag[n].wait_recv()
    ffn(2, False)
    rs[2, 0].start()
    rs[2, 1].start()
    for d, f in ((0, 1), (3, 0), (3, 1), (1, 0), (1, 1), (2, 0), (2, 1)):
        e = (4 - d) % 4
        rs[d, f].wait_recv()

        def add(i, e=e, f=f):
            acc[:, cols(i, 512)] += rb[e, f, :, cols(i, 512)].astype(F32)

        loop(4, add)
    for r in range(9):
        out[r] = acc[12 * r : 12 * r + 12, :].astype(BF)
    for cp in pair:
        cp.wait_send()
    swap.wait_send()
    for cp in ag.values():
        cp.wait_send()
    for cp in rs.values():
        cp.wait_send()


VM = pl.BlockSpec(memory_space=pltpu.VMEM)
ANY = pl.BlockSpec(memory_space=pl.ANY)
DMA = pltpu.SemaphoreType.DMA


def per_device(tokens, qkv_weight, out_weight, merge_weight, up_weight, down_weight):
    order, patch = _tables()
    p1 = jnp.asarray(order, BF)
    p1t = jnp.asarray(order.T, BF)
    pg = jnp.asarray(patch, BF)
    mid, merged, wg = pl.pallas_call(
        attention_kernel,
        name="attention",
        out_shape=(
            jax.ShapeDtypeStruct((CELLS, D), BF),
            jax.ShapeDtypeStruct((GROUP, 4 * D), BF),
            jax.ShapeDtypeStruct((8, 4 * D, 128), BF),
        ),
        in_specs=[VM, VM, VM, ANY, ANY, ANY, ANY, ANY],
        out_specs=(ANY, ANY, ANY),
        scratch_shapes=[
            pltpu.VMEM((D, 3 * D), BF),
            pltpu.VMEM((D, D), BF),
            pltpu.VMEM((CELLS, OWN), BF),
            pltpu.VMEM((4 * GROUP, CELLS), BF),
            pltpu.VMEM((CELLS, D), BF),
            pltpu.VMEM((OWN, D), BF),
            pltpu.VMEM((HALO, D), BF),
            pltpu.VMEM((OWN, 3 * D), BF),
            pltpu.VMEM((HALO, 2 * D), BF),
            pltpu.VMEM((OWN, D), BF),
            pltpu.VMEM((CELLS, D), BF),
            pltpu.VMEM((CELLS, D), BF),
            pltpu.VMEM((GROUP, 4 * D), BF),
            DMA((7,)),
            DMA((HALO_SENDS,)),
            DMA((HALO_SENDS,)),
            DMA((len(WSEMS),)),
            DMA((len(WSEMS),)),
        ],
        compiler_params=pltpu.CompilerParams(
            collective_id=0, has_side_effects=True, vmem_limit_bytes=50 * 2**20
        ),
    )(tokens.reshape(CELLS, D), p1, jnp.asarray(_bias()), qkv_weight, out_weight, merge_weight, p1t, pg)
    coarse_out = pl.pallas_call(
        coarse_kernel,
        name="coarse",
        out_shape=jax.ShapeDtypeStruct((ROWS // 2, COLS // 2, DC), BF),
        in_specs=[ANY, ANY, ANY, ANY],
        out_specs=VM,
        scratch_shapes=[
            pltpu.VMEM((2 * GROUP, 4 * D), BF),
            pltpu.VMEM((4 * D, D), BF),
            pltpu.VMEM((DC, D), BF),
            pltpu.VMEM((D, DC), BF),
            pltpu.VMEM((2, GROUP, D), BF),
            pltpu.VMEM((GROUP, D), BF),
            pltpu.VMEM((GROUP, DC), BF),
            pltpu.VMEM((4, 2, GROUP, DC), BF),
            pltpu.VMEM((2 * GROUP, D), BF),
            pltpu.VMEM((GROUP, DC), F32),
            pltpu.VMEM((4, 2, GROUP, DC), BF),
            pltpu.VMEM((4, 2, GROUP, DC), BF),
            DMA((11,)),
            DMA((4,)),
            DMA((4,)),
            DMA((len(AG),)),
            DMA((len(AG),)),
            DMA((8,)),
            DMA((8,)),
        ],
        compiler_params=pltpu.CompilerParams(
            collective_id=1, has_side_effects=True, vmem_limit_bytes=50 * 2**20
        ),
    )(merged, wg, up_weight, down_weight)
    return mid.reshape(ROWS, COLS, D), coarse_out


def solution(mesh):
    return jax.shard_map(
        per_device,
        mesh=mesh,
        in_specs=(P("lat", "lon", None), P(), P(), P(None, "lon"), P(None, "lon"), P("lon", None)),
        out_specs=(P("lat", "lon", None), P("lat", "lon", None)),
        check_vma=False,
    )
```

```python
import functools

import jax
import jax.numpy as jnp
import numpy as np
from jax import lax
from jax.experimental import pallas as pl
from jax.experimental.pallas import tpu as pltpu
from jax.sharding import PartitionSpec as P

MESH = pl.DeviceIdType.MESH
BF = jnp.bfloat16
F32 = jnp.float32
NEG = -1e30

ROWS, COLS, D, DC, HEADS = 18, 24, 1024, 2048, 16
CELLS = ROWS * COLS
GROUP = 112
HIGH = (3, 6, 6, 3)
WIDE = (6, 12, 6)
TOP = (0, 3, 9, 15)
LEFT = (0, 6, 18)


def _round(n):
    return -(-n // 16) * 16


PIECE = {}
_at = 0
for _b in range(3):
    for _a in range(4):
        PIECE[_a, _b] = (_at, _round(HIGH[_a] * WIDE[_b]), HIGH[_a] * WIDE[_b])
        _at += PIECE[_a, _b][1]
OWN = _at
HALO_W, HALO_E, HALO_N, HALO_S = 0, 160, 320, 432
HALO_NW, HALO_NE, HALO_SW, HALO_SE = 544, 576, 608, 640
HALO = 672


def _tables():
    order = np.zeros((OWN, CELLS), np.float32)
    for (a, b), (at, _, _) in PIECE.items():
        k = 0
        for i in range(HIGH[a]):
            for j in range(WIDE[b]):
                order[at + k, (TOP[a] + i) * COLS + LEFT[b] + j] = 1
                k += 1
    patch = np.zeros((4 * GROUP, CELLS), np.float32)
    for g in range(4):
        for r in range(ROWS // 2):
            for c in range(COLS // 2):
                cell = (2 * r + g // 2) * COLS + 2 * c + g % 2
                patch[g * GROUP + r * (COLS // 2) + c, cell] = 1
    return order, patch


def _window_parts():
    out = []
    for b in range(3):
        for a in range(4):
            at, rows, valid = PIECE[a, b]
            parts = []
            side = "n" if a == 0 else "s" if a == 3 else ""
            if b == 0:
                off = PIECE[a, 2][0] - PIECE[0, 2][0]
                parts.append((HALO_W + off, PIECE[a, 2][1], PIECE[a, 2][2], ""))
            if b == 2:
                off = PIECE[a, 0][0]
                parts.append((HALO_E + off, PIECE[a, 0][1], PIECE[a, 0][2], ""))
            if a == 0:
                off = HALO_N + (0, 32, 80)[b]
                parts.append((off, PIECE[3, b][1], PIECE[3, b][2], side))
            if a == 3:
                off = HALO_S + (0, 32, 80)[b]
                parts.append((off, PIECE[0, b][1], PIECE[0, b][2], side))
            corner = {(0, 0): HALO_NW, (0, 2): HALO_NE, (3, 0): HALO_SW, (3, 2): HALO_SE}
            if (a, b) in corner:
                parts.append((corner[a, b], 32, 18, side))
            out.append(((at, rows, valid), parts))
    return out


WINDOWS = _window_parts()


def _bias():
    bias = np.full((3, 16, 128), NEG, np.float32)
    for edge in range(3):
        for w, ((_, rows, valid), parts) in enumerate(WINDOWS):
            bias[edge, w, :valid] = 0
            at = rows
            for _, prows, pvalid, side in parts:
                gone = (edge == 1 and side == "n") or (edge == 2 and side == "s")
                if not gone:
                    bias[edge, w, at : at + pvalid] = 0
                at += prows
    return bias


def place():
    lat, lon = lax.axis_index("lat"), lax.axis_index("lon")
    z, xl = lat // 2, lat % 2
    y, xh, c = lon // 4, (lon // 2) % 2, lon % 2
    return lat, lon, z, xl, y, xh, c


def norm_rows(x):
    center = x - jnp.mean(x, axis=-1, keepdims=True)
    spread = jnp.mean(center * center, axis=-1, keepdims=True)
    return center * lax.rsqrt(spread + 1e-5)


def loop(n, body):
    def step(i, carry):
        body(i)
        return carry

    lax.fori_loop(0, n, step, 0)


def cols(i, size, base=0):
    return pl.ds(pl.multiple_of(base + i * size, 128), size)


HALO_SENDS = 12
WSEMS = {}
for _n in (
    ["yq+", "yq-", "yqf+", "yqf-"]
    + [f"yr{s}{i}" for s in "+-" for i in (1, 2, 3)]
    + ["yrf1", "yrf3", "yrf2+", "yrf2-"]
    + [f"x{k}" for k in range(6)]
    + [f"z{k}{s}" for k in range(6) for s in ("+", "-", "f+", "f-")]
    + [f"s{k}{i}" for k in (4, 5) for i in range(5)]
    + ["up", "down", "merged", "swap"]
    + ["ag+", "ag-", "ag2+", "ag2-", "rs1", "rs2", "rs3"]
):
    WSEMS[_n] = len(WSEMS)
A_ROWS, B_ROWS = pl.ds(0, 64), pl.ds(64, 48)


def gelu(x):
    return 0.5 * x * (1.0 + lax.erf(x * np.float32(0.5**0.5)))


def kernel(
    tok_in, p1_in, bias, qkvw, outw, mw, p1t_in, pg_in, up, down,
    mid_out, out,
    tok, p1, p1t, pg, qkvv, outv, wv, up4, down4,
    normed, xp, halo, qkv, kvh, mid, mgd,
    xs, cc, theirs, coarse, cn, hid, acc, pt, rb,
    lsem, hs, hr, ws, wr,
):
    lat, lon, z, xl, y, xh, c = place()
    north, south = lat > 0, lat < 7
    west, east = (lon + 15) % 16, (lon + 1) % 16
    yp = (lat, (lon + 4) % 16)
    ym = (lat, (lon + 12) % 16)
    y2 = (lat, (lon + 8) % 16)
    zp = ((lat + 2) % 8, lon)
    zm = ((lat + 6) % 8, lon)
    xpart = (2 * z + 1 - xl, 4 * y + 2 * (1 - xh) + c)
    sibling = (lat, lon + 1 - 2 * c)

    barrier = pltpu.get_barrier_semaphore()

    def greet(dev):
        pl.semaphore_signal(barrier, inc=1, device_id=dev, device_id_type=MESH)

    partners = ((lat, west), (lat, east), yp, ym, y2, zp, zm, xpart, sibling)
    for dev in partners:
        greet(dev)

    @pl.when(north)
    def _():
        for o in (west, lon, east):
            greet((lat - 1, o))

    @pl.when(south)
    def _():
        for o in (west, lon, east):
            greet((lat + 1, o))

    own = 2 * y + xh
    local = [
        pltpu.make_async_copy(tok_in, tok, lsem.at[0]),
        pltpu.make_async_copy(p1_in, p1, lsem.at[1]),
        pltpu.make_async_copy(qkvw, qkvv, lsem.at[2]),
        pltpu.make_async_copy(p1t_in, p1t, lsem.at[3]),
        pltpu.make_async_copy(outw, outv, lsem.at[4]),
        pltpu.make_async_copy(pg_in, pg, lsem.at[5]),
        pltpu.make_async_copy(mw, wv.at[own], lsem.at[6]),
        pltpu.make_async_copy(up, up4.at[0], lsem.at[7]),
        pltpu.make_async_copy(down, down4.at[0], lsem.at[8]),
    ]
    for cp in local:
        cp.start()

    count = len(partners) + jnp.where(north, 3, 0) + jnp.where(south, 3, 0)
    pl.semaphore_wait(barrier, count)

    def block(k, other):
        yy = (y + (0, 3, 1, 2)[k]) % 4
        return 2 * yy + (1 - xh if other else xh)

    def rows_of(size, quarter, part):
        base = (quarter % 4) * size
        if part == 0:
            return pl.ds(pl.multiple_of(base, size), size)
        return pl.ds(pl.multiple_of(base + (part - 1) * (size // 2), size // 2), size // 2)

    sends = {}

    def remote(name, src, dst, dev):
        i = WSEMS[name]
        return pltpu.make_async_remote_copy(
            src_ref=src, dst_ref=dst, send_sem=ws.at[i], recv_sem=wr.at[i],
            device_id=dev, device_id_type=MESH,
        )

    def send(name, src, dst, dev):
        sends[name] = remote(name, src, dst, dev)
        sends[name].start()

    def await_to(name, dst):
        remote(name, dst, dst, yp).wait_recv()

    def near(k, quarter, part):
        return wv.at[block(k, False), rows_of(1024, quarter, part), :]

    def send_own(name, quarter, dev):
        send(name, mw.at[rows_of(1024, quarter, 0), :], near(0, quarter, 0), dev)

    def far(k, quarter, part):
        if k < 4:
            return wv.at[block(k, True), rows_of(1024, quarter, part), :]
        if k == 4:
            return up4.at[2, rows_of(512, quarter, part), :]
        return down4.at[2, rows_of(128, quarter, part), :]

    send("x0", mw.at[rows_of(1024, z, 0), :], near(0, z, 0), xpart)
    send_own("yq+", z, yp)
    send_own("yq-", z, ym)

    def pump_y():
        await_to("yq+", near(1, z, 0))
        send("yqf+", near(1, z, 1), near(1, z, 1), yp)
        send("x1", near(1, z, 0), near(1, z, 0), xpart)
        await_to("yq-", near(2, z, 0))
        send("yqf-", near(2, z, 2), near(2, z, 2), ym)
        send("x2", near(2, z, 0), near(2, z, 0), xpart)
        for i in (1, 3, 2):
            send_own(f"yr+{i}", z + i, yp)
            send_own(f"yr-{i}", z + i, ym)

    def pump_y2():
        await_to("yqf+", near(3, z, 1))
        await_to("yqf-", near(3, z, 2))
        send("x3", near(3, z, 0), near(3, z, 0), xpart)

    def send_ffn():
        send("x4", up.at[rows_of(512, z, 0), :], far(4, z, 0), xpart)
        send("x5", down.at[rows_of(128, z, 0), :], far(5, z, 0), xpart)

    def share(k, i, quarter, part):
        if k >= 4:
            src = far(k, quarter, part)
            to = up4 if k == 4 else down4
            dst = to.at[3, rows_of(512 if k == 4 else 128, quarter, part), :]
            send(f"s{k}{i}", src, dst, sibling)

    def pump_x(k):
        await_to(f"x{k}", far(k, z, 0))
        send(f"z{k}+", far(k, z, 0), far(k, z, 0), zp)
        send(f"z{k}-", far(k, z, 0), far(k, z, 0), zm)
        share(k, 0, z, 0)

    def pump_z(k):
        await_to(f"z{k}+", far(k, z + 3, 0))
        send(f"z{k}f+", far(k, z + 3, 1), far(k, z + 3, 1), zp)
        share(k, 1, z + 3, 0)
        await_to(f"z{k}-", far(k, z + 1, 0))
        send(f"z{k}f-", far(k, z + 1, 2), far(k, z + 1, 2), zm)
        share(k, 2, z + 1, 0)

    def end_z(k):
        await_to(f"z{k}f+", far(k, z + 2, 1))
        share(k, 3, z + 2, 1)
        await_to(f"z{k}f-", far(k, z + 2, 2))
        share(k, 4, z + 2, 2)

    def pump_r1():
        await_to("yr+1", near(1, z + 1, 0))
        send("yrf1", near(1, z + 1, 0), near(1, z + 1, 0), yp)
        await_to("yr-3", near(2, z + 3, 0))
        send("yrf3", near(2, z + 3, 0), near(2, z + 3, 0), ym)

    def pump_r2():
        await_to("yr+2", near(1, z + 2, 0))
        send("yrf2+", near(1, z + 2, 1), near(1, z + 2, 1), yp)
        await_to("yr-2", near(2, z + 2, 0))
        send("yrf2-", near(2, z + 2, 2), near(2, z + 2, 2), ym)

    local[0].wait()

    def norm_block(i):
        r = pl.ds(pl.multiple_of(i * 48, 16), 48)
        normed[r, :] = norm_rows(tok[r, :].astype(F32)).astype(BF)

    loop(9, norm_block)
    local[1].wait()

    def permute(i):
        xp[:, cols(i, 256)] = jnp.dot(
            p1[...], normed[:, cols(i, 256)], preferred_element_type=F32
        ).astype(BF)

    loop(4, permute)

    def hcopy(i, src_at, dst_at, rows, dev):
        return pltpu.make_async_remote_copy(
            src_ref=xp.at[pl.ds(src_at, rows), :], dst_ref=halo.at[pl.ds(dst_at, rows), :],
            send_sem=hs.at[i], recv_sem=hr.at[i], device_id=dev, device_id_type=MESH,
        )

    at = {k: v[0] for k, v in PIECE.items()}
    middle_sends = [
        hcopy(0, 0, HALO_E, 160, (lat, west)),
        hcopy(1, at[0, 2], HALO_W, 160, (lat, east)),
    ]
    north_sends = [
        hcopy(2, at[0, 0], HALO_S, 32, (lat - 1, lon)),
        hcopy(3, at[0, 1], HALO_S + 32, 48, (lat - 1, lon)),
        hcopy(4, at[0, 2], HALO_S + 80, 32, (lat - 1, lon)),
        hcopy(5, at[0, 0], HALO_SE, 32, (lat - 1, west)),
        hcopy(6, at[0, 2], HALO_SW, 32, (lat - 1, east)),
    ]
    south_sends = [
        hcopy(7, at[3, 0], HALO_N, 32, (lat + 1, lon)),
        hcopy(8, at[3, 1], HALO_N + 32, 48, (lat + 1, lon)),
        hcopy(9, at[3, 2], HALO_N + 80, 32, (lat + 1, lon)),
        hcopy(10, at[3, 0], HALO_NE, 32, (lat + 1, west)),
        hcopy(11, at[3, 2], HALO_NW, 32, (lat + 1, east)),
    ]
    for cp in middle_sends:
        cp.start()

    @pl.when(north)
    def _():
        for cp in north_sends:
            cp.start()

    @pl.when(south)
    def _():
        for cp in south_sends:
            cp.start()

    @pl.when(jnp.logical_not(north))
    def _():
        halo[HALO_N : HALO_N + 112, :] = jnp.zeros((112, D), BF)
        halo[HALO_NW : HALO_NW + 64, :] = jnp.zeros((64, D), BF)

    @pl.when(jnp.logical_not(south))
    def _():
        halo[HALO_S : HALO_S + 112, :] = jnp.zeros((112, D), BF)
        halo[HALO_SW : HALO_SW + 64, :] = jnp.zeros((64, D), BF)

    pump_y()
    local[2].wait()

    def project(i):
        qkv[:, cols(i, 256)] = jnp.dot(
            xp[...], qkvv[:, cols(i, 256)], preferred_element_type=F32
        ).astype(BF)

    loop(12, project)
    pump_x(0)
    pump_y2()
    send("up", up, up4.at[1], sibling)
    send("down", down, down4.at[1], sibling)

    for cp in middle_sends:
        cp.wait()

    @pl.when(north)
    def _():
        for cp in south_sends:
            cp.wait_recv()
        for cp in north_sends:
            cp.wait_send()

    @pl.when(south)
    def _():
        for cp in north_sends:
            cp.wait_recv()
        for cp in south_sends:
            cp.wait_send()

    def project_halo(i):
        kvh[:, cols(i, 256)] = jnp.dot(
            halo[...], qkvv[:, cols(i, 256, D)], preferred_element_type=F32
        ).astype(BF)

    loop(8, project_halo)
    pump_x(1)
    pump_x(2)
    pump_z(0)

    edge = jnp.where(north, jnp.where(south, 0, 2), 1)
    low = lax.broadcasted_iota(jnp.int32, (1, 128), 1) < 64
    att = xp

    def pair(i):
        head = cols(i, 128)
        head_k, head_v = cols(i, 128, D), cols(i, 128, 2 * D)
        for w, ((start, rows, _), parts) in enumerate(WINDOWS):
            r = slice(start, start + rows)
            q = qkv[r, head] * jnp.asarray(0.125, BF)
            zero = jnp.zeros_like(q)
            q = jnp.concatenate([jnp.where(low, q, zero), jnp.where(low, zero, q)], axis=0)
            ks, vs = [qkv[r, head_k]], [qkv[r, head_v]]
            for off, prows, _, _ in parts:
                ks.append(kvh[off : off + prows, head])
                vs.append(kvh[off : off + prows, head_k])
            k = jnp.concatenate(ks, axis=0) if parts else ks[0]
            v = jnp.concatenate(vs, axis=0) if parts else vs[0]
            m = k.shape[0]
            s = lax.dot_general(q, k, (((1,), (1,)), ((), ())), preferred_element_type=F32)
            s = s + bias[edge, w : w + 1, :m]
            e = jnp.exp(s - jnp.max(s, axis=-1, keepdims=True)).astype(BF)
            ve = jnp.concatenate([v, jnp.ones((m, 128), BF)], axis=1)
            o = jnp.dot(e, ve, preferred_element_type=F32)
            num = jnp.where(low, o[:rows, :128], o[rows:, :128])
            den = jnp.where(low, o[:rows, 128:], o[rows:, 128:])
            att[r, head] = (num / den).astype(BF)

    def pair_late(i):
        pair(i + 4)

    loop(4, pair)
    pump_x(3)
    pump_r1()
    pump_z(1)
    send_ffn()
    loop(4, pair_late)
    pump_z(2)
    pump_r2()

    local[3].wait()
    attr = normed

    def unpermute(i):
        attr[:, cols(i, 256)] = jnp.dot(
            p1t[...], att[:, cols(i, 256)], preferred_element_type=F32
        ).astype(BF)

    loop(4, unpermute)
    local[4].wait()

    def out_project(i):
        mixed = jnp.dot(attr[...], outv[:, cols(i, 256)], preferred_element_type=F32)
        mid[:, cols(i, 256)] = (tok[:, cols(i, 256)].astype(F32) + mixed).astype(BF)

    loop(4, out_project)
    store_mid = pltpu.make_async_copy(mid, mid_out, lsem.at[9])
    store_mid.start()
    pump_z(3)
    local[5].wait()

    def patch(i):
        g, t = i // 4, i % 4
        mgd[:, cols(i, 256)] = jnp.dot(
            pg[pl.ds(pl.multiple_of(g * GROUP, 16), GROUP), :], mid[:, cols(t, 256)],
            preferred_element_type=F32,
        ).astype(BF)

    loop(16, patch)

    def merge_norm(i):
        r = pl.ds(pl.multiple_of(i * 16, 16), 16)
        mgd[r, :] = norm_rows(mgd[r, :].astype(F32)).astype(BF)

    loop(GROUP // 16, merge_norm)
    mine = pl.ds(pl.multiple_of(c * GROUP, 16), GROUP)
    send("merged", mgd, xs.at[mine, :], sibling)
    keep_mgd = pltpu.make_async_copy(mgd, xs.at[mine, :], lsem.at[10])
    keep_mgd.start()

    local[6].wait()
    await_to("yr+3", near(1, z + 3, 0))
    await_to("yr-1", near(2, z + 1, 0))
    await_to("yrf1", near(3, z + 1, 0))
    await_to("yrf3", near(3, z + 3, 0))
    await_to("yrf2+", near(3, z + 2, 1))
    await_to("yrf2-", near(3, z + 2, 2))
    for k in range(4):
        end_z(k)
    pump_x(4)
    pump_x(5)
    keep_mgd.wait()
    theirs_rows = pl.ds(pl.multiple_of((1 - c) * GROUP, 16), GROUP)
    await_to("merged", xs.at[theirs_rows, :])

    def merge(i):
        v = jnp.zeros((2 * GROUP, 256), F32)
        for g in range(4):
            r = slice(g * D, (g + 1) * D)
            w = jnp.concatenate([wv[2 * i, r, :], wv[2 * i + 1, r, :]], axis=1)
            v += jnp.dot(xs[:, r], w, preferred_element_type=F32)
        v = v.astype(BF)
        cc[0, :, cols(i, 256)] = v[:GROUP]
        cc[1, :, cols(i, 256)] = v[GROUP:]

    loop(4, merge)
    send("swap", cc.at[1 - c], theirs, sibling)
    for j in range(8):
        coarse[:, pl.ds(pl.multiple_of((2 * j + c) * 128, 128), 128)] = cc[c, :, j * 128 : (j + 1) * 128]
    await_to("swap", theirs)
    for j in range(8):
        coarse[:, pl.ds(pl.multiple_of((2 * j + 1 - c) * 128, 128), 128)] = theirs[:, j * 128 : (j + 1) * 128]

    def coarse_norm(i):
        r = pl.ds(pl.multiple_of(i * 16, 16), 16)
        cn[0, r, :] = norm_rows(coarse[r, :].astype(F32)).astype(BF)

    loop(GROUP // 16, coarse_norm)

    send("ag+", cn.at[0], cn.at[2], yp)
    send("ag-", cn.at[0], cn.at[3], ym)
    pump_z(4)
    pump_z(5)
    for n in (7, 8):
        local[n].wait()
    await_to("up", up4.at[1])
    await_to("down", down4.at[1])

    def ffn(first, count):
        rows = count * GROUP

        def up_step(i):
            q, t = i // 2, i % 2
            x = cn[first : first + count].reshape(rows, DC)
            h = jnp.dot(x, up4[q, :, cols(t, 256)], preferred_element_type=F32)
            hid[:rows, cols(i, 256)] = gelu(h).astype(BF)

        loop(8, up_step)

        def down_step(i):
            t = cols(i, 256)
            v = jnp.zeros((rows, 256), F32)
            for q in range(4):
                v += jnp.dot(hid[:rows, q * 512 : (q + 1) * 512], down4[q, :, t], preferred_element_type=F32)
            for n in range(count):
                part = v[n * GROUP : (n + 1) * GROUP]
                if first + n == 0:
                    acc[:, t] = part + coarse[:, t].astype(F32)
                else:
                    pt[first + n, :, t] = part.astype(BF)

        loop(8, down_step)

    await_to("ag+", cn.at[2])
    send("ag2+", cn.at[2, A_ROWS, :], cn.at[1, A_ROWS, :], yp)
    await_to("ag-", cn.at[3])
    send("ag2-", cn.at[3, B_ROWS, :], cn.at[1, B_ROWS, :], ym)
    end_z(4)
    end_z(5)
    for k in (4, 5):
        to, size = (up4, 512) if k == 4 else (down4, 128)
        for i, (quarter, part) in enumerate(((z, 0), (z + 3, 0), (z + 1, 0), (z + 2, 1), (z + 2, 2))):
            await_to(f"s{k}{i}", to.at[3, rows_of(size, quarter, part), :])
    ffn(2, 2)
    send("rs2", pt.at[2], rb.at[3], ym)
    send("rs3", pt.at[3], rb.at[2], yp)
    await_to("ag2+", cn.at[1, A_ROWS, :])
    await_to("ag2-", cn.at[1, B_ROWS, :])
    ffn(0, 2)
    send("rs1", pt.at[1], rb.at[1], y2)
    await_to("rs2", rb.at[3])
    await_to("rs3", rb.at[2])

    def add_near(i):
        t = cols(i, 512)
        acc[:, t] += rb[2, :, t].astype(F32) + rb[3, :, t].astype(F32)

    loop(4, add_near)
    await_to("rs1", rb.at[1])

    def add_far(i):
        t = cols(i, 512)
        acc[:, t] += rb[1, :, t].astype(F32)

    loop(4, add_far)
    for r in range(9):
        out[r] = acc[12 * r : 12 * r + 12, :].astype(BF)
    for cp in sends.values():
        cp.wait_send()
    store_mid.wait()


VM = pl.BlockSpec(memory_space=pltpu.VMEM)
HBM = pl.BlockSpec(memory_space=pltpu.HBM)
DMA = pltpu.SemaphoreType.DMA


def per_device(tokens, qkv_weight, out_weight, merge_weight, up_weight, down_weight):
    order, patch = _tables()
    p1 = jnp.asarray(order, BF)
    p1t = jnp.asarray(order.T, BF)
    pg = jnp.asarray(patch, BF)

    def vmem(*shape, kind=BF):
        return pltpu.VMEM(shape, kind)

    mid, coarse_out = pl.pallas_call(
        kernel,
        name="whole",
        out_shape=(
            jax.ShapeDtypeStruct((CELLS, D), BF),
            jax.ShapeDtypeStruct((ROWS // 2, COLS // 2, DC), BF),
        ),
        in_specs=[HBM, HBM, VM] + [HBM] * 7,
        out_specs=(HBM, VM),
        scratch_shapes=[
            vmem(CELLS, D),
            vmem(OWN, CELLS),
            vmem(CELLS, OWN),
            vmem(4 * GROUP, CELLS),
            vmem(D, 3 * D),
            vmem(D, D),
            vmem(8, 4 * D, 128),
            vmem(4, DC, 512),
            vmem(4, 512, DC),
            vmem(CELLS, D),
            vmem(OWN, D),
            vmem(HALO, D),
            vmem(OWN, 3 * D),
            vmem(HALO, 2 * D),
            vmem(CELLS, D),
            vmem(GROUP, 4 * D),
            vmem(2 * GROUP, 4 * D),
            vmem(2, GROUP, D),
            vmem(GROUP, D),
            vmem(GROUP, DC),
            vmem(4, GROUP, DC),
            vmem(2 * GROUP, DC),
            vmem(GROUP, DC, kind=F32),
            vmem(4, GROUP, DC),
            vmem(4, GROUP, DC),
            DMA((11,)),
            DMA((HALO_SENDS,)),
            DMA((HALO_SENDS,)),
            DMA((len(WSEMS),)),
            DMA((len(WSEMS),)),
        ],
        compiler_params=pltpu.CompilerParams(
            collective_id=0, has_side_effects=True, vmem_limit_bytes=62 * 2**20
        ),
    )(
        tokens.reshape(CELLS, D), p1, jnp.asarray(_bias()), qkv_weight, out_weight, merge_weight, p1t, pg,
        up_weight, down_weight,
    )
    return mid.reshape(ROWS, COLS, D), coarse_out


def solution(mesh):
    return jax.shard_map(
        per_device,
        mesh=mesh,
        in_specs=(P("lat", "lon", None), P(), P(), P(None, "lon"), P(None, "lon"), P("lon", None)),
        out_specs=(P("lat", "lon", None), P("lat", "lon", None)),
        check_vma=False,
    )
```

```python
import functools

import jax
import jax.numpy as jnp
import numpy as np
from jax import lax
from jax.experimental import pallas as pl
from jax.experimental.pallas import tpu as pltpu
from jax.sharding import PartitionSpec as P

MESH = pl.DeviceIdType.MESH
BF = jnp.bfloat16
F32 = jnp.float32
NEG = -1e30

ROWS, COLS, D, DC, HEADS = 18, 24, 1024, 2048, 16
CELLS = ROWS * COLS
GROUP = 112
HIGH = (3, 6, 6, 3)
WIDE = (6, 12, 6)
TOP = (0, 3, 9, 15)
LEFT = (0, 6, 18)


def _round(n):
    return -(-n // 16) * 16


PIECE = {}
_at = 0
for _b in range(3):
    for _a in range(4):
        PIECE[_a, _b] = (_at, _round(HIGH[_a] * WIDE[_b]), HIGH[_a] * WIDE[_b])
        _at += PIECE[_a, _b][1]
OWN = _at
SEND_W, SEND_E, SEND_N, SEND_S, SENT = 0, 112, 224, 304, 384
HALO_W, HALO_E, HALO_N, HALO_S = 0, 112, 224, 304
HALO_NW, HALO_NE, HALO_SW, HALO_SE = 384, 416, 448, 480
HALO = 512


def _tables():
    order = np.zeros((OWN, CELLS), np.float32)
    for (a, b), (at, _, _) in PIECE.items():
        k = 0
        for i in range(HIGH[a]):
            for j in range(WIDE[b]):
                order[at + k, (TOP[a] + i) * COLS + LEFT[b] + j] = 1
                k += 1
    packed = np.zeros((SENT, CELLS), np.float32)
    column = [(a, 0) for a in range(4)]
    for start, pieces in (
        (SEND_W, column),
        (SEND_E, [(a, 2) for a, _ in column]),
        (SEND_N, [(0, b) for b in range(3)]),
        (SEND_S, [(3, b) for b in range(3)]),
    ):
        k = start
        for a, b in pieces:
            n = PIECE[a, b][2]
            packed[k : k + n] = order[PIECE[a, b][0] : PIECE[a, b][0] + n]
            k += n
    patch = np.zeros((4 * GROUP, CELLS), np.float32)
    for g in range(4):
        for r in range(ROWS // 2):
            for c in range(COLS // 2):
                cell = (2 * r + g // 2) * COLS + 2 * c + g % 2
                patch[g * GROUP + r * (COLS // 2) + c, cell] = 1
    return order, packed, patch


def _span(base, start, count, side):
    low = start // 16 * 16
    return base + low, _round(start + count) - low, start - low, start - low + count, side


def _window_parts():
    out = []
    along, across = ((0, 18), (18, 36), (54, 36), (90, 18)), ((0, 18), (18, 36), (54, 18))
    for b in range(3):
        for a in range(4):
            side = "n" if a == 0 else "s" if a == 3 else ""
            parts = []
            if b != 1:
                parts.append(_span(HALO_W if b == 0 else HALO_E, *along[a], ""))
            if side:
                parts.append(_span(HALO_N if a == 0 else HALO_S, *across[b], side))
            corner = {(0, 0): HALO_NW, (0, 2): HALO_NE, (3, 0): HALO_SW, (3, 2): HALO_SE}
            if (a, b) in corner:
                first = 6 if b == 0 else 0
                parts.append((corner[a, b], 32, first, first + 18, side))
            out.append((PIECE[a, b], parts))
    return out


WINDOWS = _window_parts()


def _bias():
    bias = np.full((3, 16, 128), NEG, np.float32)
    for edge in range(3):
        for w, ((_, rows, valid), parts) in enumerate(WINDOWS):
            bias[edge, w, :valid] = 0
            at = rows
            for _, prows, first, last, side in parts:
                gone = (edge == 1 and side == "n") or (edge == 2 and side == "s")
                if not gone:
                    bias[edge, w, at + first : at + last] = 0
                at += prows
    return bias


def place():
    lat, lon = lax.axis_index("lat"), lax.axis_index("lon")
    z, xl = lat // 2, lat % 2
    y, xh, c = lon // 4, (lon // 2) % 2, lon % 2
    return lat, lon, z, xl, y, xh, c


def norm_rows(x):
    center = x - jnp.mean(x, axis=-1, keepdims=True)
    spread = jnp.mean(center * center, axis=-1, keepdims=True)
    return center * lax.rsqrt(spread + 1e-5)


def loop(n, body):
    def step(i, carry):
        body(i)
        return carry

    lax.fori_loop(0, n, step, 0)


def cols(i, size, base=0):
    return pl.ds(pl.multiple_of(base + i * size, 128), size)


HALO_SENDS = 8
WSEMS = {}
for _n in (
    ["yq+", "yq-", "yqf+", "yqf-"]
    + [f"yr{s}{i}" for s in "+-" for i in (1, 2, 3)]
    + ["yrf1", "yrf3", "yrf2+", "yrf2-"]
    + [f"x{k}" for k in range(6)]
    + [f"z{k}{s}" for k in range(6) for s in ("+", "-", "f+", "f-")]
    + [f"n{k}{i}" for k in (4, 5) for i in range(5)]
    + [f"s{k}{i}" for k in (4, 5) for i in range(2)]
    + ["up", "down", "merged", "swap0", "swap1"]
    + ["ag+", "ag-", "ag2+", "ag2-", "rs1", "rs2", "rs3"]
):
    WSEMS[_n] = len(WSEMS)
A_ROWS, B_ROWS = pl.ds(0, 64), pl.ds(64, 48)


def gelu(x):
    return 0.5 * x * (1.0 + lax.erf(x * np.float32(0.5**0.5)))


def kernel(
    tok_in, ps_in, p1_in, bias, qkvw, outw, mw, p1t_in, pg_in, up, down,
    mid_out, out,
    tok, ps, p1, p1t, pg, qkvv, outv, wv, up4, down4,
    normed, packed, xp, halo, qkv, kvh, mid, mgd,
    xs, cc, theirs, coarse, cn, hid, acc, pt, rb,
    lsem, hs, hr, ws, wr,
):
    lat, lon, z, xl, y, xh, c = place()
    north, south = lat > 0, lat < 7
    west, east = (lon + 15) % 16, (lon + 1) % 16
    yp = (lat, (lon + 4) % 16)
    ym = (lat, (lon + 12) % 16)
    y2 = (lat, (lon + 8) % 16)
    zp = ((lat + 2) % 8, lon)
    zm = ((lat + 6) % 8, lon)
    xpart = (2 * z + 1 - xl, 4 * y + 2 * (1 - xh) + c)
    xn = (lat + 1 - 2 * xl, lon)
    sibling = (lat, lon + 1 - 2 * c)

    barrier = pltpu.get_barrier_semaphore()

    def greet(dev):
        pl.semaphore_signal(barrier, inc=1, device_id=dev, device_id_type=MESH)

    partners = ((lat, west), (lat, east), yp, ym, y2, zp, zm, xpart, xn, sibling)
    for dev in partners:
        greet(dev)

    @pl.when(north)
    def _():
        for o in (west, lon, east):
            greet((lat - 1, o))

    @pl.when(south)
    def _():
        for o in (west, lon, east):
            greet((lat + 1, o))

    own = 2 * y + xh
    local = [
        pltpu.make_async_copy(tok_in, tok, lsem.at[0]),
        pltpu.make_async_copy(p1_in, p1, lsem.at[1]),
        pltpu.make_async_copy(qkvw, qkvv, lsem.at[2]),
        pltpu.make_async_copy(p1t_in, p1t, lsem.at[3]),
        pltpu.make_async_copy(outw, outv, lsem.at[4]),
        pltpu.make_async_copy(pg_in, pg, lsem.at[5]),
        pltpu.make_async_copy(mw, wv.at[own], lsem.at[6]),
        pltpu.make_async_copy(up, up4.at[0], lsem.at[7]),
        pltpu.make_async_copy(down, down4.at[0], lsem.at[8]),
    ]
    early = pltpu.make_async_copy(ps_in, ps, lsem.at[11])
    local[0].start()
    early.start()
    local[1].start()
    local[2].start()

    count = len(partners) + jnp.where(north, 3, 0) + jnp.where(south, 3, 0)
    pl.semaphore_wait(barrier, count)

    def block(k, other):
        yy = (y + (0, 3, 1, 2)[k]) % 4
        return 2 * yy + (1 - xh if other else xh)

    def rows_of(size, quarter, part):
        base = (quarter % 4) * size
        if part == 0:
            return pl.ds(pl.multiple_of(base, size), size)
        return pl.ds(pl.multiple_of(base + (part - 1) * (size // 2), size // 2), size // 2)

    sends = {}

    def remote(name, src, dst, dev):
        i = WSEMS[name]
        return pltpu.make_async_remote_copy(
            src_ref=src, dst_ref=dst, send_sem=ws.at[i], recv_sem=wr.at[i],
            device_id=dev, device_id_type=MESH,
        )

    def send(name, src, dst, dev):
        sends[name] = remote(name, src, dst, dev)
        sends[name].start()

    def await_to(name, dst):
        remote(name, dst, dst, yp).wait_recv()

    def near(k, quarter, part):
        return wv.at[block(k, False), rows_of(1024, quarter, part), :]

    def send_own(name, quarter, dev):
        send(name, mw.at[rows_of(1024, quarter, 0), :], near(0, quarter, 0), dev)

    def far(k, quarter, part, half=xl):
        if k < 4:
            return wv.at[block(k, True), rows_of(1024, quarter, part), :]
        size = 256 if k == 4 else 64
        base = (quarter % 4) * size + half * 4 * size
        if part == 0:
            rows = pl.ds(pl.multiple_of(base, size), size)
        else:
            rows = pl.ds(pl.multiple_of(base + (part - 1) * (size // 2), size // 2), size // 2)
        return (up4 if k == 4 else down4).at[2, rows, :]

    def half_rows(k, half):
        size = 1024 if k == 4 else 256
        return pl.ds(pl.multiple_of(half * size, size), size)

    def pump_y():
        await_to("yq+", near(1, z, 0))
        send("yqf+", near(1, z, 1), near(1, z, 1), yp)
        send("x1", near(1, z, 0), near(1, z, 0), xpart)
        await_to("yq-", near(2, z, 0))
        send("yqf-", near(2, z, 2), near(2, z, 2), ym)
        send("x2", near(2, z, 0), near(2, z, 0), xpart)
        for i in (1, 3, 2):
            send_own(f"yr+{i}", z + i, yp)
            send_own(f"yr-{i}", z + i, ym)

    def pump_y2():
        await_to("yqf+", near(3, z, 1))
        await_to("yqf-", near(3, z, 2))
        send("x3", near(3, z, 0), near(3, z, 0), xpart)

    def send_ffn():
        for k, w in ((4, up), (5, down)):
            size = 256 if k == 4 else 64
            base = (1 - xl) * 4 * size + z * size
            send(f"x{k}", w.at[pl.ds(pl.multiple_of(base, size), size), :], far(k, z, 0, 1 - xl), xpart)

    def pass_on(k, i, quarter, part):
        if k >= 4:
            send(f"n{k}{i}", far(k, quarter, part), far(k, quarter, part), xn)

    def pump_x(k):
        await_to(f"x{k}", far(k, z, 0))
        send(f"z{k}+", far(k, z, 0), far(k, z, 0), zp)
        send(f"z{k}-", far(k, z, 0), far(k, z, 0), zm)
        pass_on(k, 0, z, 0)

    def pump_z(k):
        await_to(f"z{k}+", far(k, z + 3, 0))
        send(f"z{k}f+", far(k, z + 3, 1), far(k, z + 3, 1), zp)
        pass_on(k, 1, z + 3, 0)
        await_to(f"z{k}-", far(k, z + 1, 0))
        send(f"z{k}f-", far(k, z + 1, 2), far(k, z + 1, 2), zm)
        pass_on(k, 2, z + 1, 0)

    def end_z(k):
        await_to(f"z{k}f+", far(k, z + 2, 1))
        pass_on(k, 3, z + 2, 1)
        await_to(f"z{k}f-", far(k, z + 2, 2))
        pass_on(k, 4, z + 2, 2)

    def share(k, i):
        to = up4 if k == 4 else down4
        rows = half_rows(k, xl if i == 0 else 1 - xl)
        send(f"s{k}{i}", to.at[2, rows, :], to.at[3, rows, :], sibling)

    def end_n(k):
        for i, (quarter, part) in enumerate(((z, 0), (z + 3, 0), (z + 1, 0), (z + 2, 1), (z + 2, 2))):
            await_to(f"n{k}{i}", far(k, quarter, part, 1 - xl))

    def pump_r1():
        await_to("yr+1", near(1, z + 1, 0))
        send("yrf1", near(1, z + 1, 0), near(1, z + 1, 0), yp)
        await_to("yr-3", near(2, z + 3, 0))
        send("yrf3", near(2, z + 3, 0), near(2, z + 3, 0), ym)

    def pump_r2():
        await_to("yr+2", near(1, z + 2, 0))
        send("yrf2+", near(1, z + 2, 1), near(1, z + 2, 1), yp)
        await_to("yr-2", near(2, z + 2, 0))
        send("yrf2-", near(2, z + 2, 2), near(2, z + 2, 2), ym)

    send("x0", mw.at[rows_of(1024, z, 0), :], near(0, z, 0), xpart)
    send_own("yq+", z, yp)
    send_own("yq-", z, ym)
    send_ffn()

    local[0].wait()

    def norm_block(i):
        r = pl.ds(pl.multiple_of(i * 48, 16), 48)
        normed[r, :] = norm_rows(tok[r, :].astype(F32)).astype(BF)

    loop(9, norm_block)
    for n in (6, 3, 4, 5):
        local[n].start()
    early.wait()

    def pack(i):
        packed[:, cols(i, 256)] = jnp.dot(
            ps[...], normed[:, cols(i, 256)], preferred_element_type=F32
        ).astype(BF)

    loop(4, pack)

    def hcopy(i, src_at, dst_at, rows, dev):
        return pltpu.make_async_remote_copy(
            src_ref=packed.at[pl.ds(src_at, rows), :], dst_ref=halo.at[pl.ds(dst_at, rows), :],
            send_sem=hs.at[i], recv_sem=hr.at[i], device_id=dev, device_id_type=MESH,
        )

    middle_sends = [
        hcopy(0, SEND_W, HALO_E, 112, (lat, west)),
        hcopy(1, SEND_E, HALO_W, 112, (lat, east)),
    ]
    north_sends = [
        hcopy(2, SEND_N, HALO_S, 80, (lat - 1, lon)),
        hcopy(3, SEND_N, HALO_SE, 32, (lat - 1, west)),
        hcopy(4, SEND_N + 48, HALO_SW, 32, (lat - 1, east)),
    ]
    south_sends = [
        hcopy(5, SEND_S, HALO_N, 80, (lat + 1, lon)),
        hcopy(6, SEND_S, HALO_NE, 32, (lat + 1, west)),
        hcopy(7, SEND_S + 48, HALO_NW, 32, (lat + 1, east)),
    ]
    for cp in middle_sends:
        cp.start()

    @pl.when(north)
    def _():
        for cp in north_sends:
            cp.start()

    @pl.when(south)
    def _():
        for cp in south_sends:
            cp.start()

    local[1].wait()

    def permute(i):
        xp[:, cols(i, 256)] = jnp.dot(
            p1[...], normed[:, cols(i, 256)], preferred_element_type=F32
        ).astype(BF)

    loop(4, permute)

    @pl.when(jnp.logical_not(north))
    def _():
        halo[HALO_N : HALO_N + 80, :] = jnp.zeros((80, D), BF)
        halo[HALO_NW : HALO_NW + 64, :] = jnp.zeros((64, D), BF)

    @pl.when(jnp.logical_not(south))
    def _():
        halo[HALO_S : HALO_S + 80, :] = jnp.zeros((80, D), BF)
        halo[HALO_SW : HALO_SW + 64, :] = jnp.zeros((64, D), BF)

    local[2].wait()

    def project(i):
        qkv[:, cols(i, 256)] = jnp.dot(
            xp[...], qkvv[:, cols(i, 256)], preferred_element_type=F32
        ).astype(BF)

    def project_late(i):
        project(i + 6)

    loop(6, project)
    pump_y()
    local[7].start()
    local[8].start()
    loop(6, project_late)
    pump_x(0)
    send("up", up, up4.at[1], sibling)
    send("down", down, down4.at[1], sibling)

    edge = jnp.where(north, jnp.where(south, 0, 2), 1)
    low = lax.broadcasted_iota(jnp.int32, (1, 128), 1) < 64

    def attend(i, inner):
        head = cols(i, 128)
        head_k, head_v = cols(i, 128, D), cols(i, 128, 2 * D)
        for w, ((start, rows, _), parts) in enumerate(WINDOWS):
            if inner == bool(parts):
                continue
            r = slice(start, start + rows)
            q = qkv[r, head] * jnp.asarray(0.125, BF)
            zero = jnp.zeros_like(q)
            q = jnp.concatenate([jnp.where(low, q, zero), jnp.where(low, zero, q)], axis=0)
            ks, vs = [qkv[r, head_k]], [qkv[r, head_v]]
            for off, prows, _, _, _ in parts:
                ks.append(kvh[off : off + prows, head])
                vs.append(kvh[off : off + prows, head_k])
            k = jnp.concatenate(ks, axis=0) if parts else ks[0]
            v = jnp.concatenate(vs, axis=0) if parts else vs[0]
            m = k.shape[0]
            s = lax.dot_general(q, k, (((1,), (1,)), ((), ())), preferred_element_type=F32)
            s = s + bias[edge, w : w + 1, :m]
            e = jnp.exp(s - jnp.max(s, axis=-1, keepdims=True)).astype(BF)
            ve = jnp.concatenate([v, jnp.ones((m, 128), BF)], axis=1)
            o = jnp.dot(e, ve, preferred_element_type=F32)
            num = jnp.where(low, o[:rows, :128], o[rows:, :128])
            den = jnp.where(low, o[:rows, 128:], o[rows:, 128:])
            att[r, head] = (num / den).astype(BF)

    att = xp

    def pair_inner(i):
        attend(i, True)

    loop(8, pair_inner)
    pump_y2()

    for cp in middle_sends:
        cp.wait()

    @pl.when(north)
    def _():
        for cp in south_sends:
            cp.wait_recv()
        for cp in north_sends:
            cp.wait_send()

    @pl.when(south)
    def _():
        for cp in north_sends:
            cp.wait_recv()
        for cp in south_sends:
            cp.wait_send()

    def project_halo(i):
        kvh[:, cols(i, 256)] = jnp.dot(
            halo[...], qkvv[:, cols(i, 256, D)], preferred_element_type=F32
        ).astype(BF)

    loop(8, project_halo)
    pump_x(1)
    pump_x(2)
    pump_x(4)
    pump_x(5)
    pump_z(0)

    def quarter_of(n):
        def pair(i):
            attend(i + 2 * n, False)

        return pair

    loop(2, quarter_of(0))
    pump_x(3)
    pump_r1()
    loop(2, quarter_of(1))
    pump_z(1)
    pump_z(4)
    loop(2, quarter_of(2))
    pump_z(2)
    pump_z(5)
    pump_r2()
    loop(2, quarter_of(3))
    pump_z(3)

    local[3].wait()
    attr = normed

    def unpermute(i):
        attr[:, cols(i, 256)] = jnp.dot(
            p1t[...], att[:, cols(i, 256)], preferred_element_type=F32
        ).astype(BF)

    loop(4, unpermute)
    local[4].wait()

    def out_project(i):
        mixed = jnp.dot(attr[...], outv[:, cols(i, 256)], preferred_element_type=F32)
        mid[:, cols(i, 256)] = (tok[:, cols(i, 256)].astype(F32) + mixed).astype(BF)

    loop(4, out_project)
    store_mid = pltpu.make_async_copy(mid, mid_out, lsem.at[9])
    store_mid.start()
    end_z(4)
    share(4, 0)
    end_z(5)
    share(5, 0)
    local[5].wait()

    def patch(i):
        g, t = i // 4, i % 4
        mgd[:, cols(i, 256)] = jnp.dot(
            pg[pl.ds(pl.multiple_of(g * GROUP, 16), GROUP), :], mid[:, cols(t, 256)],
            preferred_element_type=F32,
        ).astype(BF)

    loop(16, patch)

    def merge_norm(i):
        r = pl.ds(pl.multiple_of(i * 16, 16), 16)
        mgd[r, :] = norm_rows(mgd[r, :].astype(F32)).astype(BF)

    loop(GROUP // 16, merge_norm)
    mine = pl.ds(pl.multiple_of(c * GROUP, 16), GROUP)
    send("merged", mgd, xs.at[mine, :], sibling)
    keep_mgd = pltpu.make_async_copy(mgd, xs.at[mine, :], lsem.at[10])
    keep_mgd.start()

    local[6].wait()
    await_to("yr+3", near(1, z + 3, 0))
    await_to("yr-1", near(2, z + 1, 0))
    await_to("yrf1", near(3, z + 1, 0))
    await_to("yrf3", near(3, z + 3, 0))
    await_to("yrf2+", near(3, z + 2, 1))
    await_to("yrf2-", near(3, z + 2, 2))
    keep_mgd.wait()
    theirs_rows = pl.ds(pl.multiple_of((1 - c) * GROUP, 16), GROUP)
    await_to("merged", xs.at[theirs_rows, :])

    def merge_of(n):
        h = xh if n == 0 else 1 - xh

        def merge(i):
            v = jnp.zeros((2 * GROUP, 256), F32)
            for g in range(4):
                r = slice(g * D, (g + 1) * D)
                w = jnp.concatenate([wv[4 * i + h, r, :], wv[4 * i + 2 + h, r, :]], axis=1)
                v += jnp.dot(xs[:, r], w, preferred_element_type=F32)
            v = v.astype(BF)
            cc[0, n, :, cols(i, 256)] = v[:GROUP]
            cc[1, n, :, cols(i, 256)] = v[GROUP:]

        return merge

    def place_columns(n, core, get):
        h = xh if n == 0 else 1 - xh
        for j in range(4):
            at = pl.multiple_of((4 * j + 2 * h + core) * 128, 128)
            coarse[:, pl.ds(at, 128)] = get(slice(j * 128, (j + 1) * 128))

    loop(2, merge_of(0))
    send("swap0", cc.at[1 - c, 0], theirs.at[0], sibling)
    for k in range(4):
        end_z(k)
    loop(2, merge_of(1))
    send("swap1", cc.at[1 - c, 1], theirs.at[1], sibling)
    for n in (0, 1):
        place_columns(n, c, lambda t, n=n: cc[c, n, :, t])
    for n in (0, 1):
        await_to(f"swap{n}", theirs.at[n])
        place_columns(n, 1 - c, lambda t, n=n: theirs[n, :, t])

    def coarse_norm(i):
        r = pl.ds(pl.multiple_of(i * 16, 16), 16)
        cn[0, r, :] = norm_rows(coarse[r, :].astype(F32)).astype(BF)

    loop(GROUP // 16, coarse_norm)

    send("ag+", cn.at[0], cn.at[2], yp)
    send("ag-", cn.at[0], cn.at[3], ym)
    end_n(4)
    share(4, 1)
    end_n(5)
    share(5, 1)
    for n in (7, 8):
        local[n].wait()
    await_to("up", up4.at[1])
    await_to("down", down4.at[1])

    def ffn(first, count):
        rows = count * GROUP

        def up_step(i):
            q, t = i // 2, i % 2
            x = cn[first : first + count].reshape(rows, DC)
            h = jnp.dot(x, up4[q, :, cols(t, 256)], preferred_element_type=F32)
            hid[:rows, cols(i, 256)] = gelu(h).astype(BF)

        loop(8, up_step)

        def down_step(i):
            t = cols(i, 256)
            v = jnp.zeros((rows, 256), F32)
            for q in range(4):
                v += jnp.dot(hid[:rows, q * 512 : (q + 1) * 512], down4[q, :, t], preferred_element_type=F32)
            for n in range(count):
                part = v[n * GROUP : (n + 1) * GROUP]
                if first + n == 0:
                    acc[:, t] = part + coarse[:, t].astype(F32)
                else:
                    pt[first + n, :, t] = part.astype(BF)

        loop(8, down_step)

    await_to("ag+", cn.at[2])
    send("ag2+", cn.at[2, A_ROWS, :], cn.at[1, A_ROWS, :], yp)
    await_to("ag-", cn.at[3])
    send("ag2-", cn.at[3, B_ROWS, :], cn.at[1, B_ROWS, :], ym)
    for k, to in ((4, up4), (5, down4)):
        for i in range(2):
            await_to(f"s{k}{i}", to.at[3, half_rows(k, xl if i == 0 else 1 - xl), :])
    ffn(2, 2)
    send("rs2", pt.at[2], rb.at[3], ym)
    send("rs3", pt.at[3], rb.at[2], yp)
    await_to("ag2+", cn.at[1, A_ROWS, :])
    await_to("ag2-", cn.at[1, B_ROWS, :])
    ffn(0, 2)
    send("rs1", pt.at[1], rb.at[1], y2)
    await_to("rs2", rb.at[3])
    await_to("rs3", rb.at[2])

    def add_near(i):
        t = cols(i, 512)
        acc[:, t] += rb[2, :, t].astype(F32) + rb[3, :, t].astype(F32)

    loop(4, add_near)
    await_to("rs1", rb.at[1])

    def add_far(i):
        t = cols(i, 512)
        acc[:, t] += rb[1, :, t].astype(F32)

    loop(4, add_far)
    for r in range(9):
        out[r] = acc[12 * r : 12 * r + 12, :].astype(BF)
    for cp in sends.values():
        cp.wait_send()
    store_mid.wait()


VM = pl.BlockSpec(memory_space=pltpu.VMEM)
HBM = pl.BlockSpec(memory_space=pltpu.HBM)
DMA = pltpu.SemaphoreType.DMA


def per_device(tokens, qkv_weight, out_weight, merge_weight, up_weight, down_weight):
    order, packed, patch = _tables()
    p1 = jnp.asarray(order, BF)
    p1t = jnp.asarray(order.T, BF)
    pg = jnp.asarray(patch, BF)

    def vmem(*shape, kind=BF):
        return pltpu.VMEM(shape, kind)

    mid, coarse_out = pl.pallas_call(
        kernel,
        name="whole",
        out_shape=(
            jax.ShapeDtypeStruct((CELLS, D), BF),
            jax.ShapeDtypeStruct((ROWS // 2, COLS // 2, DC), BF),
        ),
        in_specs=[HBM, HBM, HBM, VM] + [HBM] * 7,
        out_specs=(HBM, VM),
        scratch_shapes=[
            vmem(CELLS, D),
            vmem(SENT, CELLS),
            vmem(OWN, CELLS),
            vmem(CELLS, OWN),
            vmem(4 * GROUP, CELLS),
            vmem(D, 3 * D),
            vmem(D, D),
            vmem(8, 4 * D, 128),
            vmem(4, DC, 512),
            vmem(4, 512, DC),
            vmem(CELLS, D),
            vmem(SENT, D),
            vmem(OWN, D),
            vmem(HALO, D),
            vmem(OWN, 3 * D),
            vmem(HALO, 2 * D),
            vmem(CELLS, D),
            vmem(GROUP, 4 * D),
            vmem(2 * GROUP, 4 * D),
            vmem(2, 2, GROUP, 512),
            vmem(2, GROUP, 512),
            vmem(GROUP, DC),
            vmem(4, GROUP, DC),
            vmem(2 * GROUP, DC),
            vmem(GROUP, DC, kind=F32),
            vmem(4, GROUP, DC),
            vmem(4, GROUP, DC),
            DMA((12,)),
            DMA((HALO_SENDS,)),
            DMA((HALO_SENDS,)),
            DMA((len(WSEMS),)),
            DMA((len(WSEMS),)),
        ],
        compiler_params=pltpu.CompilerParams(
            collective_id=0, has_side_effects=True, vmem_limit_bytes=62 * 2**20
        ),
    )(
        tokens.reshape(CELLS, D), jnp.asarray(packed, BF), p1, jnp.asarray(_bias()), qkv_weight, out_weight, merge_weight, p1t, pg,
        up_weight, down_weight,
    )
    return mid.reshape(ROWS, COLS, D), coarse_out


def solution(mesh):
    return jax.shard_map(
        per_device,
        mesh=mesh,
        in_specs=(P("lat", "lon", None), P(), P(), P(None, "lon"), P(None, "lon"), P("lon", None)),
        out_specs=(P("lat", "lon", None), P("lat", "lon", None)),
        check_vma=False,
    )
```

```python
import functools

import jax
import jax.numpy as jnp
import numpy as np
from jax import lax
from jax.experimental import pallas as pl
from jax.experimental.pallas import tpu as pltpu
from jax.sharding import PartitionSpec as P

MESH = pl.DeviceIdType.MESH
BF = jnp.bfloat16
F32 = jnp.float32
NEG = -1e30

ROWS, COLS, D, DC, HEADS = 18, 24, 1024, 2048, 16
CELLS = ROWS * COLS
GROUP = 112
HIGH = (3, 6, 6, 3)
WIDE = (6, 12, 6)
TOP = (0, 3, 9, 15)
LEFT = (0, 6, 18)


def _round(n):
    return -(-n // 16) * 16


PIECE = {}
_at = 0
for _b in range(3):
    for _a in range(4):
        PIECE[_a, _b] = (_at, _round(HIGH[_a] * WIDE[_b]), HIGH[_a] * WIDE[_b])
        _at += PIECE[_a, _b][1]
OWN = _at
SEND_W, SEND_E, SEND_N, SEND_S, SENT = 0, 112, 224, 304, 384
HALO_W, HALO_E, HALO_N, HALO_S = 0, 112, 224, 304
HALO_NW, HALO_NE, HALO_SW, HALO_SE = 384, 416, 448, 480
HALO = 512


def _tables():
    order = np.zeros((OWN, CELLS), np.float32)
    for (a, b), (at, _, _) in PIECE.items():
        k = 0
        for i in range(HIGH[a]):
            for j in range(WIDE[b]):
                order[at + k, (TOP[a] + i) * COLS + LEFT[b] + j] = 1
                k += 1
    packed = np.zeros((SENT, CELLS), np.float32)
    column = [(a, 0) for a in range(4)]
    for start, pieces in (
        (SEND_W, column),
        (SEND_E, [(a, 2) for a, _ in column]),
        (SEND_N, [(0, b) for b in range(3)]),
        (SEND_S, [(3, b) for b in range(3)]),
    ):
        k = start
        for a, b in pieces:
            n = PIECE[a, b][2]
            packed[k : k + n] = order[PIECE[a, b][0] : PIECE[a, b][0] + n]
            k += n
    patch = np.zeros((4 * GROUP, CELLS), np.float32)
    for g in range(4):
        for r in range(ROWS // 2):
            for c in range(COLS // 2):
                cell = (2 * r + g // 2) * COLS + 2 * c + g % 2
                patch[g * GROUP + r * (COLS // 2) + c, cell] = 1
    return order, packed, patch


def _span(base, start, count, side):
    low = start // 16 * 16
    return base + low, _round(start + count) - low, start - low, start - low + count, side


def _window_parts():
    out = []
    along, across = ((0, 18), (18, 36), (54, 36), (90, 18)), ((0, 18), (18, 36), (54, 18))
    for b in range(3):
        for a in range(4):
            side = "n" if a == 0 else "s" if a == 3 else ""
            parts = []
            if b != 1:
                parts.append(_span(HALO_W if b == 0 else HALO_E, *along[a], ""))
            if side:
                parts.append(_span(HALO_N if a == 0 else HALO_S, *across[b], side))
            corner = {(0, 0): HALO_NW, (0, 2): HALO_NE, (3, 0): HALO_SW, (3, 2): HALO_SE}
            if (a, b) in corner:
                first = 6 if b == 0 else 0
                parts.append((corner[a, b], 32, first, first + 18, side))
            out.append((PIECE[a, b], parts))
    return out


WINDOWS = _window_parts()


def _bias():
    bias = np.full((3, 16, 128), NEG, np.float32)
    for edge in range(3):
        for w, ((_, rows, valid), parts) in enumerate(WINDOWS):
            bias[edge, w, :valid] = 0
            at = rows
            for _, prows, first, last, side in parts:
                gone = (edge == 1 and side == "n") or (edge == 2 and side == "s")
                if not gone:
                    bias[edge, w, at + first : at + last] = 0
                at += prows
    return bias


def place():
    lat, lon = lax.axis_index("lat"), lax.axis_index("lon")
    z, xl = lat // 2, lat % 2
    y, xh, c = lon // 4, (lon // 2) % 2, lon % 2
    return lat, lon, z, xl, y, xh, c


def norm_rows(x):
    center = x - jnp.mean(x, axis=-1, keepdims=True)
    spread = jnp.mean(center * center, axis=-1, keepdims=True)
    return center * lax.rsqrt(spread + 1e-5)


def loop(n, body):
    def step(i, carry):
        body(i)
        return carry

    lax.fori_loop(0, n, step, 0)


def cols(i, size, base=0):
    return pl.ds(pl.multiple_of(base + i * size, 128), size)


HALO_SENDS = 8
ORDER = (
    ("x00", 3), ("ya+0", 3), ("ya-1", 3), ("ya+1", 7), ("ya-0", 7), ("z00a", 8), ("yb+", 11), ("yb-", 11),
    ("n00", 11), ("x01", 12), ("yq+", 14), ("yq-", 14), ("x10", 15), ("z00b", 16), ("n01", 17), ("z01a", 17),
    ("x11", 18), ("ye+", 20), ("ye-", 20), ("n10", 20), ("z10a", 20), ("x20", 21), ("z01b", 22), ("yt+", 23),
    ("yt-", 23), ("n11", 23), ("x21", 24), ("z10b", 25), ("z11a", 25), ("n20", 26), ("x30", 27), ("z11b", 28),
    ("z20a", 28), ("yu+", 29), ("yu-", 29), ("n21", 29), ("x31", 30), ("z20b", 31), ("z21a", 31), ("yef+", 32),
    ("yef-", 32), ("n30", 32), ("x40", 33), ("z21b", 34), ("z30a", 34), ("yqf+", 35), ("yqf-", 35), ("n31", 35),
    ("x41", 36), ("z30b", 37), ("z31a", 37), ("n40", 38), ("x50", 39), ("z31b", 40), ("z40a", 40), ("n41", 41),
    ("x51", 42), ("z40b", 43), ("z41a", 43), ("n50", 44), ("x60", 46), ("z41b", 46), ("z50a", 46), ("n51", 48),
    ("x61", 49), ("z50b", 50), ("z51a", 50), ("n60", 51), ("x70", 52), ("z51b", 53), ("z60a", 53), ("n61", 54),
    ("x71", 55), ("z60b", 56), ("z61a", 56), ("n70", 57), ("z61b", 59), ("z70a", 59), ("n71", 60), ("z70b", 62),
    ("z71a", 62), ("z71b", 65),
)
WSEMS = {}
for _n in (
    [n for n, _ in ORDER]
    + [f"s{k}" for k in (4, 5, 6, 7)]
    + ["up", "down", "merged", "swap0", "swap1"]
    + ["ag+", "ag-", "ag2+", "ag2-", "rs1", "rs2", "rs3"]
):
    WSEMS[_n] = len(WSEMS)


def needs(name):
    if name[0] in "nz":
        return [("n" if name[-1] == "b" else "x") + name[1:3]]
    if name[0] == "x":
        k, i = int(name[1]), name[2]
        return {1: [f"ya+{i}"], 2: [f"ya-{i}"], 3: ["yb+" if i == "0" else "yb-"]}.get(k, [])
    first = {"yb+": "ya+0", "yb-": "ya-1", "yqf+": "yq+", "yqf-": "yq-", "yef+": "ye+", "yef-": "ye-"}
    return [first[name]] if name in first else []


A_ROWS, B_ROWS = pl.ds(0, 64), pl.ds(64, 48)


def gelu(x):
    return 0.5 * x * (1.0 + lax.erf(x * np.float32(0.5**0.5)))


def kernel(
    tok_in, ps_in, p1_in, bias, qkvw, outw, mw, p1t_in, pg_in, up, down,
    mid_out, out,
    tok, ps, p1, p1t, pg, qkvv, outv, wv, up4, down4,
    normed, packed, xp, halo, qkv, kvh, mid, mgd,
    xs, cc, theirs, coarse, cn, hid, acc, pt, rb,
    lsem, hs, hr, ws, wr,
):
    lat, lon, z, xl, y, xh, c = place()
    north, south = lat > 0, lat < 7
    west, east = (lon + 15) % 16, (lon + 1) % 16
    yp = (lat, (lon + 4) % 16)
    ym = (lat, (lon + 12) % 16)
    y2 = (lat, (lon + 8) % 16)
    zp = ((lat + 2) % 8, lon)
    zm = ((lat + 6) % 8, lon)
    xpart = (2 * z + 1 - xl, 4 * y + 2 * (1 - xh) + c)
    xn = (lat + 1 - 2 * xl, lon)
    sibling = (lat, lon + 1 - 2 * c)

    barrier = pltpu.get_barrier_semaphore()

    def greet(dev):
        pl.semaphore_signal(barrier, inc=1, device_id=dev, device_id_type=MESH)

    partners = ((lat, west), (lat, east), yp, ym, y2, zp, zm, xpart, xn, sibling)
    for dev in partners:
        greet(dev)

    @pl.when(north)
    def _():
        for o in (west, lon, east):
            greet((lat - 1, o))

    @pl.when(south)
    def _():
        for o in (west, lon, east):
            greet((lat + 1, o))

    own = 2 * y + xh
    local = [
        pltpu.make_async_copy(tok_in, tok, lsem.at[0]),
        pltpu.make_async_copy(p1_in, p1, lsem.at[1]),
        pltpu.make_async_copy(qkvw, qkvv, lsem.at[2]),
        pltpu.make_async_copy(p1t_in, p1t, lsem.at[3]),
        pltpu.make_async_copy(outw, outv, lsem.at[4]),
        pltpu.make_async_copy(pg_in, pg, lsem.at[5]),
        pltpu.make_async_copy(mw, wv.at[own], lsem.at[6]),
        pltpu.make_async_copy(up, up4.at[0], lsem.at[7]),
        pltpu.make_async_copy(down, down4.at[0], lsem.at[8]),
    ]
    early = pltpu.make_async_copy(ps_in, ps, lsem.at[11])
    local[0].start()
    early.start()
    local[1].start()
    local[2].start()

    count = len(partners) + jnp.where(north, 3, 0) + jnp.where(south, 3, 0)
    pl.semaphore_wait(barrier, count)

    def block(k, other):
        yy = (y + (0, 3, 1, 2)[k]) % 4
        return 2 * yy + (1 - xh if other else xh)

    def rows_of(size, quarter, half, base=0):
        at = base + (quarter % 4) * 2 * size
        if half is None:
            return pl.ds(pl.multiple_of(at, size), 2 * size)
        return pl.ds(pl.multiple_of(at + half * size, size), size)

    sends = {}

    def remote(name, src, dst, dev):
        i = WSEMS[name]
        return pltpu.make_async_remote_copy(
            src_ref=src, dst_ref=dst, send_sem=ws.at[i], recv_sem=wr.at[i],
            device_id=dev, device_id_type=MESH,
        )

    def send(name, src, dst, dev):
        sends[name] = remote(name, src, dst, dev)
        sends[name].start()

    def await_to(name, dst):
        remote(name, dst, dst, yp).wait_recv()

    def near(k, quarter, half):
        return wv.at[block(k, False), rows_of(512, quarter, half), :]

    def far_rows(k, quarter, half):
        if k < 6:
            return rows_of(128, quarter, half, (k - 4) * 1024)
        return rows_of(32, quarter, half, (k - 6) * 256)

    def far(k, quarter, half):
        if k < 4:
            return wv.at[block(k, True), rows_of(512, quarter, half), :]
        return (up4 if k < 6 else down4).at[2, far_rows(k, quarter, half), :]

    ox = 1 - xl

    def region(name):
        kind, sign = name[:-2] if name[1] == "a" else name[:-1], name[2] if name[1] == "a" else name[-1]
        plus = sign == "+"
        if kind == "ya":
            return z + int(name[3]), ox
        if kind == "yb":
            return (z, ox) if plus else (z + 1, ox)
        if kind in ("yq", "yqf"):
            return (z + 2, None) if plus else (z + 3, None)
        if kind == "yt":
            return (z + 3, None) if plus else (z + 2, None)
        if kind in ("ye", "yef"):
            return (z, xl) if plus else (z + 1, xl)
        return (z + 1, xl) if plus else (z, xl)

    def landing(name):
        if name[0] == "y":
            second = name[:2] == "yb" or name[:3] in ("yqf", "yef")
            k = 3 if second else 1 if "+" in name else 2
            return near(k, *region(name))
        k, i = int(name[1]), int(name[2])
        if name[0] == "x":
            return far(k, z + i, xl)
        if name[0] == "n":
            return far(k, z + i, ox)
        return far(k, z + 3 if i == 0 else z + 2, xl if name[3] == "a" else ox)

    def start(name):
        if name[0] == "y":
            plus = "+" in name
            dev = yp if plus else ym
            if name[:2] == "yb" or name[:3] in ("yqf", "yef"):
                ref = near(1 if plus else 2, *region(name))
                send(name, ref, ref, dev)
            else:
                quarter, half = region(name)
                send(name, mw.at[rows_of(512, quarter, half), :], near(0, quarter, half), dev)
            return
        k, i = int(name[1]), int(name[2])
        if name[0] == "x":
            if k == 0:
                send(name, mw.at[rows_of(512, z + i, ox), :], near(0, z + i, ox), xpart)
            elif k < 4:
                send(name, near(k, z + i, ox), near(k, z + i, ox), xpart)
            else:
                send(name, (up if k < 6 else down).at[far_rows(k, z + i, ox), :], far(k, z + i, ox), xpart)
        elif name[0] == "n":
            send(name, far(k, z + i, xl), far(k, z + i, xl), xn)
        else:
            ref = far(k, z + i, xl if name[3] == "a" else ox)
            send(name, ref, ref, zp if i == 0 else zm)

    landed = set()
    queue = list(ORDER)

    def need(name):
        if name not in landed:
            landed.add(name)
            await_to(name, landing(name))

    def pump(time):
        while queue and queue[0][1] <= time:
            name = queue.pop(0)[0]
            for other in needs(name):
                need(other)
            start(name)

    def need_far(k):
        for n, _ in ORDER:
            if n[0] in "xnz" and n[1] == str(k):
                need(n)

    def share(k):
        size = 1024 if k < 6 else 256
        rows = pl.ds((k % 2) * size, size)
        to = up4 if k < 6 else down4
        send(f"s{k}", to.at[2, rows, :], to.at[3, rows, :], sibling)

    pump(3)

    local[0].wait()

    def norm_block(i):
        r = pl.ds(pl.multiple_of(i * 48, 16), 48)
        normed[r, :] = norm_rows(tok[r, :].astype(F32)).astype(BF)

    loop(9, norm_block)
    for n in (6, 3, 4, 5):
        local[n].start()
    early.wait()

    def pack(i):
        packed[:, cols(i, 256)] = jnp.dot(
            ps[...], normed[:, cols(i, 256)], preferred_element_type=F32
        ).astype(BF)

    loop(4, pack)

    def hcopy(i, src_at, dst_at, rows, dev):
        return pltpu.make_async_remote_copy(
            src_ref=packed.at[pl.ds(src_at, rows), :], dst_ref=halo.at[pl.ds(dst_at, rows), :],
            send_sem=hs.at[i], recv_sem=hr.at[i], device_id=dev, device_id_type=MESH,
        )

    middle_sends = [
        hcopy(0, SEND_W, HALO_E, 112, (lat, west)),
        hcopy(1, SEND_E, HALO_W, 112, (lat, east)),
    ]
    north_sends = [
        hcopy(2, SEND_N, HALO_S, 80, (lat - 1, lon)),
        hcopy(3, SEND_N, HALO_SE, 32, (lat - 1, west)),
        hcopy(4, SEND_N + 48, HALO_SW, 32, (lat - 1, east)),
    ]
    south_sends = [
        hcopy(5, SEND_S, HALO_N, 80, (lat + 1, lon)),
        hcopy(6, SEND_S, HALO_NE, 32, (lat + 1, west)),
        hcopy(7, SEND_S + 48, HALO_NW, 32, (lat + 1, east)),
    ]
    for cp in middle_sends:
        cp.start()

    @pl.when(north)
    def _():
        for cp in north_sends:
            cp.start()

    @pl.when(south)
    def _():
        for cp in south_sends:
            cp.start()

    local[1].wait()

    def permute(i):
        xp[:, cols(i, 256)] = jnp.dot(
            p1[...], normed[:, cols(i, 256)], preferred_element_type=F32
        ).astype(BF)

    loop(4, permute)

    @pl.when(jnp.logical_not(north))
    def _():
        halo[HALO_N : HALO_N + 80, :] = jnp.zeros((80, D), BF)
        halo[HALO_NW : HALO_NW + 64, :] = jnp.zeros((64, D), BF)

    @pl.when(jnp.logical_not(south))
    def _():
        halo[HALO_S : HALO_S + 80, :] = jnp.zeros((80, D), BF)
        halo[HALO_SW : HALO_SW + 64, :] = jnp.zeros((64, D), BF)

    local[2].wait()

    def project(i):
        qkv[:, cols(i, 256)] = jnp.dot(
            xp[...], qkvv[:, cols(i, 256)], preferred_element_type=F32
        ).astype(BF)

    def project_mid(i):
        project(i + 4)

    def project_late(i):
        project(i + 8)

    pump(8)
    loop(4, project)
    pump(11)
    local[7].start()
    local[8].start()
    loop(4, project_mid)
    pump(13)
    loop(4, project_late)
    pump(14)
    send("up", up, up4.at[1], sibling)
    send("down", down, down4.at[1], sibling)

    edge = jnp.where(north, jnp.where(south, 0, 2), 1)
    low = lax.broadcasted_iota(jnp.int32, (1, 128), 1) < 64

    def attend(i, inner):
        head = cols(i, 128)
        head_k, head_v = cols(i, 128, D), cols(i, 128, 2 * D)
        for w, ((start, rows, _), parts) in enumerate(WINDOWS):
            if inner == bool(parts):
                continue
            r = slice(start, start + rows)
            q = qkv[r, head] * jnp.asarray(0.125, BF)
            zero = jnp.zeros_like(q)
            q = jnp.concatenate([jnp.where(low, q, zero), jnp.where(low, zero, q)], axis=0)
            ks, vs = [qkv[r, head_k]], [qkv[r, head_v]]
            for off, prows, _, _, _ in parts:
                ks.append(kvh[off : off + prows, head])
                vs.append(kvh[off : off + prows, head_k])
            k = jnp.concatenate(ks, axis=0) if parts else ks[0]
            v = jnp.concatenate(vs, axis=0) if parts else vs[0]
            m = k.shape[0]
            s = lax.dot_general(q, k, (((1,), (1,)), ((), ())), preferred_element_type=F32)
            s = s + bias[edge, w : w + 1, :m]
            e = jnp.exp(s - jnp.max(s, axis=-1, keepdims=True)).astype(BF)
            ve = jnp.concatenate([v, jnp.ones((m, 128), BF)], axis=1)
            o = jnp.dot(e, ve, preferred_element_type=F32)
            num = jnp.where(low, o[:rows, :128], o[rows:, :128])
            den = jnp.where(low, o[:rows, 128:], o[rows:, 128:])
            att[r, head] = (num / den).astype(BF)

    att = xp

    def pair_inner(i):
        attend(i, True)

    loop(8, pair_inner)
    pump(16)

    for cp in middle_sends:
        cp.wait()

    @pl.when(north)
    def _():
        for cp in south_sends:
            cp.wait_recv()
        for cp in north_sends:
            cp.wait_send()

    @pl.when(south)
    def _():
        for cp in north_sends:
            cp.wait_recv()
        for cp in south_sends:
            cp.wait_send()

    def project_halo(i):
        kvh[:, cols(i, 256)] = jnp.dot(
            halo[...], qkvv[:, cols(i, 256, D)], preferred_element_type=F32
        ).astype(BF)

    loop(8, project_halo)
    pump(20)

    def quarter_of(n):
        def pair(i):
            attend(i + 2 * n, False)

        return pair

    loop(2, quarter_of(0))
    pump(23)
    loop(2, quarter_of(1))
    pump(25)
    loop(2, quarter_of(2))
    pump(28)
    loop(2, quarter_of(3))
    pump(30)

    local[3].wait()
    attr = normed

    def unpermute(i):
        attr[:, cols(i, 256)] = jnp.dot(
            p1t[...], att[:, cols(i, 256)], preferred_element_type=F32
        ).astype(BF)

    loop(4, unpermute)
    local[4].wait()

    def out_project(i):
        mixed = jnp.dot(attr[...], outv[:, cols(i, 256)], preferred_element_type=F32)
        mid[:, cols(i, 256)] = (tok[:, cols(i, 256)].astype(F32) + mixed).astype(BF)

    loop(4, out_project)
    store_mid = pltpu.make_async_copy(mid, mid_out, lsem.at[9])
    store_mid.start()
    pump(33)
    local[5].wait()

    def patch(i):
        g, t = i // 4, i % 4
        mgd[:, cols(i, 256)] = jnp.dot(
            pg[pl.ds(pl.multiple_of(g * GROUP, 16), GROUP), :], mid[:, cols(t, 256)],
            preferred_element_type=F32,
        ).astype(BF)

    loop(16, patch)

    def merge_norm(i):
        r = pl.ds(pl.multiple_of(i * 16, 16), 16)
        mgd[r, :] = norm_rows(mgd[r, :].astype(F32)).astype(BF)

    loop(GROUP // 16, merge_norm)
    mine = pl.ds(pl.multiple_of(c * GROUP, 16), GROUP)
    send("merged", mgd, xs.at[mine, :], sibling)
    keep_mgd = pltpu.make_async_copy(mgd, xs.at[mine, :], lsem.at[10])
    keep_mgd.start()

    pump(38)
    local[6].wait()
    pump(40)
    for n, _ in ORDER:
        if n[0] == "y":
            need(n)
    pump(42)
    keep_mgd.wait()
    theirs_rows = pl.ds(pl.multiple_of((1 - c) * GROUP, 16), GROUP)
    await_to("merged", xs.at[theirs_rows, :])

    def merge_of(n):
        h = xh if n == 0 else 1 - xh

        def merge(i):
            v = jnp.zeros((2 * GROUP, 256), F32)
            for g in range(4):
                r = slice(g * D, (g + 1) * D)
                w = jnp.concatenate([wv[4 * i + h, r, :], wv[4 * i + 2 + h, r, :]], axis=1)
                v += jnp.dot(xs[:, r], w, preferred_element_type=F32)
            v = v.astype(BF)
            cc[0, n, :, cols(i, 256)] = v[:GROUP]
            cc[1, n, :, cols(i, 256)] = v[GROUP:]

        return merge

    def place_columns(n, core, get):
        h = xh if n == 0 else 1 - xh
        for j in range(4):
            at = pl.multiple_of((4 * j + 2 * h + core) * 128, 128)
            coarse[:, pl.ds(at, 128)] = get(slice(j * 128, (j + 1) * 128))

    loop(2, merge_of(0))
    send("swap0", cc.at[1 - c, 0], theirs.at[0], sibling)
    pump(45)
    for k in range(4):
        need_far(k)
    loop(2, merge_of(1))
    send("swap1", cc.at[1 - c, 1], theirs.at[1], sibling)
    pump(48)
    for n in (0, 1):
        place_columns(n, c, lambda t, n=n: cc[c, n, :, t])
    for n in (0, 1):
        await_to(f"swap{n}", theirs.at[n])
        place_columns(n, 1 - c, lambda t, n=n: theirs[n, :, t])

    def coarse_norm(i):
        r = pl.ds(pl.multiple_of(i * 16, 16), 16)
        cn[0, r, :] = norm_rows(coarse[r, :].astype(F32)).astype(BF)

    loop(GROUP // 16, coarse_norm)

    send("ag+", cn.at[0], cn.at[2], yp)
    send("ag-", cn.at[0], cn.at[3], ym)
    pump(57)
    need_far(4)
    share(4)
    for n in (7, 8):
        local[n].wait()
    await_to("up", up4.at[1])
    await_to("down", down4.at[1])

    def ffn(first, count):
        rows = count * GROUP

        def up_step(i):
            q, t = i // 2, i % 2
            x = cn[first : first + count].reshape(rows, DC)
            h = jnp.dot(x, up4[q, :, cols(t, 256)], preferred_element_type=F32)
            hid[:rows, cols(i, 256)] = gelu(h).astype(BF)

        loop(8, up_step)

        def down_step(i):
            t = cols(i, 256)
            v = jnp.zeros((rows, 256), F32)
            for q in range(4):
                v += jnp.dot(hid[:rows, q * 512 : (q + 1) * 512], down4[q, :, t], preferred_element_type=F32)
            for n in range(count):
                part = v[n * GROUP : (n + 1) * GROUP]
                if first + n == 0:
                    acc[:, t] = part + coarse[:, t].astype(F32)
                else:
                    pt[first + n, :, t] = part.astype(BF)

        loop(8, down_step)

    await_to("ag+", cn.at[2])
    send("ag2+", cn.at[2, A_ROWS, :], cn.at[1, A_ROWS, :], yp)
    await_to("ag-", cn.at[3])
    send("ag2-", cn.at[3, B_ROWS, :], cn.at[1, B_ROWS, :], ym)
    pump(99)
    for k in (5, 6, 7):
        need_far(k)
        share(k)
    for k in (4, 5, 6, 7):
        size = 1024 if k < 6 else 256
        await_to(f"s{k}", (up4 if k < 6 else down4).at[3, pl.ds((k % 2) * size, size), :])
    ffn(2, 2)
    send("rs2", pt.at[2], rb.at[3], ym)
    send("rs3", pt.at[3], rb.at[2], yp)
    await_to("ag2+", cn.at[1, A_ROWS, :])
    await_to("ag2-", cn.at[1, B_ROWS, :])
    ffn(0, 2)
    send("rs1", pt.at[1], rb.at[1], y2)
    await_to("rs2", rb.at[3])
    await_to("rs3", rb.at[2])

    def add_near(i):
        t = cols(i, 512)
        acc[:, t] += rb[2, :, t].astype(F32) + rb[3, :, t].astype(F32)

    loop(4, add_near)
    await_to("rs1", rb.at[1])

    def add_far(i):
        t = cols(i, 512)
        acc[:, t] += rb[1, :, t].astype(F32)

    loop(4, add_far)
    for r in range(9):
        out[r] = acc[12 * r : 12 * r + 12, :].astype(BF)
    for cp in sends.values():
        cp.wait_send()
    store_mid.wait()


VM = pl.BlockSpec(memory_space=pltpu.VMEM)
HBM = pl.BlockSpec(memory_space=pltpu.HBM)
DMA = pltpu.SemaphoreType.DMA


def per_device(tokens, qkv_weight, out_weight, merge_weight, up_weight, down_weight):
    order, packed, patch = _tables()
    p1 = jnp.asarray(order, BF)
    p1t = jnp.asarray(order.T, BF)
    pg = jnp.asarray(patch, BF)

    def vmem(*shape, kind=BF):
        return pltpu.VMEM(shape, kind)

    mid, coarse_out = pl.pallas_call(
        kernel,
        name="whole",
        out_shape=(
            jax.ShapeDtypeStruct((CELLS, D), BF),
            jax.ShapeDtypeStruct((ROWS // 2, COLS // 2, DC), BF),
        ),
        in_specs=[HBM, HBM, HBM, VM] + [HBM] * 7,
        out_specs=(HBM, VM),
        scratch_shapes=[
            vmem(CELLS, D),
            vmem(SENT, CELLS),
            vmem(OWN, CELLS),
            vmem(CELLS, OWN),
            vmem(4 * GROUP, CELLS),
            vmem(D, 3 * D),
            vmem(D, D),
            vmem(8, 4 * D, 128),
            vmem(4, DC, 512),
            vmem(4, 512, DC),
            vmem(CELLS, D),
            vmem(SENT, D),
            vmem(OWN, D),
            vmem(HALO, D),
            vmem(OWN, 3 * D),
            vmem(HALO, 2 * D),
            vmem(CELLS, D),
            vmem(GROUP, 4 * D),
            vmem(2 * GROUP, 4 * D),
            vmem(2, 2, GROUP, 512),
            vmem(2, GROUP, 512),
            vmem(GROUP, DC),
            vmem(4, GROUP, DC),
            vmem(2 * GROUP, DC),
            vmem(GROUP, DC, kind=F32),
            vmem(4, GROUP, DC),
            vmem(4, GROUP, DC),
            DMA((12,)),
            DMA((HALO_SENDS,)),
            DMA((HALO_SENDS,)),
            DMA((len(WSEMS),)),
            DMA((len(WSEMS),)),
        ],
        compiler_params=pltpu.CompilerParams(
            collective_id=0, has_side_effects=True, vmem_limit_bytes=62 * 2**20
        ),
    )(
        tokens.reshape(CELLS, D), jnp.asarray(packed, BF), p1, jnp.asarray(_bias()), qkv_weight, out_weight, merge_weight, p1t, pg,
        up_weight, down_weight,
    )
    return mid.reshape(ROWS, COLS, D), coarse_out


def solution(mesh):
    return jax.shard_map(
        per_device,
        mesh=mesh,
        in_specs=(P("lat", "lon", None), P(), P(), P(None, "lon"), P(None, "lon"), P("lon", None)),
        out_specs=(P("lat", "lon", None), P("lat", "lon", None)),
        check_vma=False,
    )
```

```python
import functools

import jax
import jax.numpy as jnp
import numpy as np
from jax import lax
from jax.experimental import pallas as pl
from jax.experimental.pallas import tpu as pltpu
from jax.sharding import PartitionSpec as P

MESH = pl.DeviceIdType.MESH
BF = jnp.bfloat16
F32 = jnp.float32
NEG = -1e30

ROWS, COLS, D, DC, HEADS = 18, 24, 1024, 2048, 16
CELLS = ROWS * COLS
GROUP = 112
HIGH = (3, 6, 6, 3)
WIDE = (6, 12, 6)
TOP = (0, 3, 9, 15)
LEFT = (0, 6, 18)


def _round(n):
    return -(-n // 16) * 16


PIECE = {}
_at = 0
for _b in range(3):
    for _a in range(4):
        PIECE[_a, _b] = (_at, _round(HIGH[_a] * WIDE[_b]), HIGH[_a] * WIDE[_b])
        _at += PIECE[_a, _b][1]
OWN = _at
SEND_W, SEND_E, SEND_N, SEND_S, SENT = 0, 112, 224, 304, 384
HALO_W, HALO_E, HALO_N, HALO_S = 0, 112, 224, 304
HALO_NW, HALO_NE, HALO_SW, HALO_SE = 384, 416, 448, 480
HALO = 512


def _tables():
    order = np.zeros((OWN, CELLS), np.float32)
    for (a, b), (at, _, _) in PIECE.items():
        k = 0
        for i in range(HIGH[a]):
            for j in range(WIDE[b]):
                order[at + k, (TOP[a] + i) * COLS + LEFT[b] + j] = 1
                k += 1
    packed = np.zeros((SENT, CELLS), np.float32)
    column = [(a, 0) for a in range(4)]
    for start, pieces in (
        (SEND_W, column),
        (SEND_E, [(a, 2) for a, _ in column]),
        (SEND_N, [(0, b) for b in range(3)]),
        (SEND_S, [(3, b) for b in range(3)]),
    ):
        k = start
        for a, b in pieces:
            n = PIECE[a, b][2]
            packed[k : k + n] = order[PIECE[a, b][0] : PIECE[a, b][0] + n]
            k += n
    patch = np.zeros((4 * GROUP, CELLS), np.float32)
    for g in range(4):
        for r in range(ROWS // 2):
            for c in range(COLS // 2):
                cell = (2 * r + g // 2) * COLS + 2 * c + g % 2
                patch[g * GROUP + r * (COLS // 2) + c, cell] = 1
    return order, packed, patch


def _span(base, start, count, side):
    low = start // 16 * 16
    return base + low, _round(start + count) - low, start - low, start - low + count, side


def _window_parts():
    out = []
    along, across = ((0, 18), (18, 36), (54, 36), (90, 18)), ((0, 18), (18, 36), (54, 18))
    for b in range(3):
        for a in range(4):
            side = "n" if a == 0 else "s" if a == 3 else ""
            parts = []
            if b != 1:
                parts.append(_span(HALO_W if b == 0 else HALO_E, *along[a], ""))
            if side:
                parts.append(_span(HALO_N if a == 0 else HALO_S, *across[b], side))
            corner = {(0, 0): HALO_NW, (0, 2): HALO_NE, (3, 0): HALO_SW, (3, 2): HALO_SE}
            if (a, b) in corner:
                first = 6 if b == 0 else 0
                parts.append((corner[a, b], 32, first, first + 18, side))
            out.append((PIECE[a, b], parts))
    return out


WINDOWS = _window_parts()


def _bias():
    bias = np.full((3, 16, 128), NEG, np.float32)
    for edge in range(3):
        for w, ((_, rows, valid), parts) in enumerate(WINDOWS):
            bias[edge, w, :valid] = 0
            at = rows
            for _, prows, first, last, side in parts:
                gone = (edge == 1 and side == "n") or (edge == 2 and side == "s")
                if not gone:
                    bias[edge, w, at + first : at + last] = 0
                at += prows
    return bias


def place():
    lat, lon = lax.axis_index("lat"), lax.axis_index("lon")
    z, xl = lat // 2, lat % 2
    y, xh, c = lon // 4, (lon // 2) % 2, lon % 2
    return lat, lon, z, xl, y, xh, c


def norm_rows(x):
    center = x - jnp.mean(x, axis=-1, keepdims=True)
    spread = jnp.mean(center * center, axis=-1, keepdims=True)
    return center * lax.rsqrt(spread + 1e-5)


def loop(n, body):
    def step(i, carry):
        body(i)
        return carry

    lax.fori_loop(0, n, step, 0)


def cols(i, size, base=0):
    return pl.ds(pl.multiple_of(base + i * size, 128), size)


HALO_SENDS = 8
ORDER = (
    ("x00", 3), ("ya+0", 3), ("ya-1", 3), ("ya+1", 7), ("ya-0", 7), ("z00a", 8), ("yb+", 11), ("yb-", 11),
    ("n00", 11), ("x01", 12), ("yq+", 14), ("yq-", 14), ("x10", 15), ("z00b", 16), ("n01", 17), ("z01a", 17),
    ("x11", 18), ("ye+", 20), ("ye-", 20), ("n10", 20), ("z10a", 20), ("x20", 21), ("z01b", 22), ("yt+", 23),
    ("yt-", 23), ("n11", 23), ("x21", 24), ("z10b", 25), ("z11a", 25), ("n20", 26), ("x30", 27), ("z11b", 28),
    ("z20a", 28), ("yu+", 29), ("yu-", 29), ("n21", 29), ("x31", 30), ("z20b", 31), ("z21a", 31), ("yef+", 32),
    ("yef-", 32), ("n30", 32), ("x40", 33), ("z21b", 34), ("z30a", 34), ("yqf+", 35), ("yqf-", 35), ("n31", 35),
    ("x41", 36), ("z30b", 37), ("z31a", 37), ("n40", 38), ("x50", 39), ("z31b", 40), ("z40a", 40), ("n41", 41),
    ("x51", 42), ("z40b", 43), ("z41a", 43), ("n50", 44), ("x60", 46), ("z41b", 46), ("z50a", 46), ("n51", 48),
    ("x61", 49), ("z50b", 50), ("z51a", 50), ("n60", 51), ("x70", 52), ("z51b", 53), ("z60a", 53), ("n61", 54),
    ("x71", 55), ("z60b", 56), ("z61a", 56), ("n70", 57), ("z61b", 59), ("z70a", 59), ("n71", 60), ("z70b", 62),
    ("z71a", 62), ("z71b", 65),
)
WSEMS = {}
for _n in (
    [n for n, _ in ORDER]
    + [f"s{k}" for k in (4, 5, 6, 7)]
    + ["up", "down", "merged", "swap0", "swap1"]
    + ["ag+", "ag-", "ag2+", "ag2-", "rs1", "rs2", "rs3"]
):
    WSEMS[_n] = len(WSEMS)


def needs(name):
    if name[0] in "nz":
        return [("n" if name[-1] == "b" else "x") + name[1:3]]
    if name[0] == "x":
        k, i = int(name[1]), name[2]
        return {1: [f"ya+{i}"], 2: [f"ya-{i}"], 3: ["yb+" if i == "0" else "yb-"]}.get(k, [])
    first = {"yb+": "ya+0", "yb-": "ya-1", "yqf+": "yq+", "yqf-": "yq-", "yef+": "ye+", "yef-": "ye-"}
    return [first[name]] if name in first else []


A_ROWS, B_ROWS = pl.ds(0, 64), pl.ds(64, 48)


def gelu(x):
    return 0.5 * x * (1.0 + lax.erf(x * np.float32(0.5**0.5)))


def kernel(
    tok_in, ps_in, p1_in, bias, qkvw, outw, mw, p1t_in, pg_in, up, down,
    mid_out, out,
    tok, ps, p1, p1t, pg, qkvv, outv, wv, up4, down4,
    normed, packed, xp, halo, qkv, kvh, mid, mgd,
    xs, cc, theirs, coarse, cn, hid, acc, pt, rb,
    lsem, hs, hr, ws, wr,
):
    lat, lon, z, xl, y, xh, c = place()
    north, south = lat > 0, lat < 7
    west, east = (lon + 15) % 16, (lon + 1) % 16
    yp = (lat, (lon + 4) % 16)
    ym = (lat, (lon + 12) % 16)
    y2 = (lat, (lon + 8) % 16)
    zp = ((lat + 2) % 8, lon)
    zm = ((lat + 6) % 8, lon)
    xpart = (2 * z + 1 - xl, 4 * y + 2 * (1 - xh) + c)
    xn = (lat + 1 - 2 * xl, lon)
    sibling = (lat, lon + 1 - 2 * c)

    barrier = pltpu.get_barrier_semaphore()

    def greet(dev):
        pl.semaphore_signal(barrier, inc=1, device_id=dev, device_id_type=MESH)

    partners = ((lat, west), (lat, east), yp, ym, y2, zp, zm, xpart, xn, sibling)
    for dev in partners:
        greet(dev)

    @pl.when(north)
    def _():
        for o in (west, lon, east):
            greet((lat - 1, o))

    @pl.when(south)
    def _():
        for o in (west, lon, east):
            greet((lat + 1, o))

    own = 2 * y + xh
    local = [
        pltpu.make_async_copy(tok_in, tok, lsem.at[0]),
        pltpu.make_async_copy(p1_in, p1, lsem.at[1]),
        pltpu.make_async_copy(qkvw, qkvv, lsem.at[2]),
        pltpu.make_async_copy(p1t_in, p1t, lsem.at[3]),
        pltpu.make_async_copy(outw, outv, lsem.at[4]),
        pltpu.make_async_copy(pg_in, pg, lsem.at[5]),
        pltpu.make_async_copy(mw, wv.at[own], lsem.at[6]),
        pltpu.make_async_copy(up, up4.at[0], lsem.at[7]),
        pltpu.make_async_copy(down, down4.at[0], lsem.at[8]),
    ]
    early = pltpu.make_async_copy(ps_in, ps, lsem.at[11])
    local[0].start()
    early.start()
    local[1].start()
    local[2].start()

    count = len(partners) + jnp.where(north, 3, 0) + jnp.where(south, 3, 0)
    pl.semaphore_wait(barrier, count)

    shift = [2 * ((y + d) % 4) for d in (0, 3, 1, 2)]
    slots = {False: [v + xh for v in shift], True: [v + 1 - xh for v in shift]}
    zq = [(z + d) % 4 for d in range(4)]

    def block(k, other):
        return slots[other][k]

    def rows_of(size, quarter, half, base=0):
        at = base + quarter * 2 * size
        if half is None:
            return pl.ds(pl.multiple_of(at, size), 2 * size)
        return pl.ds(pl.multiple_of(at + half * size, size), size)

    sends = {}

    def remote(name, src, dst, dev):
        i = WSEMS[name]
        return pltpu.make_async_remote_copy(
            src_ref=src, dst_ref=dst, send_sem=ws.at[i], recv_sem=wr.at[i],
            device_id=dev, device_id_type=MESH,
        )

    def send(name, src, dst, dev, like=None):
        remote(name, src, dst, dev).start()
        if like is None:
            rows, width = dst.shape
            buffer = {128: wv, 512: up4, DC: down4}[width]

            def like():
                return buffer.at[0, pl.ds(0, rows), :]

        sends[name] = like

    def await_to(name, dst):
        remote(name, dst, dst, yp).wait_recv()

    def near(k, quarter, half):
        return wv.at[block(k, False), rows_of(512, quarter, half), :]

    def far_rows(k, quarter, half):
        if k < 6:
            return rows_of(128, quarter, half, (k - 4) * 1024)
        return rows_of(32, quarter, half, (k - 6) * 256)

    def far(k, quarter, half):
        if k < 4:
            return wv.at[block(k, True), rows_of(512, quarter, half), :]
        return (up4 if k < 6 else down4).at[2, far_rows(k, quarter, half), :]

    ox = 1 - xl

    def region(name):
        kind, sign = name[:-2] if name[1] == "a" else name[:-1], name[2] if name[1] == "a" else name[-1]
        plus = sign == "+"
        if kind == "ya":
            return zq[int(name[3])], ox
        if kind == "yb":
            return (zq[0], ox) if plus else (zq[1], ox)
        if kind in ("yq", "yqf"):
            return (zq[2], None) if plus else (zq[3], None)
        if kind == "yt":
            return (zq[3], None) if plus else (zq[2], None)
        if kind in ("ye", "yef"):
            return (zq[0], xl) if plus else (zq[1], xl)
        return (zq[1], xl) if plus else (zq[0], xl)

    def landing(name):
        if name[0] == "y":
            second = name[:2] == "yb" or name[:3] in ("yqf", "yef")
            k = 3 if second else 1 if "+" in name else 2
            return near(k, *region(name))
        k, i = int(name[1]), int(name[2])
        if name[0] == "x":
            return far(k, zq[i], xl)
        if name[0] == "n":
            return far(k, zq[i], ox)
        return far(k, zq[3 if i == 0 else 2], xl if name[3] == "a" else ox)

    def start(name):
        if name[0] == "y":
            plus = "+" in name
            dev = yp if plus else ym
            if name[:2] == "yb" or name[:3] in ("yqf", "yef"):
                ref = near(1 if plus else 2, *region(name))
                send(name, ref, ref, dev)
            else:
                quarter, half = region(name)
                send(name, mw.at[rows_of(512, quarter, half), :], near(0, quarter, half), dev)
            return
        k, i = int(name[1]), int(name[2])
        if name[0] == "x":
            if k == 0:
                send(name, mw.at[rows_of(512, zq[i], ox), :], near(0, zq[i], ox), xpart)
            elif k < 4:
                send(name, near(k, zq[i], ox), near(k, zq[i], ox), xpart)
            else:
                send(name, (up if k < 6 else down).at[far_rows(k, zq[i], ox), :], far(k, zq[i], ox), xpart)
        elif name[0] == "n":
            send(name, far(k, zq[i], xl), far(k, zq[i], xl), xn)
        else:
            ref = far(k, zq[i], xl if name[3] == "a" else ox)
            send(name, ref, ref, zp if i == 0 else zm)

    landed = set()
    queue = list(ORDER)

    def need(name):
        if name not in landed:
            landed.add(name)
            await_to(name, landing(name))

    def pump_at(i, steps):
        for n, time in steps.items():

            @pl.when(i == n)
            def _(time=time):
                pump(time)

    def pump(time):
        while queue and queue[0][1] <= time:
            name = queue.pop(0)[0]
            for other in needs(name):
                need(other)
            start(name)

    def need_far(k):
        for n, _ in ORDER:
            if n[0] in "xnz" and n[1] == str(k):
                need(n)

    def share(k):
        size = 1024 if k < 6 else 256
        rows = pl.ds((k % 2) * size, size)
        to = up4 if k < 6 else down4
        send(f"s{k}", to.at[2, rows, :], to.at[3, rows, :], sibling, lambda: to.at[3, rows, :])

    pump(3)

    local[0].wait()

    def norm_block(i):
        r = pl.ds(pl.multiple_of(i * 48, 16), 48)
        normed[r, :] = norm_rows(tok[r, :].astype(F32)).astype(BF)

    loop(9, norm_block)
    for n in (6, 3, 4, 5):
        local[n].start()
    early.wait()

    def pack(i):
        packed[:, cols(i, 256)] = jnp.dot(
            ps[...], normed[:, cols(i, 256)], preferred_element_type=F32
        ).astype(BF)

    loop(4, pack)

    def hcopy(i, src_at, dst_at, rows, dev):
        return pltpu.make_async_remote_copy(
            src_ref=packed.at[pl.ds(src_at, rows), :], dst_ref=halo.at[pl.ds(dst_at, rows), :],
            send_sem=hs.at[i], recv_sem=hr.at[i], device_id=dev, device_id_type=MESH,
        )

    middle_sends = [
        hcopy(0, SEND_W, HALO_E, 112, (lat, west)),
        hcopy(1, SEND_E, HALO_W, 112, (lat, east)),
    ]
    north_sends = [
        hcopy(2, SEND_N, HALO_S, 80, (lat - 1, lon)),
        hcopy(3, SEND_N, HALO_SE, 32, (lat - 1, west)),
        hcopy(4, SEND_N + 48, HALO_SW, 32, (lat - 1, east)),
    ]
    south_sends = [
        hcopy(5, SEND_S, HALO_N, 80, (lat + 1, lon)),
        hcopy(6, SEND_S, HALO_NE, 32, (lat + 1, west)),
        hcopy(7, SEND_S + 48, HALO_NW, 32, (lat + 1, east)),
    ]
    for cp in middle_sends:
        cp.start()

    @pl.when(north)
    def _():
        for cp in north_sends:
            cp.start()

    @pl.when(south)
    def _():
        for cp in south_sends:
            cp.start()

    local[1].wait()

    def permute(i):
        xp[:, cols(i, 256)] = jnp.dot(
            p1[...], normed[:, cols(i, 256)], preferred_element_type=F32
        ).astype(BF)

    loop(4, permute)

    @pl.when(jnp.logical_not(north))
    def _():
        halo[HALO_N : HALO_N + 80, :] = jnp.zeros((80, D), BF)
        halo[HALO_NW : HALO_NW + 64, :] = jnp.zeros((64, D), BF)

    @pl.when(jnp.logical_not(south))
    def _():
        halo[HALO_S : HALO_S + 80, :] = jnp.zeros((80, D), BF)
        halo[HALO_SW : HALO_SW + 64, :] = jnp.zeros((64, D), BF)

    local[2].wait()

    def project(i):
        qkv[:, cols(i, 256)] = jnp.dot(
            xp[...], qkvv[:, cols(i, 256)], preferred_element_type=F32
        ).astype(BF)
        pump_at(i, {3: 10, 7: 12})

    local[7].start()
    local[8].start()
    pump(8)
    loop(12, project)
    pump(14)
    send("up", up, up4.at[1], sibling, lambda: up4.at[1])
    send("down", down, down4.at[1], sibling, lambda: down4.at[1])

    edge = jnp.where(north, jnp.where(south, 0, 2), 1)
    low = lax.broadcasted_iota(jnp.int32, (1, 128), 1) < 64

    def attend(i, inner):
        head = cols(i, 128)
        head_k, head_v = cols(i, 128, D), cols(i, 128, 2 * D)
        for w, ((start, rows, _), parts) in enumerate(WINDOWS):
            if inner: continue
            r = slice(start, start + rows)
            q = qkv[r, head] * jnp.asarray(0.125, BF)
            zero = jnp.zeros_like(q)
            q = jnp.concatenate([jnp.where(low, q, zero), jnp.where(low, zero, q)], axis=0)
            ks, vs = [qkv[r, head_k]], [qkv[r, head_v]]
            for off, prows, _, _, _ in parts:
                ks.append(kvh[off : off + prows, head])
                vs.append(kvh[off : off + prows, head_k])
            k = jnp.concatenate(ks, axis=0) if parts else ks[0]
            v = jnp.concatenate(vs, axis=0) if parts else vs[0]
            m = k.shape[0]
            s = lax.dot_general(q, k, (((1,), (1,)), ((), ())), preferred_element_type=F32)
            s = s + bias[edge, w : w + 1, :m]
            e = jnp.exp(s - jnp.max(s, axis=-1, keepdims=True)).astype(BF)
            ve = jnp.concatenate([v, jnp.ones((m, 128), BF)], axis=1)
            o = jnp.dot(e, ve, preferred_element_type=F32)
            num = jnp.where(low, o[:rows, :128], o[rows:, :128])
            den = jnp.where(low, o[:rows, 128:], o[rows:, 128:])
            att[r, head] = (num / den).astype(BF)

    att = xp

    def pair_inner(i):
        attend(i, True)

    pump(16)

    for cp in middle_sends:
        cp.wait()

    @pl.when(north)
    def _():
        for cp in south_sends:
            cp.wait_recv()
        for cp in north_sends:
            cp.wait_send()

    @pl.when(south)
    def _():
        for cp in north_sends:
            cp.wait_recv()
        for cp in south_sends:
            cp.wait_send()

    def project_halo(i):
        kvh[:, cols(i, 256)] = jnp.dot(
            halo[...], qkvv[:, cols(i, 256, D)], preferred_element_type=F32
        ).astype(BF)

    pump(20)
    loop(8, project_halo)
    pump(22)

    def pair_outer(i):
        attend(i, False)
        pump_at(i, {0: 24, 1: 26, 2: 27, 3: 29, 4: 31, 5: 33, 6: 34, 7: 36})

    loop(8, pair_outer)

    local[3].wait()
    attr = normed

    def unpermute(i):
        attr[:, cols(i, 256)] = jnp.dot(
            p1t[...], att[:, cols(i, 256)], preferred_element_type=F32
        ).astype(BF)

    loop(4, unpermute)
    local[4].wait()

    def out_project(i):
        mixed = jnp.dot(attr[...], outv[:, cols(i, 256)], preferred_element_type=F32)
        mid[:, cols(i, 256)] = (tok[:, cols(i, 256)].astype(F32) + mixed).astype(BF)

    loop(4, out_project)
    store_mid = pltpu.make_async_copy(mid, mid_out, lsem.at[9])
    store_mid.start()
    pump(38)
    local[5].wait()

    def patch(i):
        g, t = i // 4, i % 4
        mgd[:, cols(i, 256)] = jnp.dot(
            pg[pl.ds(pl.multiple_of(g * GROUP, 16), GROUP), :], mid[:, cols(t, 256)],
            preferred_element_type=F32,
        ).astype(BF)

    loop(16, patch)

    def merge_norm(i):
        r = pl.ds(pl.multiple_of(i * 16, 16), 16)
        mgd[r, :] = norm_rows(mgd[r, :].astype(F32)).astype(BF)

    loop(GROUP // 16, merge_norm)
    mine = pl.ds(pl.multiple_of(c * GROUP, 16), GROUP)
    send("merged", mgd, xs.at[mine, :], sibling, lambda: mgd)
    keep_mgd = pltpu.make_async_copy(mgd, xs.at[mine, :], lsem.at[10])
    keep_mgd.start()

    pump(40)
    local[6].wait()
    for n, _ in ORDER:
        if n[0] == "y":
            need(n)
    pump(42)
    keep_mgd.wait()
    theirs_rows = pl.ds(pl.multiple_of((1 - c) * GROUP, 16), GROUP)
    await_to("merged", xs.at[theirs_rows, :])

    def merge(i):
        n = i // 2

        @pl.when(i == 2)
        def _():
            send("swap0", cc.at[1 - c, 0], theirs.at[0], sibling, lambda: theirs.at[0])
            pump(45)
            for k in range(4):
                need_far(k)

        h = jnp.where(n == 0, xh, 1 - xh)
        first = 4 * (i % 2) + h
        v = jnp.zeros((2 * GROUP, 256), F32)
        for g in range(4):
            r = slice(g * D, (g + 1) * D)
            w = jnp.concatenate([wv[first, r, :], wv[first + 2, r, :]], axis=1)
            v += jnp.dot(xs[:, r], w, preferred_element_type=F32)
        v = v.astype(BF)
        cc[0, n, :, cols(i % 2, 256)] = v[:GROUP]
        cc[1, n, :, cols(i % 2, 256)] = v[GROUP:]

    def place_columns(n, core, get):
        h = xh if n == 0 else 1 - xh
        for j in range(4):
            at = pl.multiple_of((4 * j + 2 * h + core) * 128, 128)
            coarse[:, pl.ds(at, 128)] = get(slice(j * 128, (j + 1) * 128))

    loop(4, merge)
    send("swap1", cc.at[1 - c, 1], theirs.at[1], sibling, lambda: theirs.at[1])
    pump(48)
    for n in (0, 1):
        place_columns(n, c, lambda t, n=n: cc[c, n, :, t])
    for n in (0, 1):
        await_to(f"swap{n}", theirs.at[n])
        place_columns(n, 1 - c, lambda t, n=n: theirs[n, :, t])

    def coarse_norm(i):
        r = pl.ds(pl.multiple_of(i * 16, 16), 16)
        cn[0, r, :] = norm_rows(coarse[r, :].astype(F32)).astype(BF)

    loop(GROUP // 16, coarse_norm)

    send("ag+", cn.at[0], cn.at[2], yp, lambda: cn.at[2])
    send("ag-", cn.at[0], cn.at[3], ym, lambda: cn.at[3])
    pump(57)
    need_far(4)
    share(4)
    for n in (7, 8):
        local[n].wait()
    await_to("up", up4.at[1])
    await_to("down", down4.at[1])

    def ffn(n):
        first = 2 - 2 * n
        rows = 2 * GROUP

        def up_step(i):
            q, t = i // 2, i % 2
            x = cn[pl.ds(first, 2)].reshape(rows, DC)
            h = jnp.dot(x, up4[q, :, cols(t, 256)], preferred_element_type=F32)
            hid[:, cols(i, 256)] = gelu(h).astype(BF)

        loop(8, up_step)

        def down_step(i):
            t = cols(i, 256)
            v = jnp.zeros((rows, 256), F32)
            for q in range(4):
                v += jnp.dot(hid[:, q * 512 : (q + 1) * 512], down4[q, :, t], preferred_element_type=F32)
            acc[:, t] = v[:GROUP] + coarse[:, t].astype(F32)
            pt[first, :, t] = v[:GROUP].astype(BF)
            pt[first + 1, :, t] = v[GROUP:].astype(BF)

        loop(8, down_step)

        @pl.when(n == 0)
        def _():
            send("rs2", pt.at[2], rb.at[3], ym, lambda: rb.at[3])
            send("rs3", pt.at[3], rb.at[2], yp, lambda: rb.at[2])
            await_to("ag2+", cn.at[1, A_ROWS, :])
            await_to("ag2-", cn.at[1, B_ROWS, :])

    await_to("ag+", cn.at[2])
    send("ag2+", cn.at[2, A_ROWS, :], cn.at[1, A_ROWS, :], yp, lambda: cn.at[1, A_ROWS, :])
    await_to("ag-", cn.at[3])
    send("ag2-", cn.at[3, B_ROWS, :], cn.at[1, B_ROWS, :], ym, lambda: cn.at[1, B_ROWS, :])
    pump(99)
    for k in (5, 6, 7):
        need_far(k)
        share(k)
    for k in (4, 5, 6, 7):
        size = 1024 if k < 6 else 256
        await_to(f"s{k}", (up4 if k < 6 else down4).at[3, pl.ds((k % 2) * size, size), :])
    loop(2, ffn)
    send("rs1", pt.at[1], rb.at[1], y2, lambda: rb.at[1])
    await_to("rs2", rb.at[3])
    await_to("rs3", rb.at[2])

    def add_near(i):
        t = cols(i, 512)
        acc[:, t] += rb[2, :, t].astype(F32) + rb[3, :, t].astype(F32)

    loop(4, add_near)
    await_to("rs1", rb.at[1])

    def add_far(i):
        t = cols(i, 512)
        acc[:, t] += rb[1, :, t].astype(F32)

    loop(4, add_far)
    for r in range(9):
        out[r] = acc[12 * r : 12 * r + 12, :].astype(BF)
    for name, like in sends.items():
        remote(name, like(), like(), yp).wait_send()
    store_mid.wait()


VM = pl.BlockSpec(memory_space=pltpu.VMEM)
HBM = pl.BlockSpec(memory_space=pltpu.HBM)
DMA = pltpu.SemaphoreType.DMA


def per_device(tokens, qkv_weight, out_weight, merge_weight, up_weight, down_weight):
    order, packed, patch = _tables()
    p1 = jnp.asarray(order, BF)
    p1t = jnp.asarray(order.T, BF)
    pg = jnp.asarray(patch, BF)

    def vmem(*shape, kind=BF):
        return pltpu.VMEM(shape, kind)

    mid, coarse_out = pl.pallas_call(
        kernel,
        name="whole",
        out_shape=(
            jax.ShapeDtypeStruct((CELLS, D), BF),
            jax.ShapeDtypeStruct((ROWS // 2, COLS // 2, DC), BF),
        ),
        in_specs=[HBM, HBM, HBM, VM] + [HBM] * 7,
        out_specs=(HBM, VM),
        scratch_shapes=[
            vmem(CELLS, D),
            vmem(SENT, CELLS),
            vmem(OWN, CELLS),
            vmem(CELLS, OWN),
            vmem(4 * GROUP, CELLS),
            vmem(D, 3 * D),
            vmem(D, D),
            vmem(8, 4 * D, 128),
            vmem(4, DC, 512),
            vmem(4, 512, DC),
            vmem(CELLS, D),
            vmem(SENT, D),
            vmem(OWN, D),
            vmem(HALO, D),
            vmem(OWN, 3 * D),
            vmem(HALO, 2 * D),
            vmem(CELLS, D),
            vmem(GROUP, 4 * D),
            vmem(2 * GROUP, 4 * D),
            vmem(2, 2, GROUP, 512),
            vmem(2, GROUP, 512),
            vmem(GROUP, DC),
            vmem(4, GROUP, DC),
            vmem(2 * GROUP, DC),
            vmem(GROUP, DC, kind=F32),
            vmem(4, GROUP, DC),
            vmem(4, GROUP, DC),
            DMA((12,)),
            DMA((HALO_SENDS,)),
            DMA((HALO_SENDS,)),
            DMA((len(WSEMS),)),
            DMA((len(WSEMS),)),
        ],
        compiler_params=pltpu.CompilerParams(
            collective_id=0, has_side_effects=True, vmem_limit_bytes=62 * 2**20
        ),
    )(
        tokens.reshape(CELLS, D), jnp.asarray(packed, BF), p1, jnp.asarray(_bias()), qkv_weight, out_weight, merge_weight, p1t, pg,
        up_weight, down_weight,
    )
    return mid.reshape(ROWS, COLS, D), coarse_out


def solution(mesh):
    return jax.shard_map(
        per_device,
        mesh=mesh,
        in_specs=(P("lat", "lon", None), P(), P(), P(None, "lon"), P(None, "lon"), P("lon", None)),
        out_specs=(P("lat", "lon", None), P("lat", "lon", None)),
        check_vma=False,
    )
```

```python
import functools

import jax
import jax.numpy as jnp
import numpy as np
from jax import lax
from jax.experimental import pallas as pl
from jax.experimental.pallas import tpu as pltpu
from jax.sharding import PartitionSpec as P

MESH = pl.DeviceIdType.MESH
BF = jnp.bfloat16
F32 = jnp.float32
NEG = -1e30

ROWS, COLS, D, DC, HEADS = 18, 24, 1024, 2048, 16
CELLS = ROWS * COLS
GROUP = 112
HIGH = (3, 6, 6, 3)
WIDE = (6, 12, 6)
TOP = (0, 3, 9, 15)
LEFT = (0, 6, 18)


def _round(n):
    return -(-n // 16) * 16


PIECE = {}
_at = 0
for _b in range(3):
    for _a in range(4):
        PIECE[_a, _b] = (_at, _round(HIGH[_a] * WIDE[_b]), HIGH[_a] * WIDE[_b])
        _at += PIECE[_a, _b][1]
OWN = _at
SEND_W, SEND_E, SEND_N, SEND_S, SENT = 0, 112, 224, 304, 384
HALO_W, HALO_E, HALO_N, HALO_S = 0, 112, 224, 304
HALO_NW, HALO_NE, HALO_SW, HALO_SE = 384, 416, 448, 480
HALO = 512


def _tables():
    order = np.zeros((OWN, CELLS), np.float32)
    for (a, b), (at, _, _) in PIECE.items():
        k = 0
        for i in range(HIGH[a]):
            for j in range(WIDE[b]):
                order[at + k, (TOP[a] + i) * COLS + LEFT[b] + j] = 1
                k += 1
    packed = np.zeros((SENT, CELLS), np.float32)
    column = [(a, 0) for a in range(4)]
    for start, pieces in (
        (SEND_W, column),
        (SEND_E, [(a, 2) for a, _ in column]),
        (SEND_N, [(0, b) for b in range(3)]),
        (SEND_S, [(3, b) for b in range(3)]),
    ):
        k = start
        for a, b in pieces:
            n = PIECE[a, b][2]
            packed[k : k + n] = order[PIECE[a, b][0] : PIECE[a, b][0] + n]
            k += n
    patch = np.zeros((4 * GROUP, CELLS), np.float32)
    for g in range(4):
        for r in range(ROWS // 2):
            for c in range(COLS // 2):
                cell = (2 * r + g // 2) * COLS + 2 * c + g % 2
                patch[g * GROUP + r * (COLS // 2) + c, cell] = 1
    return order, packed, patch


def _span(base, start, count, side):
    low = start // 16 * 16
    return base + low, _round(start + count) - low, start - low, start - low + count, side


def _window_parts():
    out = []
    along, across = ((0, 18), (18, 36), (54, 36), (90, 18)), ((0, 18), (18, 36), (54, 18))
    for b in range(3):
        for a in range(4):
            side = "n" if a == 0 else "s" if a == 3 else ""
            parts = []
            if b != 1:
                parts.append(_span(HALO_W if b == 0 else HALO_E, *along[a], ""))
            if side:
                parts.append(_span(HALO_N if a == 0 else HALO_S, *across[b], side))
            corner = {(0, 0): HALO_NW, (0, 2): HALO_NE, (3, 0): HALO_SW, (3, 2): HALO_SE}
            if (a, b) in corner:
                first = 6 if b == 0 else 0
                parts.append((corner[a, b], 32, first, first + 18, side))
            out.append((PIECE[a, b], parts))
    return out


WINDOWS = _window_parts()


def _bias():
    bias = np.full((3, 16, 128), NEG, np.float32)
    for edge in range(3):
        for w, ((_, rows, valid), parts) in enumerate(WINDOWS):
            bias[edge, w, :valid] = 0
            at = rows
            for _, prows, first, last, side in parts:
                gone = (edge == 1 and side == "n") or (edge == 2 and side == "s")
                if not gone:
                    bias[edge, w, at + first : at + last] = 0
                at += prows
    return bias


def place():
    lat, lon = lax.axis_index("lat"), lax.axis_index("lon")
    z, xl = lat // 2, lat % 2
    y, xh, c = lon // 4, (lon // 2) % 2, lon % 2
    return lat, lon, z, xl, y, xh, c


def norm_rows(x):
    center = x - jnp.mean(x, axis=-1, keepdims=True)
    spread = jnp.mean(center * center, axis=-1, keepdims=True)
    return center * lax.rsqrt(spread + 1e-5)


def loop(n, body):
    def step(i, carry):
        body(i)
        return carry

    lax.fori_loop(0, n, step, 0)


def cols(i, size, base=0):
    return pl.ds(pl.multiple_of(base + i * size, 128), size)


HALO_SENDS = 8
ORDER = (
    ("x00", 3), ("ya+0", 3), ("ya-1", 3), ("ya+1", 7), ("ya-0", 7), ("z00a", 8),
    ("yb+", 11), ("yb-", 11), ("n00", 11), ("x01", 12), ("yq+", 14), ("yq-", 14),
    ("x10", 15), ("z00b", 16), ("n01", 17), ("z01a", 17), ("x11", 18), ("ye+", 20),
    ("ye-", 20), ("n10", 20), ("z10a", 20), ("x20", 21), ("z01b", 22), ("yt+", 23),
    ("yt-", 23), ("n11", 23), ("x21", 24), ("z10b", 25), ("z11a", 25), ("n20", 26),
    ("x30", 27), ("z11b", 28), ("z20a", 28), ("yu+", 29), ("yu-", 29), ("n21", 29),
    ("x31", 30), ("z20b", 31), ("z21a", 31), ("yef+", 32), ("yef-", 32), ("n30", 32),
    ("x40", 33), ("z21b", 34), ("z30a", 34), ("yqf+", 35), ("yqf-", 35), ("n31", 35),
    ("x41", 36), ("z30b", 37), ("z31a", 37), ("n40", 38), ("x50", 39), ("z31b", 40),
    ("z40a", 40), ("n41", 41), ("x51", 42), ("z40b", 43), ("z41a", 43), ("n50", 44),
    ("x60", 46), ("z41b", 46), ("z50a", 46), ("n51", 48), ("x61", 49), ("z50b", 50),
    ("z51a", 50), ("n60", 51), ("x70", 52), ("z51b", 53), ("z60a", 53), ("n61", 54),
    ("x71", 55), ("z60b", 56), ("z61a", 56), ("n70", 57), ("z61b", 59), ("z70a", 59),
    ("n71", 60), ("z70b", 62), ("z71a", 62), ("z71b", 65),
)
WSEMS = {}
for _n in (
    [n for n, _ in ORDER]
    + [f"s{k}" for k in (4, 5, 6, 7)]
    + ["up", "down", "merged", "swap0", "swap1"]
    + ["ag+", "ag-", "ag2+", "ag2-", "rs1", "rs2", "rs3"]
):
    WSEMS[_n] = len(WSEMS)


def needs(name):
    if name[0] in "nz":
        return [("n" if name[-1] == "b" else "x") + name[1:3]]
    if name[0] == "x":
        k, i = int(name[1]), name[2]
        return {1: [f"ya+{i}"], 2: [f"ya-{i}"], 3: ["yb+" if i == "0" else "yb-"]}.get(k, [])
    first = {"yb+": "ya+0", "yb-": "ya-1", "yqf+": "yq+", "yqf-": "yq-", "yef+": "ye+", "yef-": "ye-"}
    return [first[name]] if name in first else []


A_ROWS, B_ROWS = pl.ds(0, 64), pl.ds(64, 48)


def gelu(x):
    return 0.5 * x * (1.0 + lax.erf(x * np.float32(0.5**0.5)))


def kernel(
    tok_in, ps_in, p1_in, bias, qkvw, outw, mw, p1t_in, pg_in, up, down,
    mid_out, out,
    tok, ps, p1, p1t, pg, qkvv, outv, wv, up4, down4,
    normed, packed, xp, halo, qkv, kvh, mid, mgd,
    xs, cc, theirs, coarse, cn, hid, acc, pt, rb,
    lsem, hs, hr, ws, wr,
):
    lat, lon, z, xl, y, xh, c = place()
    north, south = lat > 0, lat < 7
    west, east = (lon + 15) % 16, (lon + 1) % 16
    yp = (lat, (lon + 4) % 16)
    ym = (lat, (lon + 12) % 16)
    y2 = (lat, (lon + 8) % 16)
    zp = ((lat + 2) % 8, lon)
    zm = ((lat + 6) % 8, lon)
    xpart = (2 * z + 1 - xl, 4 * y + 2 * (1 - xh) + c)
    xn = (lat + 1 - 2 * xl, lon)
    sibling = (lat, lon + 1 - 2 * c)

    barrier = pltpu.get_barrier_semaphore()

    def greet(dev):
        pl.semaphore_signal(barrier, inc=1, device_id=dev, device_id_type=MESH)

    partners = ((lat, west), (lat, east), yp, ym, y2, zp, zm, xpart, xn, sibling)
    for dev in partners:
        greet(dev)

    @pl.when(north)
    def _():
        for o in (west, lon, east):
            greet((lat - 1, o))

    @pl.when(south)
    def _():
        for o in (west, lon, east):
            greet((lat + 1, o))

    own = 2 * y + xh
    local = [
        pltpu.make_async_copy(tok_in, tok, lsem.at[0]),
        pltpu.make_async_copy(p1_in, p1, lsem.at[1]),
        pltpu.make_async_copy(qkvw, qkvv, lsem.at[2]),
        pltpu.make_async_copy(p1t_in, p1t, lsem.at[3]),
        pltpu.make_async_copy(outw, outv, lsem.at[4]),
        pltpu.make_async_copy(pg_in, pg, lsem.at[5]),
        pltpu.make_async_copy(mw, wv.at[own], lsem.at[6]),
        pltpu.make_async_copy(up, up4.at[0], lsem.at[7]),
        pltpu.make_async_copy(down, down4.at[0], lsem.at[8]),
    ]
    early = pltpu.make_async_copy(ps_in, ps, lsem.at[11])
    local[0].start()
    early.start()
    local[1].start()
    local[2].start()

    count = len(partners) + jnp.where(north, 3, 0) + jnp.where(south, 3, 0)
    pl.semaphore_wait(barrier, count)

    shift = [2 * ((y + d) % 4) for d in (0, 3, 1, 2)]
    slots = {False: [v + xh for v in shift], True: [v + 1 - xh for v in shift]}
    zq = [(z + d) % 4 for d in range(4)]

    def block(k, other):
        return slots[other][k]

    def rows_of(size, quarter, half, base=0):
        at = base + quarter * 2 * size
        if half is None:
            return pl.ds(pl.multiple_of(at, size), 2 * size)
        return pl.ds(pl.multiple_of(at + half * size, size), size)

    sends = {}

    def remote(name, src, dst, dev):
        i = WSEMS[name]
        return pltpu.make_async_remote_copy(
            src_ref=src, dst_ref=dst, send_sem=ws.at[i], recv_sem=wr.at[i],
            device_id=dev, device_id_type=MESH,
        )

    def send(name, src, dst, dev, like=None):
        remote(name, src, dst, dev).start()
        if like is None:
            rows, width = dst.shape
            buffer = {128: wv, 512: up4, DC: down4}[width]

            def like():
                return buffer.at[0, pl.ds(0, rows), :]

        sends[name] = like

    def await_to(name, dst):
        remote(name, dst, dst, yp).wait_recv()

    def near(k, quarter, half):
        return wv.at[block(k, False), rows_of(512, quarter, half), :]

    def far_rows(k, quarter, half):
        if k < 6:
            return rows_of(128, quarter, half, (k - 4) * 1024)
        return rows_of(32, quarter, half, (k - 6) * 256)

    def far(k, quarter, half):
        if k < 4:
            return wv.at[block(k, True), rows_of(512, quarter, half), :]
        return (up4 if k < 6 else down4).at[2, far_rows(k, quarter, half), :]

    ox = 1 - xl

    def region(name):
        kind, sign = name[:-2] if name[1] == "a" else name[:-1], name[2] if name[1] == "a" else name[-1]
        plus = sign == "+"
        if kind == "ya":
            return zq[int(name[3])], ox
        if kind == "yb":
            return (zq[0], ox) if plus else (zq[1], ox)
        if kind in ("yq", "yqf"):
            return (zq[2], None) if plus else (zq[3], None)
        if kind == "yt":
            return (zq[3], None) if plus else (zq[2], None)
        if kind in ("ye", "yef"):
            return (zq[0], xl) if plus else (zq[1], xl)
        return (zq[1], xl) if plus else (zq[0], xl)

    def landing(name):
        if name[0] == "y":
            second = name[:2] == "yb" or name[:3] in ("yqf", "yef")
            k = 3 if second else 1 if "+" in name else 2
            return near(k, *region(name))
        k, i = int(name[1]), int(name[2])
        if name[0] == "x":
            return far(k, zq[i], xl)
        if name[0] == "n":
            return far(k, zq[i], ox)
        return far(k, zq[3 if i == 0 else 2], xl if name[3] == "a" else ox)

    def start(name):
        if name[0] == "y":
            plus = "+" in name
            dev = yp if plus else ym
            if name[:2] == "yb" or name[:3] in ("yqf", "yef"):
                ref = near(1 if plus else 2, *region(name))
                send(name, ref, ref, dev)
            else:
                quarter, half = region(name)
                send(name, mw.at[rows_of(512, quarter, half), :], near(0, quarter, half), dev)
            return
        k, i = int(name[1]), int(name[2])
        if name[0] == "x":
            if k == 0:
                send(name, mw.at[rows_of(512, zq[i], ox), :], near(0, zq[i], ox), xpart)
            elif k < 4:
                send(name, near(k, zq[i], ox), near(k, zq[i], ox), xpart)
            else:
                send(name, (up if k < 6 else down).at[far_rows(k, zq[i], ox), :], far(k, zq[i], ox), xpart)
        elif name[0] == "n":
            send(name, far(k, zq[i], xl), far(k, zq[i], xl), xn)
        else:
            ref = far(k, zq[i], xl if name[3] == "a" else ox)
            send(name, ref, ref, zp if i == 0 else zm)

    landed = set()
    queue = list(ORDER)

    def need(name):
        if name not in landed:
            landed.add(name)
            await_to(name, landing(name))

    def pump_at(i, steps):
        for n, time in steps.items():

            @pl.when(i == n)
            def _(time=time):
                pump(time)

    def pump(time):
        while queue and queue[0][1] <= time:
            name = queue.pop(0)[0]
            for other in needs(name):
                need(other)
            start(name)

    def need_far(k):
        for n, _ in ORDER:
            if n[0] in "xnz" and n[1] == str(k):
                need(n)

    def share(k):
        size = 1024 if k < 6 else 256
        rows = pl.ds((k % 2) * size, size)
        to = up4 if k < 6 else down4
        send(f"s{k}", to.at[2, rows, :], to.at[3, rows, :], sibling, lambda: to.at[3, rows, :])

    pump(3)

    local[0].wait()

    def norm_block(i):
        r = pl.ds(pl.multiple_of(i * 48, 16), 48)
        normed[r, :] = norm_rows(tok[r, :].astype(F32)).astype(BF)

    loop(9, norm_block)
    for n in (6, 3, 4, 5):
        local[n].start()
    early.wait()

    def pack(i):
        packed[:, cols(i, 256)] = jnp.dot(
            ps[...], normed[:, cols(i, 256)], preferred_element_type=F32
        ).astype(BF)

    loop(4, pack)

    def hcopy(i, src_at, dst_at, rows, dev):
        return pltpu.make_async_remote_copy(
            src_ref=packed.at[pl.ds(src_at, rows), :], dst_ref=halo.at[pl.ds(dst_at, rows), :],
            send_sem=hs.at[i], recv_sem=hr.at[i], device_id=dev, device_id_type=MESH,
        )

    middle_sends = [
        hcopy(0, SEND_W, HALO_E, 112, (lat, west)),
        hcopy(1, SEND_E, HALO_W, 112, (lat, east)),
    ]
    north_sends = [
        hcopy(2, SEND_N, HALO_S, 80, (lat - 1, lon)),
        hcopy(3, SEND_N, HALO_SE, 32, (lat - 1, west)),
        hcopy(4, SEND_N + 48, HALO_SW, 32, (lat - 1, east)),
    ]
    south_sends = [
        hcopy(5, SEND_S, HALO_N, 80, (lat + 1, lon)),
        hcopy(6, SEND_S, HALO_NE, 32, (lat + 1, west)),
        hcopy(7, SEND_S + 48, HALO_NW, 32, (lat + 1, east)),
    ]
    for cp in middle_sends:
        cp.start()

    @pl.when(north)
    def _():
        for cp in north_sends:
            cp.start()

    @pl.when(south)
    def _():
        for cp in south_sends:
            cp.start()

    local[1].wait()

    def permute(i):
        xp[:, cols(i, 256)] = jnp.dot(
            p1[...], normed[:, cols(i, 256)], preferred_element_type=F32
        ).astype(BF)

    loop(4, permute)

    @pl.when(jnp.logical_not(north))
    def _():
        halo[HALO_N : HALO_N + 80, :] = jnp.zeros((80, D), BF)
        halo[HALO_NW : HALO_NW + 64, :] = jnp.zeros((64, D), BF)

    @pl.when(jnp.logical_not(south))
    def _():
        halo[HALO_S : HALO_S + 80, :] = jnp.zeros((80, D), BF)
        halo[HALO_SW : HALO_SW + 64, :] = jnp.zeros((64, D), BF)

    local[2].wait()

    def project(i):
        qkv[:, cols(i, 256)] = jnp.dot(
            xp[...], qkvv[:, cols(i, 256)], preferred_element_type=F32
        ).astype(BF)
        pump_at(i, {3: 10, 7: 12})

    local[7].start()
    local[8].start()
    pump(8)
    loop(12, project)
    pump(14)
    send("up", up, up4.at[1], sibling, lambda: up4.at[1])
    send("down", down, down4.at[1], sibling, lambda: down4.at[1])

    edge = jnp.where(north, jnp.where(south, 0, 2), 1)
    low = lax.broadcasted_iota(jnp.int32, (1, 128), 1) < 64

    def attend(i, inner):
        head = cols(i, 128)
        head_k, head_v = cols(i, 128, D), cols(i, 128, 2 * D)
        for w, ((start, rows, _), parts) in enumerate(WINDOWS):
            if inner: continue
            r = slice(start, start + rows)
            q = qkv[r, head] * jnp.asarray(0.125, BF)
            zero = jnp.zeros_like(q)
            q = jnp.concatenate([jnp.where(low, q, zero), jnp.where(low, zero, q)], axis=0)
            ks, vs = [qkv[r, head_k]], [qkv[r, head_v]]
            for off, prows, _, _, _ in parts:
                ks.append(kvh[off : off + prows, head])
                vs.append(kvh[off : off + prows, head_k])
            k = jnp.concatenate(ks, axis=0) if parts else ks[0]
            v = jnp.concatenate(vs, axis=0) if parts else vs[0]
            m = k.shape[0]
            s = lax.dot_general(q, k, (((1,), (1,)), ((), ())), preferred_element_type=F32)
            s = s + bias[edge, w : w + 1, :m]
            e = jnp.exp(s - jnp.max(s, axis=-1, keepdims=True)).astype(BF)
            ve = jnp.concatenate([v, jnp.ones((m, 128), BF)], axis=1)
            o = jnp.dot(e, ve, preferred_element_type=F32)
            num = jnp.where(low, o[:rows, :128], o[rows:, :128])
            den = jnp.where(low, o[:rows, 128:], o[rows:, 128:])
            att[r, head] = (num / den).astype(BF)

    att = xp

    def pair_inner(i):
        attend(i, True)

    pump(16)

    for cp in middle_sends:
        cp.wait()

    @pl.when(north)
    def _():
        for cp in south_sends:
            cp.wait_recv()
        for cp in north_sends:
            cp.wait_send()

    @pl.when(south)
    def _():
        for cp in north_sends:
            cp.wait_recv()
        for cp in south_sends:
            cp.wait_send()

    def project_halo(i):
        kvh[:, cols(i, 256)] = jnp.dot(
            halo[...], qkvv[:, cols(i, 256, D)], preferred_element_type=F32
        ).astype(BF)
        pump_at(i, {3: 21})

    pump(20)
    loop(8, project_halo)
    pump(22)

    def pair_outer(i):
        attend(i, False)
        pump_at(i, {0: 24, 1: 26, 2: 27, 3: 29, 4: 31, 5: 33, 6: 34, 7: 36})

    loop(8, pair_outer)

    local[3].wait()
    attr = normed

    def unpermute(i):
        attr[:, cols(i, 256)] = jnp.dot(
            p1t[...], att[:, cols(i, 256)], preferred_element_type=F32
        ).astype(BF)
        pump_at(i, {1: 37})

    loop(4, unpermute)
    local[4].wait()

    def out_project(i):
        mixed = jnp.dot(attr[...], outv[:, cols(i, 256)], preferred_element_type=F32)
        mid[:, cols(i, 256)] = (tok[:, cols(i, 256)].astype(F32) + mixed).astype(BF)
        pump_at(i, {1: 38})

    loop(4, out_project)
    store_mid = pltpu.make_async_copy(mid, mid_out, lsem.at[9])
    store_mid.start()
    pump(38)
    local[5].wait()

    def patch(i):
        g, t = i // 4, i % 4
        mgd[:, cols(i, 256)] = jnp.dot(
            pg[pl.ds(pl.multiple_of(g * GROUP, 16), GROUP), :], mid[:, cols(t, 256)],
            preferred_element_type=F32,
        ).astype(BF)
        pump_at(i, {3: 39, 7: 40, 11: 41})

    loop(16, patch)

    def merge_norm(i):
        r = pl.ds(pl.multiple_of(i * 16, 16), 16)
        mgd[r, :] = norm_rows(mgd[r, :].astype(F32)).astype(BF)

    loop(GROUP // 16, merge_norm)
    mine = pl.ds(pl.multiple_of(c * GROUP, 16), GROUP)
    send("merged", mgd, xs.at[mine, :], sibling, lambda: mgd)
    keep_mgd = pltpu.make_async_copy(mgd, xs.at[mine, :], lsem.at[10])
    keep_mgd.start()

    pump(40)
    local[6].wait()
    for n, _ in ORDER:
        if n[0] == "y":
            need(n)
    pump(42)
    keep_mgd.wait()
    theirs_rows = pl.ds(pl.multiple_of((1 - c) * GROUP, 16), GROUP)
    await_to("merged", xs.at[theirs_rows, :])

    def merge(i):
        n = i // 2

        @pl.when(i == 2)
        def _():
            send("swap0", cc.at[1 - c, 0], theirs.at[0], sibling, lambda: theirs.at[0])
            pump(45)
            for k in range(4):
                need_far(k)

        h = jnp.where(n == 0, xh, 1 - xh)
        first = 4 * (i % 2) + h
        v = jnp.zeros((2 * GROUP, 256), F32)
        for g in range(4):
            r = slice(g * D, (g + 1) * D)
            w = jnp.concatenate([wv[first, r, :], wv[first + 2, r, :]], axis=1)
            v += jnp.dot(xs[:, r], w, preferred_element_type=F32)
        v = v.astype(BF)
        cc[0, n, :, cols(i % 2, 256)] = v[:GROUP]
        cc[1, n, :, cols(i % 2, 256)] = v[GROUP:]

    def place_columns(n, core, get):
        h = xh if n == 0 else 1 - xh
        for j in range(4):
            at = pl.multiple_of((4 * j + 2 * h + core) * 128, 128)
            coarse[:, pl.ds(at, 128)] = get(slice(j * 128, (j + 1) * 128))

    loop(4, merge)
    send("swap1", cc.at[1 - c, 1], theirs.at[1], sibling, lambda: theirs.at[1])
    pump(48)
    for n in (0, 1):
        place_columns(n, c, lambda t, n=n: cc[c, n, :, t])
    for n in (0, 1):
        await_to(f"swap{n}", theirs.at[n])
        place_columns(n, 1 - c, lambda t, n=n: theirs[n, :, t])

    def coarse_norm(i):
        r = pl.ds(pl.multiple_of(i * 16, 16), 16)
        cn[0, r, :] = norm_rows(coarse[r, :].astype(F32)).astype(BF)

    loop(GROUP // 16, coarse_norm)

    send("ag+", cn.at[0], cn.at[2], yp, lambda: cn.at[2])
    send("ag-", cn.at[0], cn.at[3], ym, lambda: cn.at[3])
    pump(58)
    for n in (7, 8):
        local[n].wait()
    await_to("up", up4.at[1])
    await_to("down", down4.at[1])

    def ffn(n):
        first = 2 - 2 * n
        rows = 2 * GROUP

        def up_step(i):
            q, t = i // 2, i % 2
            x = cn[pl.ds(first, 2)].reshape(rows, DC)
            h = jnp.dot(x, up4[q, :, cols(t, 256)], preferred_element_type=F32)
            hid[:, cols(i, 256)] = gelu(h).astype(BF)

        loop(8, up_step)

        def down_step(i):
            t = cols(i, 256)
            v = jnp.zeros((rows, 256), F32)
            for q in range(4):
                v += jnp.dot(hid[:, q * 512 : (q + 1) * 512], down4[q, :, t], preferred_element_type=F32)
            acc[:, t] = v[:GROUP] + coarse[:, t].astype(F32)
            pt[first, :, t] = v[:GROUP].astype(BF)
            pt[first + 1, :, t] = v[GROUP:].astype(BF)

        loop(8, down_step)

        @pl.when(n == 0)
        def _():
            send("rs2", pt.at[2], rb.at[3], ym, lambda: rb.at[3])
            send("rs3", pt.at[3], rb.at[2], yp, lambda: rb.at[2])
            await_to("ag2+", cn.at[1, A_ROWS, :])
            await_to("ag2-", cn.at[1, B_ROWS, :])

    await_to("ag+", cn.at[2])
    send("ag2+", cn.at[2, A_ROWS, :], cn.at[1, A_ROWS, :], yp, lambda: cn.at[1, A_ROWS, :])
    await_to("ag-", cn.at[3])
    send("ag2-", cn.at[3, B_ROWS, :], cn.at[1, B_ROWS, :], ym, lambda: cn.at[1, B_ROWS, :])
    pump(60)
    need_far(4)
    share(4)
    pump(99)
    for k in (5, 6, 7):
        need_far(k)
        share(k)
    for k in (4, 5, 6, 7):
        size = 1024 if k < 6 else 256
        await_to(f"s{k}", (up4 if k < 6 else down4).at[3, pl.ds((k % 2) * size, size), :])
    loop(2, ffn)
    send("rs1", pt.at[1], rb.at[1], y2, lambda: rb.at[1])
    await_to("rs2", rb.at[3])
    await_to("rs3", rb.at[2])

    def add_near(i):
        t = cols(i, 512)
        acc[:, t] += rb[2, :, t].astype(F32) + rb[3, :, t].astype(F32)

    loop(4, add_near)
    await_to("rs1", rb.at[1])

    def add_far(i):
        t = cols(i, 512)
        acc[:, t] += rb[1, :, t].astype(F32)

    loop(4, add_far)
    for r in range(9):
        out[r] = acc[12 * r : 12 * r + 12, :].astype(BF)
    for name, like in sends.items():
        remote(name, like(), like(), yp).wait_send()
    store_mid.wait()


VM = pl.BlockSpec(memory_space=pltpu.VMEM)
HBM = pl.BlockSpec(memory_space=pltpu.HBM)
DMA = pltpu.SemaphoreType.DMA


def per_device(tokens, qkv_weight, out_weight, merge_weight, up_weight, down_weight):
    order, packed, patch = _tables()
    p1 = jnp.asarray(order, BF)
    p1t = jnp.asarray(order.T, BF)
    pg = jnp.asarray(patch, BF)

    def vmem(*shape, kind=BF):
        return pltpu.VMEM(shape, kind)

    mid, coarse_out = pl.pallas_call(
        kernel,
        name="whole",
        out_shape=(
            jax.ShapeDtypeStruct((CELLS, D), BF),
            jax.ShapeDtypeStruct((ROWS // 2, COLS // 2, DC), BF),
        ),
        in_specs=[HBM, HBM, HBM, VM] + [HBM] * 7,
        out_specs=(HBM, VM),
        scratch_shapes=[
            vmem(CELLS, D),
            vmem(SENT, CELLS),
            vmem(OWN, CELLS),
            vmem(CELLS, OWN),
            vmem(4 * GROUP, CELLS),
            vmem(D, 3 * D),
            vmem(D, D),
            vmem(8, 4 * D, 128),
            vmem(4, DC, 512),
            vmem(4, 512, DC),
            vmem(CELLS, D),
            vmem(SENT, D),
            vmem(OWN, D),
            vmem(HALO, D),
            vmem(OWN, 3 * D),
            vmem(HALO, 2 * D),
            vmem(CELLS, D),
            vmem(GROUP, 4 * D),
            vmem(2 * GROUP, 4 * D),
            vmem(2, 2, GROUP, 512),
            vmem(2, GROUP, 512),
            vmem(GROUP, DC),
            vmem(4, GROUP, DC),
            vmem(2 * GROUP, DC),
            vmem(GROUP, DC, kind=F32),
            vmem(4, GROUP, DC),
            vmem(4, GROUP, DC),
            DMA((12,)),
            DMA((HALO_SENDS,)),
            DMA((HALO_SENDS,)),
            DMA((len(WSEMS),)),
            DMA((len(WSEMS),)),
        ],
        compiler_params=pltpu.CompilerParams(
            collective_id=0, has_side_effects=True, vmem_limit_bytes=62 * 2**20
        ),
    )(
        tokens.reshape(CELLS, D), jnp.asarray(packed, BF), p1, jnp.asarray(_bias()), qkv_weight, out_weight, merge_weight, p1t, pg,
        up_weight, down_weight,
    )
    return mid.reshape(ROWS, COLS, D), coarse_out


def solution(mesh):
    return jax.shard_map(
        per_device,
        mesh=mesh,
        in_specs=(P("lat", "lon", None), P(), P(), P(None, "lon"), P(None, "lon"), P("lon", None)),
        out_specs=(P("lat", "lon", None), P("lat", "lon", None)),
        check_vma=False,
    )
```

```python
import functools

import jax
import jax.numpy as jnp
import numpy as np
from jax import lax
from jax.experimental import pallas as pl
from jax.experimental.pallas import tpu as pltpu
from jax.sharding import PartitionSpec as P

MESH = pl.DeviceIdType.MESH
BF = jnp.bfloat16
F32 = jnp.float32
NEG = -1e30

ROWS, COLS, D, DC, HEADS = 18, 24, 1024, 2048, 16
CELLS = ROWS * COLS
GROUP = 112
HIGH = (3, 6, 6, 3)
WIDE = (6, 12, 6)
TOP = (0, 3, 9, 15)
LEFT = (0, 6, 18)


def _round(n):
    return -(-n // 16) * 16


PIECE = {}
_at = 0
for _b in range(3):
    for _a in range(4):
        PIECE[_a, _b] = (_at, _round(HIGH[_a] * WIDE[_b]), HIGH[_a] * WIDE[_b])
        _at += PIECE[_a, _b][1]
OWN = _at
SEND_W, SEND_E, SEND_N, SEND_S, SENT = 0, 112, 224, 304, 384
HALO_W, HALO_E, HALO_N, HALO_S = 0, 112, 224, 304
HALO_NW, HALO_NE, HALO_SW, HALO_SE = 384, 416, 448, 480
HALO = 512


def _tables():
    order = np.zeros((OWN, CELLS), np.float32)
    for (a, b), (at, _, _) in PIECE.items():
        k = 0
        for i in range(HIGH[a]):
            for j in range(WIDE[b]):
                order[at + k, (TOP[a] + i) * COLS + LEFT[b] + j] = 1
                k += 1
    packed = np.zeros((SENT, CELLS), np.float32)
    column = [(a, 0) for a in range(4)]
    for start, pieces in (
        (SEND_W, column),
        (SEND_E, [(a, 2) for a, _ in column]),
        (SEND_N, [(0, b) for b in range(3)]),
        (SEND_S, [(3, b) for b in range(3)]),
    ):
        k = start
        for a, b in pieces:
            n = PIECE[a, b][2]
            packed[k : k + n] = order[PIECE[a, b][0] : PIECE[a, b][0] + n]
            k += n
    patch = np.zeros((4 * GROUP, CELLS), np.float32)
    for g in range(4):
        for r in range(ROWS // 2):
            for c in range(COLS // 2):
                cell = (2 * r + g // 2) * COLS + 2 * c + g % 2
                patch[g * GROUP + r * (COLS // 2) + c, cell] = 1
    return order, packed, patch


def _span(base, start, count, side):
    low = start // 16 * 16
    return base + low, _round(start + count) - low, start - low, start - low + count, side


def _window_parts():
    out = []
    along, across = ((0, 18), (18, 36), (54, 36), (90, 18)), ((0, 18), (18, 36), (54, 18))
    for b in range(3):
        for a in range(4):
            side = "n" if a == 0 else "s" if a == 3 else ""
            parts = []
            if b != 1:
                parts.append(_span(HALO_W if b == 0 else HALO_E, *along[a], ""))
            if side:
                parts.append(_span(HALO_N if a == 0 else HALO_S, *across[b], side))
            corner = {(0, 0): HALO_NW, (0, 2): HALO_NE, (3, 0): HALO_SW, (3, 2): HALO_SE}
            if (a, b) in corner:
                first = 6 if b == 0 else 0
                parts.append((corner[a, b], 32, first, first + 18, side))
            out.append((PIECE[a, b], parts))
    return out


WINDOWS = _window_parts()


def _bias():
    bias = np.full((3, 16, 128), NEG, np.float32)
    for edge in range(3):
        for w, ((_, rows, valid), parts) in enumerate(WINDOWS):
            bias[edge, w, :valid] = 0
            at = rows
            for _, prows, first, last, side in parts:
                gone = (edge == 1 and side == "n") or (edge == 2 and side == "s")
                if not gone:
                    bias[edge, w, at + first : at + last] = 0
                at += prows
    return bias


def place():
    lat, lon = lax.axis_index("lat"), lax.axis_index("lon")
    z, xl = lat // 2, lat % 2
    y, xh, c = lon // 4, (lon // 2) % 2, lon % 2
    return lat, lon, z, xl, y, xh, c


def norm_rows(x):
    center = x - jnp.mean(x, axis=-1, keepdims=True)
    spread = jnp.mean(center * center, axis=-1, keepdims=True)
    return center * lax.rsqrt(spread + 1e-5)


def loop(n, body):
    def step(i, carry):
        body(i)
        return carry

    lax.fori_loop(0, n, step, 0)


def cols(i, size, base=0):
    return pl.ds(pl.multiple_of(base + i * size, 128), size)


HALO_SENDS = 8
ORDER = (
    ("x00", 3), ("ya+0", 3), ("ya-1", 3), ("ya+1", 7), ("ya-0", 7), ("z00a", 8),
    ("yb+", 11), ("yb-", 11), ("n00", 11), ("x01", 12), ("yq+", 14), ("yq-", 14),
    ("x10", 15), ("z00b", 16), ("n01", 17), ("z01a", 17), ("x11", 18), ("ye+", 20),
    ("ye-", 20), ("n10", 20), ("z10a", 20), ("x20", 21), ("z01b", 22), ("yt+", 23),
    ("yt-", 23), ("n11", 23), ("x21", 24), ("z10b", 25), ("z11a", 25), ("n20", 26),
    ("x30", 27), ("z11b", 28), ("z20a", 28), ("yu+", 29), ("yu-", 29), ("n21", 29),
    ("x31", 30), ("z20b", 31), ("z21a", 31), ("yef+", 32), ("yef-", 32), ("n30", 32),
    ("x40", 33), ("z21b", 34), ("z30a", 34), ("yqf+", 35), ("yqf-", 35), ("n31", 35),
    ("x41", 36), ("z30b", 37), ("z31a", 37), ("n40", 38), ("x50", 39), ("z31b", 40),
    ("z40a", 40), ("n41", 41), ("x51", 42), ("z40b", 43), ("z41a", 43), ("n50", 44),
    ("x60", 46), ("z41b", 46), ("z50a", 46), ("n51", 48), ("x61", 49), ("z50b", 50),
    ("z51a", 50), ("n60", 51), ("x70", 52), ("z51b", 53), ("z60a", 53), ("n61", 54),
    ("x71", 55), ("z60b", 56), ("z61a", 56), ("n70", 57), ("z61b", 59), ("z70a", 59),
    ("n71", 60), ("z70b", 62), ("z71a", 62), ("z71b", 65),
)
WSEMS = {}
for _n in (
    [n for n, _ in ORDER]
    + [f"s{k}" for k in (4, 5, 6, 7)]
    + ["up", "down", "merged", "swap0", "swap1"]
    + ["ag+", "ag-", "ag2+", "ag2-", "rs1", "rs2", "rs3"]
):
    WSEMS[_n] = len(WSEMS)


def needs(name):
    if name[0] in "nz":
        return [("n" if name[-1] == "b" else "x") + name[1:3]]
    if name[0] == "x":
        k, i = int(name[1]), name[2]
        return {1: [f"ya+{i}"], 2: [f"ya-{i}"], 3: ["yb+" if i == "0" else "yb-"]}.get(k, [])
    first = {"yb+": "ya+0", "yb-": "ya-1", "yqf+": "yq+", "yqf-": "yq-", "yef+": "ye+", "yef-": "ye-"}
    return [first[name]] if name in first else []


A_ROWS, B_ROWS = pl.ds(0, 64), pl.ds(64, 48)


def gelu(x):
    return 0.5 * x * (1.0 + lax.erf(x * np.float32(0.5**0.5)))


def kernel(
    tok_in, ps_in, p1_in, bias, qkvw, outw, mw, p1t_in, pg_in, up, down,
    mid_out, out,
    tok, ps, p1, p1t, pg, qkvv, outv, wv, up4, down4,
    normed, packed, xp, halo, qkv, kvh, mid, mgd,
    xs, cc, theirs, coarse, cn, hid, acc, pt, rb,
    lsem, hs, hr, ws, wr,
):
    lat, lon, z, xl, y, xh, c = place()
    north, south = lat > 0, lat < 7
    west, east = (lon + 15) % 16, (lon + 1) % 16
    yp = (lat, (lon + 4) % 16)
    ym = (lat, (lon + 12) % 16)
    y2 = (lat, (lon + 8) % 16)
    zp = ((lat + 2) % 8, lon)
    zm = ((lat + 6) % 8, lon)
    xpart = (2 * z + 1 - xl, 4 * y + 2 * (1 - xh) + c)
    xn = (lat + 1 - 2 * xl, lon)
    sibling = (lat, lon + 1 - 2 * c)

    barrier = pltpu.get_barrier_semaphore()

    def greet(dev):
        pl.semaphore_signal(barrier, inc=1, device_id=dev, device_id_type=MESH)

    partners = ((lat, west), (lat, east), yp, ym, y2, zp, zm, xpart, xn, sibling)
    for dev in partners:
        greet(dev)

    @pl.when(north)
    def _():
        for o in (west, lon, east):
            greet((lat - 1, o))

    @pl.when(south)
    def _():
        for o in (west, lon, east):
            greet((lat + 1, o))

    own = 2 * y + xh
    local = [
        pltpu.make_async_copy(tok_in, tok, lsem.at[0]),
        pltpu.make_async_copy(p1_in, p1, lsem.at[1]),
        pltpu.make_async_copy(qkvw, qkvv, lsem.at[2]),
        pltpu.make_async_copy(p1t_in, p1t, lsem.at[3]),
        pltpu.make_async_copy(outw, outv, lsem.at[4]),
        pltpu.make_async_copy(pg_in, pg, lsem.at[5]),
        pltpu.make_async_copy(mw, wv.at[own], lsem.at[6]),
        pltpu.make_async_copy(up, up4.at[0], lsem.at[7]),
        pltpu.make_async_copy(down, down4.at[0], lsem.at[8]),
    ]
    early = pltpu.make_async_copy(ps_in, ps, lsem.at[11])
    local[0].start()
    early.start()
    local[1].start()
    local[2].start()

    count = len(partners) + jnp.where(north, 3, 0) + jnp.where(south, 3, 0)
    pl.semaphore_wait(barrier, count)

    shift = [2 * ((y + d) % 4) for d in (0, 3, 1, 2)]
    slots = {False: [v + xh for v in shift], True: [v + 1 - xh for v in shift]}
    zq = [(z + d) % 4 for d in range(4)]

    def block(k, other):
        return slots[other][k]

    def rows_of(size, quarter, half, base=0):
        at = base + quarter * 2 * size
        if half is None:
            return pl.ds(pl.multiple_of(at, size), 2 * size)
        return pl.ds(pl.multiple_of(at + half * size, size), size)

    sends = {}

    def remote(name, src, dst, dev):
        i = WSEMS[name]
        return pltpu.make_async_remote_copy(
            src_ref=src, dst_ref=dst, send_sem=ws.at[i], recv_sem=wr.at[i],
            device_id=dev, device_id_type=MESH,
        )

    def send(name, src, dst, dev, like=None):
        remote(name, src, dst, dev).start()
        if like is None:
            rows, width = dst.shape
            buffer = {128: wv, 512: up4, DC: down4}[width]

            def like():
                return buffer.at[0, pl.ds(0, rows), :]

        sends[name] = like

    def await_to(name, dst):
        remote(name, dst, dst, yp).wait_recv()

    def near(k, quarter, half):
        return wv.at[block(k, False), rows_of(512, quarter, half), :]

    def far_rows(k, quarter, half):
        if k < 6:
            return rows_of(128, quarter, half, (k - 4) * 1024)
        return rows_of(32, quarter, half, (k - 6) * 256)

    def far(k, quarter, half):
        if k < 4:
            return wv.at[block(k, True), rows_of(512, quarter, half), :]
        return (up4 if k < 6 else down4).at[2, far_rows(k, quarter, half), :]

    ox = 1 - xl

    def region(name):
        kind, sign = name[:-2] if name[1] == "a" else name[:-1], name[2] if name[1] == "a" else name[-1]
        plus = sign == "+"
        if kind == "ya":
            return zq[int(name[3])], ox
        if kind == "yb":
            return (zq[0], ox) if plus else (zq[1], ox)
        if kind in ("yq", "yqf"):
            return (zq[2], None) if plus else (zq[3], None)
        if kind == "yt":
            return (zq[3], None) if plus else (zq[2], None)
        if kind in ("ye", "yef"):
            return (zq[0], xl) if plus else (zq[1], xl)
        return (zq[1], xl) if plus else (zq[0], xl)

    def landing(name):
        if name[0] == "y":
            second = name[:2] == "yb" or name[:3] in ("yqf", "yef")
            k = 3 if second else 1 if "+" in name else 2
            return near(k, *region(name))
        k, i = int(name[1]), int(name[2])
        if name[0] == "x":
            return far(k, zq[i], xl)
        if name[0] == "n":
            return far(k, zq[i], ox)
        return far(k, zq[3 if i == 0 else 2], xl if name[3] == "a" else ox)

    def start(name):
        if name[0] == "y":
            plus = "+" in name
            dev = yp if plus else ym
            if name[:2] == "yb" or name[:3] in ("yqf", "yef"):
                ref = near(1 if plus else 2, *region(name))
                send(name, ref, ref, dev)
            else:
                quarter, half = region(name)
                send(name, mw.at[rows_of(512, quarter, half), :], near(0, quarter, half), dev)
            return
        k, i = int(name[1]), int(name[2])
        if name[0] == "x":
            if k == 0:
                send(name, mw.at[rows_of(512, zq[i], ox), :], near(0, zq[i], ox), xpart)
            elif k < 4:
                send(name, near(k, zq[i], ox), near(k, zq[i], ox), xpart)
            else:
                send(name, (up if k < 6 else down).at[far_rows(k, zq[i], ox), :], far(k, zq[i], ox), xpart)
        elif name[0] == "n":
            send(name, far(k, zq[i], xl), far(k, zq[i], xl), xn)
        else:
            ref = far(k, zq[i], xl if name[3] == "a" else ox)
            send(name, ref, ref, zp if i == 0 else zm)

    landed = set()
    queue = list(ORDER)

    def need(name):
        if name not in landed:
            landed.add(name)
            await_to(name, landing(name))

    def pump_at(i, steps):
        for n, time in steps.items():

            @pl.when(i == n)
            def _(time=time):
                pump(time)

    def pump(time):
        while queue and queue[0][1] <= time:
            name = queue.pop(0)[0]
            for other in needs(name):
                need(other)
            start(name)

    def need_far(k):
        for n, _ in ORDER:
            if n[0] in "xnz" and n[1] == str(k):
                need(n)

    def share(k):
        size = 1024 if k < 6 else 256
        rows = pl.ds((k % 2) * size, size)
        to = up4 if k < 6 else down4
        send(f"s{k}", to.at[2, rows, :], to.at[3, rows, :], sibling, lambda: to.at[3, rows, :])

    pump(3)

    local[0].wait()

    def norm_block(i):
        r = pl.ds(pl.multiple_of(i * 48, 16), 48)
        normed[r, :] = norm_rows(tok[r, :].astype(F32)).astype(BF)

    loop(9, norm_block)
    for n in (6, 3, 4, 5):
        local[n].start()
    early.wait()

    def pack(i):
        packed[:, cols(i, 256)] = jnp.dot(
            ps[...], normed[:, cols(i, 256)], preferred_element_type=F32
        ).astype(BF)

    loop(4, pack)

    def hcopy(i, src_at, dst_at, rows, dev):
        return pltpu.make_async_remote_copy(
            src_ref=packed.at[pl.ds(src_at, rows), :], dst_ref=halo.at[pl.ds(dst_at, rows), :],
            send_sem=hs.at[i], recv_sem=hr.at[i], device_id=dev, device_id_type=MESH,
        )

    middle_sends = [
        hcopy(0, SEND_W, HALO_E, 112, (lat, west)),
        hcopy(1, SEND_E, HALO_W, 112, (lat, east)),
    ]
    north_sends = [
        hcopy(2, SEND_N, HALO_S, 80, (lat - 1, lon)),
        hcopy(3, SEND_N, HALO_SE, 32, (lat - 1, west)),
        hcopy(4, SEND_N + 48, HALO_SW, 32, (lat - 1, east)),
    ]
    south_sends = [
        hcopy(5, SEND_S, HALO_N, 80, (lat + 1, lon)),
        hcopy(6, SEND_S, HALO_NE, 32, (lat + 1, west)),
        hcopy(7, SEND_S + 48, HALO_NW, 32, (lat + 1, east)),
    ]
    for cp in middle_sends:
        cp.start()

    @pl.when(north)
    def _():
        for cp in north_sends:
            cp.start()

    @pl.when(south)
    def _():
        for cp in south_sends:
            cp.start()

    local[1].wait()

    def permute(i):
        xp[:, cols(i, 256)] = jnp.dot(
            p1[...], normed[:, cols(i, 256)], preferred_element_type=F32
        ).astype(BF)

    loop(4, permute)

    @pl.when(jnp.logical_not(north))
    def _():
        halo[HALO_N : HALO_N + 80, :] = jnp.zeros((80, D), BF)
        halo[HALO_NW : HALO_NW + 64, :] = jnp.zeros((64, D), BF)

    @pl.when(jnp.logical_not(south))
    def _():
        halo[HALO_S : HALO_S + 80, :] = jnp.zeros((80, D), BF)
        halo[HALO_SW : HALO_SW + 64, :] = jnp.zeros((64, D), BF)

    local[2].wait()

    def project(i):
        qkv[:, cols(i, 256)] = jnp.dot(
            xp[...], qkvv[:, cols(i, 256)], preferred_element_type=F32
        ).astype(BF)
        pump_at(i, {3: 10, 7: 12})

    local[7].start()
    local[8].start()
    pump(8)
    loop(12, project)
    pump(14)
    send("up", up, up4.at[1], sibling, lambda: up4.at[1])
    send("down", down, down4.at[1], sibling, lambda: down4.at[1])

    edge = jnp.where(north, jnp.where(south, 0, 2), 1)
    low = lax.broadcasted_iota(jnp.int32, (1, 128), 1) < 64

    def attend(i, inner):
        head = cols(i, 128)
        head_k, head_v = cols(i, 128, D), cols(i, 128, 2 * D)
        for w, ((start, rows, _), parts) in enumerate(WINDOWS):
            if inner: continue
            r = slice(start, start + rows)
            q = qkv[r, head] * jnp.asarray(0.125, BF)
            zero = jnp.zeros_like(q)
            q = jnp.concatenate([jnp.where(low, q, zero), jnp.where(low, zero, q)], axis=0)
            ks, vs = [qkv[r, head_k]], [qkv[r, head_v]]
            for off, prows, _, _, _ in parts:
                ks.append(kvh[off : off + prows, head])
                vs.append(kvh[off : off + prows, head_k])
            k = jnp.concatenate(ks, axis=0) if parts else ks[0]
            v = jnp.concatenate(vs, axis=0) if parts else vs[0]
            m = k.shape[0]
            s = lax.dot_general(q, k, (((1,), (1,)), ((), ())), preferred_element_type=F32)
            s = s + bias[edge, w : w + 1, :m]
            e = jnp.exp(s - jnp.max(s, axis=-1, keepdims=True)).astype(BF)
            ve = jnp.concatenate([v, jnp.ones((m, 128), BF)], axis=1)
            o = jnp.dot(e, ve, preferred_element_type=F32)
            num = jnp.where(low, o[:rows, :128], o[rows:, :128])
            den = jnp.where(low, o[:rows, 128:], o[rows:, 128:])
            att[r, head] = (num / den).astype(BF)

    att = xp

    def pair_inner(i):
        attend(i, True)

    pump(16)

    for cp in middle_sends:
        cp.wait()

    @pl.when(north)
    def _():
        for cp in south_sends:
            cp.wait_recv()
        for cp in north_sends:
            cp.wait_send()

    @pl.when(south)
    def _():
        for cp in north_sends:
            cp.wait_recv()
        for cp in south_sends:
            cp.wait_send()

    def project_halo(i):
        kvh[:, cols(i, 256)] = jnp.dot(
            halo[...], qkvv[:, cols(i, 256, D)], preferred_element_type=F32
        ).astype(BF)
        pump_at(i, {3: 21})

    pump(20)
    loop(8, project_halo)
    pump(22)

    def pair_outer(i):
        attend(i, False)
        pump_at(i, {0: 24, 1: 26, 2: 27, 3: 29, 4: 31, 5: 33, 6: 34, 7: 36})

    loop(8, pair_outer)

    local[3].wait()
    attr = normed

    def unpermute(i):
        attr[:, cols(i, 256)] = jnp.dot(
            p1t[...], att[:, cols(i, 256)], preferred_element_type=F32
        ).astype(BF)
        pump_at(i, {1: 37})

    loop(4, unpermute)
    local[4].wait()

    def out_project(i):
        mixed = jnp.dot(attr[...], outv[:, cols(i, 256)], preferred_element_type=F32)
        mid[:, cols(i, 256)] = (tok[:, cols(i, 256)].astype(F32) + mixed).astype(BF)
        pump_at(i, {1: 38})

    loop(4, out_project)
    store_mid = pltpu.make_async_copy(mid, mid_out, lsem.at[9])
    store_mid.start()
    pump(38)
    local[5].wait()

    def patch(i):
        g, t = i // 4, i % 4
        mgd[:, cols(i, 256)] = jnp.dot(
            pg[pl.ds(pl.multiple_of(g * GROUP, 16), GROUP), :], mid[:, cols(t, 256)],
            preferred_element_type=F32,
        ).astype(BF)
        pump_at(i, {3: 39, 7: 40, 11: 41})

    loop(16, patch)

    def merge_norm(i):
        r = pl.ds(pl.multiple_of(i * 16, 16), 16)
        mgd[r, :] = norm_rows(mgd[r, :].astype(F32)).astype(BF)

    loop(GROUP // 16, merge_norm)
    mine = pl.ds(pl.multiple_of(c * GROUP, 16), GROUP)
    send("merged", mgd, xs.at[mine, :], sibling, lambda: mgd)
    keep_mgd = pltpu.make_async_copy(mgd, xs.at[mine, :], lsem.at[10])
    keep_mgd.start()

    pump(40)
    local[6].wait()
    for n, _ in ORDER:
        if n[0] == "y":
            need(n)
    pump(42)
    keep_mgd.wait()
    theirs_rows = pl.ds(pl.multiple_of((1 - c) * GROUP, 16), GROUP)
    await_to("merged", xs.at[theirs_rows, :])

    def merge(i):
        n = i // 2

        @pl.when(i == 2)
        def _():
            send("swap0", cc.at[1 - c, 0], theirs.at[0], sibling, lambda: theirs.at[0])
            pump(45)
            for k in range(4):
                need_far(k)

        h = jnp.where(n == 0, xh, 1 - xh)
        first = 4 * (i % 2) + h
        v = jnp.zeros((2 * GROUP, 256), F32)
        for g in range(4):
            r = slice(g * D, (g + 1) * D)
            w = jnp.concatenate([wv[first, r, :], wv[first + 2, r, :]], axis=1)
            v += jnp.dot(xs[:, r], w, preferred_element_type=F32)
        v = v.astype(BF)
        cc[0, n, :, cols(i % 2, 256)] = v[:GROUP]
        cc[1, n, :, cols(i % 2, 256)] = v[GROUP:]

    def place_columns(n, core, get):
        h = xh if n == 0 else 1 - xh
        for j in range(4):
            at = pl.multiple_of((4 * j + 2 * h + core) * 128, 128)
            coarse[:, pl.ds(at, 128)] = get(slice(j * 128, (j + 1) * 128))

    loop(4, merge)
    send("swap1", cc.at[1 - c, 1], theirs.at[1], sibling, lambda: theirs.at[1])
    pump(48)
    for n in (0, 1):
        place_columns(n, c, lambda t, n=n: cc[c, n, :, t])
    for n in (0, 1):
        await_to(f"swap{n}", theirs.at[n])
        place_columns(n, 1 - c, lambda t, n=n: theirs[n, :, t])

    def coarse_norm(i):
        r = pl.ds(pl.multiple_of(i * 16, 16), 16)
        cn[0, r, :] = norm_rows(coarse[r, :].astype(F32)).astype(BF)

    loop(GROUP // 16, coarse_norm)

    send("ag+", cn.at[0], cn.at[2], yp, lambda: cn.at[2])
    send("ag-", cn.at[0], cn.at[3], ym, lambda: cn.at[3])
    pump(58)
    for n in (7, 8):
        local[n].wait()
    await_to("up", up4.at[1])
    await_to("down", down4.at[1])

    def await_share(k):
        size = 1024 if k < 6 else 256
        await_to(f"s{k}", (up4 if k < 6 else down4).at[3, pl.ds((k % 2) * size, size), :])

    def ffn(n):
        first = 2 - 2 * n
        rows = 2 * GROUP

        def up_step(i):
            q, t = i // 2, i % 2
            x = cn[pl.ds(first, 2)].reshape(rows, DC)
            h = jnp.dot(x, up4[q, :, cols(t, 256)], preferred_element_type=F32)
            hid[:, cols(i, 256)] = gelu(h).astype(BF)

        loop(8, up_step)

        @pl.when(n == 0)
        def _():
            need_far(7)
            share(7)
            await_share(6)
            await_share(7)

        def down_step(i):
            t = cols(i, 256)
            v = jnp.zeros((rows, 256), F32)
            for q in range(4):
                v += jnp.dot(hid[:, q * 512 : (q + 1) * 512], down4[q, :, t], preferred_element_type=F32)
            acc[:, t] = v[:GROUP] + coarse[:, t].astype(F32)
            pt[first, :, t] = v[:GROUP].astype(BF)
            pt[first + 1, :, t] = v[GROUP:].astype(BF)

        loop(8, down_step)

        @pl.when(n == 0)
        def _():
            send("rs2", pt.at[2], rb.at[3], ym, lambda: rb.at[3])
            send("rs3", pt.at[3], rb.at[2], yp, lambda: rb.at[2])
            await_to("ag2+", cn.at[1, A_ROWS, :])
            await_to("ag2-", cn.at[1, B_ROWS, :])

    await_to("ag+", cn.at[2])
    send("ag2+", cn.at[2, A_ROWS, :], cn.at[1, A_ROWS, :], yp, lambda: cn.at[1, A_ROWS, :])
    await_to("ag-", cn.at[3])
    send("ag2-", cn.at[3, B_ROWS, :], cn.at[1, B_ROWS, :], ym, lambda: cn.at[1, B_ROWS, :])
    pump(60)
    need_far(4)
    share(4)
    pump(99)
    for k in (5, 6):
        need_far(k)
        share(k)
    for k in (4, 5):
        await_share(k)
    loop(2, ffn)
    send("rs1", pt.at[1], rb.at[1], y2, lambda: rb.at[1])
    await_to("rs2", rb.at[3])
    await_to("rs3", rb.at[2])

    def add_near(i):
        t = cols(i, 512)
        acc[:, t] += rb[2, :, t].astype(F32) + rb[3, :, t].astype(F32)

    loop(4, add_near)
    await_to("rs1", rb.at[1])

    def add_far(i):
        t = cols(i, 512)
        acc[:, t] += rb[1, :, t].astype(F32)

    loop(4, add_far)
    for r in range(9):
        out[r] = acc[12 * r : 12 * r + 12, :].astype(BF)
    for name, like in sends.items():
        remote(name, like(), like(), yp).wait_send()
    store_mid.wait()


VM = pl.BlockSpec(memory_space=pltpu.VMEM)
HBM = pl.BlockSpec(memory_space=pltpu.HBM)
DMA = pltpu.SemaphoreType.DMA


def per_device(tokens, qkv_weight, out_weight, merge_weight, up_weight, down_weight):
    order, packed, patch = _tables()
    p1 = jnp.asarray(order, BF)
    p1t = jnp.asarray(order.T, BF)
    pg = jnp.asarray(patch, BF)

    def vmem(*shape, kind=BF):
        return pltpu.VMEM(shape, kind)

    mid, coarse_out = pl.pallas_call(
        kernel,
        name="whole",
        out_shape=(
            jax.ShapeDtypeStruct((CELLS, D), BF),
            jax.ShapeDtypeStruct((ROWS // 2, COLS // 2, DC), BF),
        ),
        in_specs=[HBM, HBM, HBM, VM] + [HBM] * 7,
        out_specs=(HBM, VM),
        scratch_shapes=[
            vmem(CELLS, D),
            vmem(SENT, CELLS),
            vmem(OWN, CELLS),
            vmem(CELLS, OWN),
            vmem(4 * GROUP, CELLS),
            vmem(D, 3 * D),
            vmem(D, D),
            vmem(8, 4 * D, 128),
            vmem(4, DC, 512),
            vmem(4, 512, DC),
            vmem(CELLS, D),
            vmem(SENT, D),
            vmem(OWN, D),
            vmem(HALO, D),
            vmem(OWN, 3 * D),
            vmem(HALO, 2 * D),
            vmem(CELLS, D),
            vmem(GROUP, 4 * D),
            vmem(2 * GROUP, 4 * D),
            vmem(2, 2, GROUP, 512),
            vmem(2, GROUP, 512),
            vmem(GROUP, DC),
            vmem(4, GROUP, DC),
            vmem(2 * GROUP, DC),
            vmem(GROUP, DC, kind=F32),
            vmem(4, GROUP, DC),
            vmem(4, GROUP, DC),
            DMA((12,)),
            DMA((HALO_SENDS,)),
            DMA((HALO_SENDS,)),
            DMA((len(WSEMS),)),
            DMA((len(WSEMS),)),
        ],
        compiler_params=pltpu.CompilerParams(
            collective_id=0, has_side_effects=True, vmem_limit_bytes=62 * 2**20
        ),
    )(
        tokens.reshape(CELLS, D), jnp.asarray(packed, BF), p1, jnp.asarray(_bias()), qkv_weight, out_weight, merge_weight, p1t, pg,
        up_weight, down_weight,
    )
    return mid.reshape(ROWS, COLS, D), coarse_out


def solution(mesh):
    return jax.shard_map(
        per_device,
        mesh=mesh,
        in_specs=(P("lat", "lon", None), P(), P(), P(None, "lon"), P(None, "lon"), P("lon", None)),
        out_specs=(P("lat", "lon", None), P("lat", "lon", None)),
        check_vma=False,
    )
```

```python
import functools

import jax
import jax.numpy as jnp
import numpy as np
from jax import lax
from jax.experimental import pallas as pl
from jax.experimental.pallas import tpu as pltpu
from jax.sharding import PartitionSpec as P

MESH = pl.DeviceIdType.MESH
BF = jnp.bfloat16
F32 = jnp.float32
NEG = -1e30

ROWS, COLS, D, DC, HEADS = 18, 24, 1024, 2048, 16
CELLS = ROWS * COLS
GROUP = 112
HIGH = (3, 6, 6, 3)
WIDE = (6, 12, 6)
TOP = (0, 3, 9, 15)
LEFT = (0, 6, 18)


def _round(n):
    return -(-n // 16) * 16


PIECE = {}
_at = 0
for _b in range(3):
    for _a in range(4):
        PIECE[_a, _b] = (_at, _round(HIGH[_a] * WIDE[_b]), HIGH[_a] * WIDE[_b])
        _at += PIECE[_a, _b][1]
OWN = _at
SEND_W, SEND_E, SEND_N, SEND_S, SENT = 0, 112, 224, 304, 384
HALO_W, HALO_E, HALO_N, HALO_S = 0, 112, 224, 304
HALO_NW, HALO_NE, HALO_SW, HALO_SE = 384, 416, 448, 480
HALO = 512


def _tables():
    order = np.zeros((OWN, CELLS), np.float32)
    for (a, b), (at, _, _) in PIECE.items():
        k = 0
        for i in range(HIGH[a]):
            for j in range(WIDE[b]):
                order[at + k, (TOP[a] + i) * COLS + LEFT[b] + j] = 1
                k += 1
    packed = np.zeros((SENT, CELLS), np.float32)
    column = [(a, 0) for a in range(4)]
    for start, pieces in (
        (SEND_W, column),
        (SEND_E, [(a, 2) for a, _ in column]),
        (SEND_N, [(0, b) for b in range(3)]),
        (SEND_S, [(3, b) for b in range(3)]),
    ):
        k = start
        for a, b in pieces:
            n = PIECE[a, b][2]
            packed[k : k + n] = order[PIECE[a, b][0] : PIECE[a, b][0] + n]
            k += n
    patch = np.zeros((4 * GROUP, CELLS), np.float32)
    for g in range(4):
        for r in range(ROWS // 2):
            for c in range(COLS // 2):
                cell = (2 * r + g // 2) * COLS + 2 * c + g % 2
                patch[g * GROUP + r * (COLS // 2) + c, cell] = 1
    return order, packed, patch


def _span(base, start, count, side):
    low = start // 16 * 16
    return base + low, _round(start + count) - low, start - low, start - low + count, side


def _window_parts():
    out = []
    along, across = ((0, 18), (18, 36), (54, 36), (90, 18)), ((0, 18), (18, 36), (54, 18))
    for b in range(3):
        for a in range(4):
            side = "n" if a == 0 else "s" if a == 3 else ""
            parts = []
            if b != 1:
                parts.append(_span(HALO_W if b == 0 else HALO_E, *along[a], ""))
            if side:
                parts.append(_span(HALO_N if a == 0 else HALO_S, *across[b], side))
            corner = {(0, 0): HALO_NW, (0, 2): HALO_NE, (3, 0): HALO_SW, (3, 2): HALO_SE}
            if (a, b) in corner:
                first = 6 if b == 0 else 0
                parts.append((corner[a, b], 32, first, first + 18, side))
            out.append((PIECE[a, b], parts))
    return out


WINDOWS = _window_parts()


def _bias():
    bias = np.full((3, 16, 128), NEG, np.float32)
    for edge in range(3):
        for w, ((_, rows, valid), parts) in enumerate(WINDOWS):
            bias[edge, w, :valid] = 0
            at = rows
            for _, prows, first, last, side in parts:
                gone = (edge == 1 and side == "n") or (edge == 2 and side == "s")
                if not gone:
                    bias[edge, w, at + first : at + last] = 0
                at += prows
    return bias


def place():
    lat, lon = lax.axis_index("lat"), lax.axis_index("lon")
    z, xl = lat // 2, lat % 2
    y, xh, c = lon // 4, (lon // 2) % 2, lon % 2
    return lat, lon, z, xl, y, xh, c


def norm_rows(x):
    center = x - jnp.mean(x, axis=-1, keepdims=True)
    spread = jnp.mean(center * center, axis=-1, keepdims=True)
    return center * lax.rsqrt(spread + 1e-5)


def loop(n, body):
    def step(i, carry):
        body(i)
        return carry

    lax.fori_loop(0, n, step, 0)


def cols(i, size, base=0):
    return pl.ds(pl.multiple_of(base + i * size, 128), size)


HALO_SENDS = 8
ORDER = (
    ("x00", 3), ("ya+0", 3), ("ya-1", 3), ("ya+1", 7), ("ya-0", 7), ("z00a", 8),
    ("yb+", 11), ("yb-", 11), ("n00", 11), ("x01", 12), ("yq+", 14), ("yq-", 14),
    ("x10", 15), ("z00b", 16), ("n01", 17), ("z01a", 17), ("x11", 18), ("ye+", 20),
    ("ye-", 20), ("n10", 20), ("z10a", 20), ("x20", 21), ("z01b", 22), ("yt+", 23),
    ("yt-", 23), ("n11", 23), ("x21", 24), ("z10b", 25), ("z11a", 25), ("n20", 26),
    ("x30", 27), ("z11b", 28), ("z20a", 28), ("yu+", 29), ("yu-", 29), ("n21", 29),
    ("x31", 30), ("z20b", 31), ("z21a", 31), ("yef+", 32), ("yef-", 32), ("n30", 32),
    ("x40", 33), ("z21b", 34), ("z30a", 34), ("yqf+", 35), ("yqf-", 35), ("n31", 35),
    ("x41", 36), ("z30b", 37), ("z31a", 37), ("n40", 38), ("x50", 39), ("z31b", 40),
    ("z40a", 40), ("n41", 41), ("x51", 42), ("z40b", 43), ("z41a", 43), ("n50", 44),
    ("x60", 46), ("z41b", 46), ("z50a", 46), ("n51", 48), ("x61", 49), ("z50b", 50),
    ("z51a", 50), ("n60", 51), ("x70", 52), ("z51b", 53), ("z60a", 53), ("n61", 54),
    ("x71", 55), ("z60b", 56), ("z61a", 56), ("n70", 57), ("z61b", 59), ("z70a", 59),
    ("n71", 60), ("z70b", 62), ("z71a", 62), ("z71b", 65),
)
WSEMS = {}
for _n in (
    [n for n, _ in ORDER]
    + [f"s{k}" for k in (4, 5, 6, 7)]
    + ["up", "down", "merged", "swap0", "swap1"]
    + ["ag+", "ag-", "ag2+", "ag2-", "rs1", "rs2", "rs3"]
):
    WSEMS[_n] = len(WSEMS)


def needs(name):
    if name[0] in "nz":
        return [("n" if name[-1] == "b" else "x") + name[1:3]]
    if name[0] == "x":
        k, i = int(name[1]), name[2]
        return {1: [f"ya+{i}"], 2: [f"ya-{i}"], 3: ["yb+" if i == "0" else "yb-"]}.get(k, [])
    first = {"yb+": "ya+0", "yb-": "ya-1", "yqf+": "yq+", "yqf-": "yq-", "yef+": "ye+", "yef-": "ye-"}
    return [first[name]] if name in first else []


A_ROWS, B_ROWS = pl.ds(0, 64), pl.ds(64, 48)


def gelu(x):
    return 0.5 * x * (1.0 + lax.erf(x * np.float32(0.5**0.5)))


def kernel(
    tok_in, ps_in, p1_in, bias, qkvw, outw, mw, p1t_in, pg_in, up, down,
    mid_out, out,
    tok, ps, p1, p1t, pg, qkvv, outv, wv, up4, down4,
    normed, packed, xp, halo, qkv, kvh, mid, mgd,
    xs, cc, theirs, coarse, cn, hid, acc, pt, rb,
    lsem, hs, hr, ws, wr,
):
    lat, lon, z, xl, y, xh, c = place()
    north, south = lat > 0, lat < 7
    west, east = (lon + 15) % 16, (lon + 1) % 16
    yp = (lat, (lon + 4) % 16)
    ym = (lat, (lon + 12) % 16)
    y2 = (lat, (lon + 8) % 16)
    zp = ((lat + 2) % 8, lon)
    zm = ((lat + 6) % 8, lon)
    xpart = (2 * z + 1 - xl, 4 * y + 2 * (1 - xh) + c)
    xn = (lat + 1 - 2 * xl, lon)
    sibling = (lat, lon + 1 - 2 * c)

    barrier = pltpu.get_barrier_semaphore()

    def greet(dev):
        pl.semaphore_signal(barrier, inc=1, device_id=dev, device_id_type=MESH)

    partners = ((lat, west), (lat, east), yp, ym, y2, zp, zm, xpart, xn, sibling)
    for dev in partners:
        greet(dev)

    @pl.when(north)
    def _():
        for o in (west, lon, east):
            greet((lat - 1, o))

    @pl.when(south)
    def _():
        for o in (west, lon, east):
            greet((lat + 1, o))

    own = 2 * y + xh
    local = [
        pltpu.make_async_copy(tok_in, tok, lsem.at[0]),
        pltpu.make_async_copy(p1_in, p1, lsem.at[1]),
        pltpu.make_async_copy(qkvw, qkvv, lsem.at[2]),
        pltpu.make_async_copy(p1t_in, p1t, lsem.at[3]),
        pltpu.make_async_copy(outw, outv, lsem.at[4]),
        pltpu.make_async_copy(pg_in, pg, lsem.at[5]),
        pltpu.make_async_copy(mw, wv.at[own], lsem.at[6]),
        pltpu.make_async_copy(up, up4.at[0], lsem.at[7]),
        pltpu.make_async_copy(down, down4.at[0], lsem.at[8]),
    ]
    early = pltpu.make_async_copy(ps_in, ps, lsem.at[11])
    local[0].start()
    early.start()
    local[1].start()
    local[2].start()

    count = len(partners) + jnp.where(north, 3, 0) + jnp.where(south, 3, 0)
    pl.semaphore_wait(barrier, count)

    shift = [2 * ((y + d) % 4) for d in (0, 3, 1, 2)]
    slots = {False: [v + xh for v in shift], True: [v + 1 - xh for v in shift]}
    zq = [(z + d) % 4 for d in range(4)]

    def block(k, other):
        return slots[other][k]

    def rows_of(size, quarter, half, base=0):
        at = base + quarter * 2 * size
        if half is None:
            return pl.ds(pl.multiple_of(at, size), 2 * size)
        return pl.ds(pl.multiple_of(at + half * size, size), size)

    sends = {}

    def remote(name, src, dst, dev):
        i = WSEMS[name]
        return pltpu.make_async_remote_copy(
            src_ref=src, dst_ref=dst, send_sem=ws.at[i], recv_sem=wr.at[i],
            device_id=dev, device_id_type=MESH,
        )

    def send(name, src, dst, dev, like=None):
        remote(name, src, dst, dev).start()
        if like is None:
            rows, width = dst.shape
            buffer = {128: wv, 512: up4, DC: down4}[width]

            def like():
                return buffer.at[0, pl.ds(0, rows), :]

        sends[name] = like

    def await_to(name, dst):
        remote(name, dst, dst, yp).wait_recv()

    def near(k, quarter, half):
        return wv.at[block(k, False), rows_of(512, quarter, half), :]

    def far_rows(k, quarter, half):
        if k < 6:
            return rows_of(128, quarter, half, (k - 4) * 1024)
        return rows_of(32, quarter, half, (k - 6) * 256)

    def far(k, quarter, half):
        if k < 4:
            return wv.at[block(k, True), rows_of(512, quarter, half), :]
        return (up4 if k < 6 else down4).at[2, far_rows(k, quarter, half), :]

    ox = 1 - xl

    def region(name):
        kind, sign = name[:-2] if name[1] == "a" else name[:-1], name[2] if name[1] == "a" else name[-1]
        plus = sign == "+"
        if kind == "ya":
            return zq[int(name[3])], ox
        if kind == "yb":
            return (zq[0], ox) if plus else (zq[1], ox)
        if kind in ("yq", "yqf"):
            return (zq[2], None) if plus else (zq[3], None)
        if kind == "yt":
            return (zq[3], None) if plus else (zq[2], None)
        if kind in ("ye", "yef"):
            return (zq[0], xl) if plus else (zq[1], xl)
        return (zq[1], xl) if plus else (zq[0], xl)

    def landing(name):
        if name[0] == "y":
            second = name[:2] == "yb" or name[:3] in ("yqf", "yef")
            k = 3 if second else 1 if "+" in name else 2
            return near(k, *region(name))
        k, i = int(name[1]), int(name[2])
        if name[0] == "x":
            return far(k, zq[i], xl)
        if name[0] == "n":
            return far(k, zq[i], ox)
        return far(k, zq[3 if i == 0 else 2], xl if name[3] == "a" else ox)

    def start(name):
        if name[0] == "y":
            plus = "+" in name
            dev = yp if plus else ym
            if name[:2] == "yb" or name[:3] in ("yqf", "yef"):
                ref = near(1 if plus else 2, *region(name))
                send(name, ref, ref, dev)
            else:
                quarter, half = region(name)
                send(name, mw.at[rows_of(512, quarter, half), :], near(0, quarter, half), dev)
            return
        k, i = int(name[1]), int(name[2])
        if name[0] == "x":
            if k == 0:
                send(name, mw.at[rows_of(512, zq[i], ox), :], near(0, zq[i], ox), xpart)
            elif k < 4:
                send(name, near(k, zq[i], ox), near(k, zq[i], ox), xpart)
            else:
                send(name, (up if k < 6 else down).at[far_rows(k, zq[i], ox), :], far(k, zq[i], ox), xpart)
        elif name[0] == "n":
            send(name, far(k, zq[i], xl), far(k, zq[i], xl), xn)
        else:
            ref = far(k, zq[i], xl if name[3] == "a" else ox)
            send(name, ref, ref, zp if i == 0 else zm)

    landed = set()
    queue = list(ORDER)

    def need(name):
        if name not in landed:
            landed.add(name)
            await_to(name, landing(name))

    def pump_at(i, steps):
        for n, time in steps.items():

            @pl.when(i == n)
            def _(time=time):
                pump(time)

    def pump(time):
        while queue and queue[0][1] <= time:
            name = queue.pop(0)[0]
            for other in needs(name):
                need(other)
            start(name)

    def need_far(k):
        for n, _ in ORDER:
            if n[0] in "xnz" and n[1] == str(k):
                need(n)

    def share(k):
        size = 1024 if k < 6 else 256
        rows = pl.ds((k % 2) * size, size)
        to = up4 if k < 6 else down4
        send(f"s{k}", to.at[2, rows, :], to.at[3, rows, :], sibling, lambda: to.at[3, rows, :])

    pump(3)

    local[0].wait()

    def norm_block(i):
        r = pl.ds(pl.multiple_of(i * 48, 16), 48)
        normed[r, :] = norm_rows(tok[r, :].astype(F32)).astype(BF)

    loop(9, norm_block)
    for n in (6, 3, 4, 5):
        local[n].start()
    early.wait()

    def pack(i):
        packed[:, cols(i, 256)] = jnp.dot(
            ps[...], normed[:, cols(i, 256)], preferred_element_type=F32
        ).astype(BF)

    loop(4, pack)

    def hcopy(i, src_at, dst_at, rows, dev):
        return pltpu.make_async_remote_copy(
            src_ref=packed.at[pl.ds(src_at, rows), :], dst_ref=halo.at[pl.ds(dst_at, rows), :],
            send_sem=hs.at[i], recv_sem=hr.at[i], device_id=dev, device_id_type=MESH,
        )

    middle_sends = [
        hcopy(0, SEND_W, HALO_E, 112, (lat, west)),
        hcopy(1, SEND_E, HALO_W, 112, (lat, east)),
    ]
    north_sends = [
        hcopy(2, SEND_N, HALO_S, 80, (lat - 1, lon)),
        hcopy(3, SEND_N, HALO_SE, 32, (lat - 1, west)),
        hcopy(4, SEND_N + 48, HALO_SW, 32, (lat - 1, east)),
    ]
    south_sends = [
        hcopy(5, SEND_S, HALO_N, 80, (lat + 1, lon)),
        hcopy(6, SEND_S, HALO_NE, 32, (lat + 1, west)),
        hcopy(7, SEND_S + 48, HALO_NW, 32, (lat + 1, east)),
    ]
    for cp in middle_sends:
        cp.start()

    @pl.when(north)
    def _():
        for cp in north_sends:
            cp.start()

    @pl.when(south)
    def _():
        for cp in south_sends:
            cp.start()

    local[1].wait()

    def permute(i):
        xp[:, cols(i, 256)] = jnp.dot(
            p1[...], normed[:, cols(i, 256)], preferred_element_type=F32
        ).astype(BF)

    loop(4, permute)

    @pl.when(jnp.logical_not(north))
    def _():
        halo[HALO_N : HALO_N + 80, :] = jnp.zeros((80, D), BF)
        halo[HALO_NW : HALO_NW + 64, :] = jnp.zeros((64, D), BF)

    @pl.when(jnp.logical_not(south))
    def _():
        halo[HALO_S : HALO_S + 80, :] = jnp.zeros((80, D), BF)
        halo[HALO_SW : HALO_SW + 64, :] = jnp.zeros((64, D), BF)

    local[2].wait()

    def project(i):
        qkv[:, cols(i, 256)] = jnp.dot(
            xp[...], qkvv[:, cols(i, 256)], preferred_element_type=F32
        ).astype(BF)
        pump_at(i, {3: 10, 7: 12})

    local[7].start()
    local[8].start()
    pump(8)
    loop(12, project)
    pump(14)
    send("up", up, up4.at[1], sibling, lambda: up4.at[1])
    send("down", down, down4.at[1], sibling, lambda: down4.at[1])

    edge = jnp.where(north, jnp.where(south, 0, 2), 1)
    low = lax.broadcasted_iota(jnp.int32, (1, 128), 1) < 64

    def attend(i, inner):
        head = cols(i, 128)
        head_k, head_v = cols(i, 128, D), cols(i, 128, 2 * D)
        for w, ((start, rows, _), parts) in enumerate(WINDOWS):
            if inner: continue
            r = slice(start, start + rows)
            q = qkv[r, head] * jnp.asarray(0.125, BF)
            zero = jnp.zeros_like(q)
            q = jnp.concatenate([jnp.where(low, q, zero), jnp.where(low, zero, q)], axis=0)
            ks, vs = [qkv[r, head_k]], [qkv[r, head_v]]
            for off, prows, _, _, _ in parts:
                ks.append(kvh[off : off + prows, head])
                vs.append(kvh[off : off + prows, head_k])
            k = jnp.concatenate(ks, axis=0) if parts else ks[0]
            v = jnp.concatenate(vs, axis=0) if parts else vs[0]
            m = k.shape[0]
            s = lax.dot_general(q, k, (((1,), (1,)), ((), ())), preferred_element_type=F32)
            s = s + bias[edge, w : w + 1, :m]
            e = jnp.exp(s - jnp.max(s, axis=-1, keepdims=True)).astype(BF)
            ve = jnp.concatenate([v, jnp.ones((m, 128), BF)], axis=1)
            o = jnp.dot(e, ve, preferred_element_type=F32)
            num = jnp.where(low, o[:rows, :128], o[rows:, :128])
            den = jnp.where(low, o[:rows, 128:], o[rows:, 128:])
            att[r, head] = (num / den).astype(BF)

    att = xp

    def pair_inner(i):
        attend(i, True)

    pump(16)

    for cp in middle_sends:
        cp.wait()

    @pl.when(north)
    def _():
        for cp in south_sends:
            cp.wait_recv()
        for cp in north_sends:
            cp.wait_send()

    @pl.when(south)
    def _():
        for cp in north_sends:
            cp.wait_recv()
        for cp in south_sends:
            cp.wait_send()

    def project_halo(i):
        kvh[:, cols(i, 256)] = jnp.dot(
            halo[...], qkvv[:, cols(i, 256, D)], preferred_element_type=F32
        ).astype(BF)
        pump_at(i, {3: 21})

    pump(20)
    loop(8, project_halo)
    pump(22)

    def pair_outer(i):
        attend(i, False)
        pump_at(i, {0: 24, 1: 26, 2: 27, 3: 29, 4: 31, 5: 33, 6: 34, 7: 36})

    loop(8, pair_outer)

    local[3].wait()
    attr = normed

    def unpermute(i):
        attr[:, cols(i, 256)] = jnp.dot(
            p1t[...], att[:, cols(i, 256)], preferred_element_type=F32
        ).astype(BF)
        pump_at(i, {1: 37})

    loop(4, unpermute)
    local[4].wait()

    def out_project(i):
        mixed = jnp.dot(attr[...], outv[:, cols(i, 256)], preferred_element_type=F32)
        mid[:, cols(i, 256)] = (tok[:, cols(i, 256)].astype(F32) + mixed).astype(BF)
        pump_at(i, {1: 38})

    loop(4, out_project)
    store_mid = pltpu.make_async_copy(mid, mid_out, lsem.at[9])
    store_mid.start()
    pump(38)
    local[5].wait()

    def patch(i):
        g, t = i // 4, i % 4
        mgd[:, cols(i, 256)] = jnp.dot(
            pg[pl.ds(pl.multiple_of(g * GROUP, 16), GROUP), :], mid[:, cols(t, 256)],
            preferred_element_type=F32,
        ).astype(BF)
        pump_at(i, {3: 39, 7: 40, 11: 41})

    loop(16, patch)

    def merge_norm(i):
        r = pl.ds(pl.multiple_of(i * 16, 16), 16)
        mgd[r, :] = norm_rows(mgd[r, :].astype(F32)).astype(BF)

    loop(GROUP // 16, merge_norm)
    mine = pl.ds(pl.multiple_of(c * GROUP, 16), GROUP)
    send("merged", mgd, xs.at[mine, :], sibling, lambda: mgd)
    keep_mgd = pltpu.make_async_copy(mgd, xs.at[mine, :], lsem.at[10])
    keep_mgd.start()

    pump(40)
    local[6].wait()
    for n, _ in ORDER:
        if n[0] == "y":
            need(n)
    pump(42)
    keep_mgd.wait()
    theirs_rows = pl.ds(pl.multiple_of((1 - c) * GROUP, 16), GROUP)
    await_to("merged", xs.at[theirs_rows, :])

    def merge(i):
        n = i // 2

        @pl.when(i == 2)
        def _():
            send("swap0", cc.at[1 - c, 0], theirs.at[0], sibling, lambda: theirs.at[0])
            pump(45)
            for k in range(4):
                need_far(k)

        h = jnp.where(n == 0, xh, 1 - xh)
        first = 4 * (i % 2) + h
        v = jnp.zeros((2 * GROUP, 256), F32)
        for g in range(4):
            r = slice(g * D, (g + 1) * D)
            w = jnp.concatenate([wv[first, r, :], wv[first + 2, r, :]], axis=1)
            v += jnp.dot(xs[:, r], w, preferred_element_type=F32)
        v = v.astype(BF)
        cc[0, n, :, cols(i % 2, 256)] = v[:GROUP]
        cc[1, n, :, cols(i % 2, 256)] = v[GROUP:]

    def place_columns(n, core, get):
        h = xh if n == 0 else 1 - xh
        for j in range(4):
            at = pl.multiple_of((4 * j + 2 * h + core) * 128, 128)
            coarse[:, pl.ds(at, 128)] = get(slice(j * 128, (j + 1) * 128))

    loop(4, merge)
    send("swap1", cc.at[1 - c, 1], theirs.at[1], sibling, lambda: theirs.at[1])
    pump(48)
    for n in (0, 1):
        place_columns(n, c, lambda t, n=n: cc[c, n, :, t])
    for n in (0, 1):
        await_to(f"swap{n}", theirs.at[n])
        place_columns(n, 1 - c, lambda t, n=n: theirs[n, :, t])

    def coarse_norm(i):
        r = pl.ds(pl.multiple_of(i * 16, 16), 16)
        cn[0, r, :] = norm_rows(coarse[r, :].astype(F32)).astype(BF)

    loop(GROUP // 16, coarse_norm)

    send("ag+", cn.at[0], cn.at[2], yp, lambda: cn.at[2])
    send("ag-", cn.at[0], cn.at[3], ym, lambda: cn.at[3])
    pump(58)
    for n in (7, 8):
        local[n].wait()
    await_to("up", up4.at[1])
    await_to("down", down4.at[1])

    def await_share(k):
        size = 1024 if k < 6 else 256
        await_to(f"s{k}", (up4 if k < 6 else down4).at[3, pl.ds((k % 2) * size, size), :])

    def ffn(n):
        first = 2 - 2 * n
        rows = 2 * GROUP

        def up_step(i):
            q, t = i // 2, i % 2
            x = cn[pl.ds(first, 2)].reshape(rows, DC)
            h = jnp.dot(x, up4[q, :, cols(t, 256)], preferred_element_type=F32)
            hid[:, cols(i, 256)] = gelu(h).astype(BF)

        loop(8, up_step)

        @pl.when(n == 0)
        def _():
            need_far(7)
            share(7)
            await_share(6)
            await_share(7)

        def down_step(i):
            t = cols(i, 256)
            v = jnp.zeros((rows, 256), F32)
            for q in range(4):
                v += jnp.dot(hid[:, q * 512 : (q + 1) * 512], down4[q, :, t], preferred_element_type=F32)
            acc[:, t] = v[:GROUP] + coarse[:, t].astype(F32)
            pt[first, :, t] = v[:GROUP].astype(BF)
            pt[first + 1, :, t] = v[GROUP:].astype(BF)

        loop(8, down_step)

        @pl.when(n == 0)
        def _():
            send("rs2", pt.at[2], rb.at[3], ym, lambda: rb.at[3])
            send("rs3", pt.at[3], rb.at[2], yp, lambda: rb.at[2])
            await_to("ag2+", cn.at[1, A_ROWS, :])
            await_to("ag2-", cn.at[1, B_ROWS, :])

    await_to("ag+", cn.at[2])
    send("ag2+", cn.at[2, A_ROWS, :], cn.at[1, A_ROWS, :], yp, lambda: cn.at[1, A_ROWS, :])
    await_to("ag-", cn.at[3])
    send("ag2-", cn.at[3, B_ROWS, :], cn.at[1, B_ROWS, :], ym, lambda: cn.at[1, B_ROWS, :])
    pump(60)
    need_far(4)
    share(4)
    pump(63)
    need_far(5)
    share(5)
    pump(99)
    need_far(6)
    share(6)
    for k in (4, 5):
        await_share(k)
    loop(2, ffn)
    send("rs1", pt.at[1], rb.at[1], y2, lambda: rb.at[1])
    await_to("rs2", rb.at[3])
    await_to("rs3", rb.at[2])

    def add_near(i):
        t = cols(i, 512)
        acc[:, t] += rb[2, :, t].astype(F32) + rb[3, :, t].astype(F32)

    loop(4, add_near)
    await_to("rs1", rb.at[1])

    def add_far(i):
        t = cols(i, 512)
        acc[:, t] += rb[1, :, t].astype(F32)

    loop(4, add_far)
    for r in range(9):
        out[r] = acc[12 * r : 12 * r + 12, :].astype(BF)
    for name, like in sends.items():
        remote(name, like(), like(), yp).wait_send()
    store_mid.wait()


VM = pl.BlockSpec(memory_space=pltpu.VMEM)
HBM = pl.BlockSpec(memory_space=pltpu.HBM)
DMA = pltpu.SemaphoreType.DMA


def per_device(tokens, qkv_weight, out_weight, merge_weight, up_weight, down_weight):
    order, packed, patch = _tables()
    p1 = jnp.asarray(order, BF)
    p1t = jnp.asarray(order.T, BF)
    pg = jnp.asarray(patch, BF)

    def vmem(*shape, kind=BF):
        return pltpu.VMEM(shape, kind)

    mid, coarse_out = pl.pallas_call(
        kernel,
        name="whole",
        out_shape=(
            jax.ShapeDtypeStruct((CELLS, D), BF),
            jax.ShapeDtypeStruct((ROWS // 2, COLS // 2, DC), BF),
        ),
        in_specs=[HBM, HBM, HBM, VM] + [HBM] * 7,
        out_specs=(HBM, VM),
        scratch_shapes=[
            vmem(CELLS, D),
            vmem(SENT, CELLS),
            vmem(OWN, CELLS),
            vmem(CELLS, OWN),
            vmem(4 * GROUP, CELLS),
            vmem(D, 3 * D),
            vmem(D, D),
            vmem(8, 4 * D, 128),
            vmem(4, DC, 512),
            vmem(4, 512, DC),
            vmem(CELLS, D),
            vmem(SENT, D),
            vmem(OWN, D),
            vmem(HALO, D),
            vmem(OWN, 3 * D),
            vmem(HALO, 2 * D),
            vmem(CELLS, D),
            vmem(GROUP, 4 * D),
            vmem(2 * GROUP, 4 * D),
            vmem(2, 2, GROUP, 512),
            vmem(2, GROUP, 512),
            vmem(GROUP, DC),
            vmem(4, GROUP, DC),
            vmem(2 * GROUP, DC),
            vmem(GROUP, DC, kind=F32),
            vmem(4, GROUP, DC),
            vmem(4, GROUP, DC),
            DMA((12,)),
            DMA((HALO_SENDS,)),
            DMA((HALO_SENDS,)),
            DMA((len(WSEMS),)),
            DMA((len(WSEMS),)),
        ],
        compiler_params=pltpu.CompilerParams(
            collective_id=0, has_side_effects=True, vmem_limit_bytes=62 * 2**20
        ),
    )(
        tokens.reshape(CELLS, D), jnp.asarray(packed, BF), p1, jnp.asarray(_bias()), qkv_weight, out_weight, merge_weight, p1t, pg,
        up_weight, down_weight,
    )
    return mid.reshape(ROWS, COLS, D), coarse_out


def solution(mesh):
    return jax.shard_map(
        per_device,
        mesh=mesh,
        in_specs=(P("lat", "lon", None), P(), P(), P(None, "lon"), P(None, "lon"), P("lon", None)),
        out_specs=(P("lat", "lon", None), P("lat", "lon", None)),
        check_vma=False,
    )
```
